32 devices in a mesh: section: 2 (over core), batch: 8 (over z, x), tensor: 2 (over y).
Axes of the slice: x: 2, y: 2, z: 4, core: 2. Of those that a mesh axis runs over, the one named last changes fastest.
Arguments:
- section_ends: bfloat16 [2, 16, 512, 768], P('section', 'batch', 'tensor'), may hold values from -6 to 6
- lengths: int32 [16, 4], P('batch'), may hold values from 1 to 256, 512 in all within a row
- w_query: bfloat16 [2, 768, 768], P('section', None, 'tensor'), may hold values from -0.21875 to 0.21875
- b_query: float32 [2, 768], P('section', 'tensor'), may hold values from -3 to 3
- w_key: bfloat16 [2, 768, 768], P('section', None, 'tensor'), may hold values from -0.21875 to 0.21875
- w_value: bfloat16 [2, 768, 768], P('section', None, 'tensor'), may hold values from -0.21875 to 0.21875
- b_value: float32 [2, 768], P('section', 'tensor'), may hold values from -3 to 3
- w_out: bfloat16 [2, 768, 768], P('section', 'tensor'), may hold values from -0.875 to 0.875
- b_out: float32 [2, 768], P('section'), may hold values from -3 to 3
- norm1_gain: float32 [2, 768], P('section'), may hold values from 0.25 to 1.75
- norm1_bias: float32 [2, 768], P('section'), may hold values from -2 to 2
- w_inner: bfloat16 [2, 768, 3072], P('section', None, 'tensor'), may hold values from -0.21875 to 0.21875
- b_inner: float32 [2, 3072], P('section', 'tensor'), may hold values from -3 to 3
- w_outer: bfloat16 [2, 3072, 768], P('section', 'tensor'), may hold values from -0.109375 to 0.109375
- b_outer: float32 [2, 768], P('section'), may hold values from -3 to 3
- norm2_gain: float32 [2, 768], P('section'), may hold values from 0.25 to 1.75
- norm2_bias: float32 [2, 768], P('section'), may hold values from -2 to 2
Outputs:
- section_results: bfloat16 [2, 16, 512, 768], P('section', 'batch', 'tensor')
- grad_w_query: float32 [2, 768, 768], P('section', None, 'tensor')
- grad_b_query: float32 [2, 768], P('section', 'tensor')
- grad_w_key: float32 [2, 768, 768], P('section', None, 'tensor')
- grad_w_value: float32 [2, 768, 768], P('section', None, 'tensor')
- grad_b_value: float32 [2, 768], P('section', 'tensor')
- grad_w_out: float32 [2, 768, 768], P('section', 'tensor')
- grad_b_out: float32 [2, 768], P('section')
- grad_norm1_gain: float32 [2, 768], P('section')
- grad_norm1_bias: float32 [2, 768], P('section')
- grad_w_inner: float32 [2, 768, 3072], P('section', None, 'tensor')
- grad_b_inner: float32 [2, 3072], P('section', 'tensor')
- grad_w_outer: float32 [2, 3072, 768], P('section', 'tensor')
- grad_b_outer: float32 [2, 768], P('section')
- grad_norm2_gain: float32 [2, 768], P('section')
- grad_norm2_bias: float32 [2, 768], P('section')
The draws below stay inside these ranges and needn't reach their ends.
Inputs may be any that keep to these rules, and one draw needn't show every extreme that they name: Each row of lengths sums to 512; a slot's sentences fill it in order with no padding, and tokens attend only within their own sentence.
All inputs are finite; a program needn't handle non-finite values.
Results may differ from the reference program's by a relative error of at most 0.025.
Values may be sent and summed in bfloat16 or wider, within the bound.
No kernel may reach another device: no remote copies, remote signals or barrier semaphores. Data moves between devices by JAX's collectives and lax.ppermute only.
A program may use at most 128 MiB of HBM per device.

```python
import math
import jax
import jax.numpy as jnp
import numpy as np
from jax import lax

D = 768
HEADS = 12
HD = 64
FF = 3072
SLOT = 512
SEGS = 4
SLOTS = 16


def level_of(stream_key, dims, shards, low, top_value):
    gain = 1.0
    for dim, blocks in shards:
        draws = jax.random.uniform(jax.random.fold_in(jax.random.fold_in(stream_key, 6), dim), (blocks,), jnp.float32, low / len(shards), top_value / len(shards))
        gain = gain * jnp.repeat(jnp.exp(draws), dims[dim] // blocks).reshape((-1,) + (1,) * (len(dims) - 1 - dim))
    return gain


def profile(number_of, total, most, slope):
    portions = [(1 << 20) // math.isqrt(standing ** slope) + 1 for standing in range(2, number_of + 1)]
    rest, given = total - most - (number_of - 1), [1] * (number_of - 1)
    while rest > 0:
        candidates = [i for i in range(number_of - 1) if given[i] < most]
        pool, left = sum([portions[i] for i in candidates]), rest
        for i in candidates:
            more = min(most - given[i], max(1, left * portions[i] // pool), rest)
            given[i] = given[i] + more
            rest = rest - more
    return np.array([most] + given)


def ragged_sizes(stream_key, amount, total, bound, lean):
    if amount == 2:
        one = jax.random.randint(stream_key, (), max(1, total - bound), min(bound, total - 1) + 1)
        return jnp.stack([one, total - one])
    tallies = jnp.asarray(profile(amount, total, bound, lean), jnp.int32)
    pairs = (amount - 1) // 2
    giver, taker = tallies[1:1 + 2 * pairs:2], tallies[2:2 + 2 * pairs:2]
    margin = jnp.minimum(giver - 1, bound - taker)
    shifted = jax.random.randint(jax.random.fold_in(stream_key, 1), (pairs,), 0, 1 << 20) % (margin + 1)
    tallies = tallies.at[1:1 + 2 * pairs:2].set(giver - shifted).at[2:2 + 2 * pairs:2].set(taker + shifted)
    return tallies[jax.random.permutation(jax.random.fold_in(stream_key, 2), amount)]


def noise(stream_key, extent, deviation, most, pieces=(), held_as=jnp.bfloat16):
    factor_of = level_of(stream_key, extent, pieces, -0.22, 0.18) if pieces else 1.0
    entries = jax.random.normal(stream_key, extent, jnp.float32) * deviation * factor_of
    return jnp.minimum(jnp.maximum(entries, -most), most).astype(held_as)


def setup_inputs(seed: int = 0) -> dict:
    splits = jax.random.split(jax.random.key(seed), 18)
    section_ends = noise(splits[0], (2, SLOTS, SLOT, D), 1.0, 6.0, ((0, 2), (1, 8), (2, 2)))
    lengths = jax.vmap(lambda own: ragged_sizes(own, SEGS, SLOT, SLOT // 2, 2))(jax.random.split(splits[1], SLOTS)).reshape((SLOTS, SEGS)).astype(jnp.int32)
    w_query = noise(splits[2], (2, D, D), D ** -0.5, 0.21875, ((0, 2), (2, 2)))
    b_query = noise(splits[3], (2, D), 0.5, 3.0, ((0, 2), (1, 2)), jnp.float32)
    w_key = noise(splits[4], (2, D, D), D ** -0.5, 0.21875, ((0, 2), (2, 2)))
    w_value = noise(splits[5], (2, D, D), D ** -0.5, 0.21875, ((0, 2), (2, 2)))
    b_value = noise(splits[6], (2, D), 0.5, 3.0, ((0, 2), (1, 2)), jnp.float32)
    w_out = noise(splits[7], (2, D, D), (D // 16) ** -0.5, 0.875, ((0, 2), (1, 2)))
    b_out = noise(splits[8], (2, D), 0.5, 3.0, ((0, 2),), jnp.float32)
    norm1_gain = jnp.clip(1.0 + 0.15 * jax.random.normal(splits[9], (2, D), jnp.float32), 0.25, 1.75)
    norm1_bias = noise(splits[10], (2, D), 0.3, 2.0, ((0, 2),), jnp.float32)
    w_inner = noise(splits[11], (2, D, FF), D ** -0.5, 0.21875, ((0, 2), (2, 2)))
    b_inner = noise(splits[12], (2, FF), 0.5, 3.0, ((0, 2), (1, 2)), jnp.float32)
    w_outer = noise(splits[13], (2, FF, D), FF ** -0.5, 0.109375, ((0, 2), (1, 2)))
    b_outer = noise(splits[14], (2, D), 0.5, 3.0, ((0, 2),), jnp.float32)
    norm2_gain = jnp.clip(1.0 + 0.15 * jax.random.normal(splits[15], (2, D), jnp.float32), 0.25, 1.75)
    norm2_bias = noise(splits[16], (2, D), 0.3, 2.0, ((0, 2),), jnp.float32)
    return dict(section_ends=section_ends, lengths=lengths, w_query=w_query, b_query=b_query, w_key=w_key, w_value=w_value, b_value=b_value, w_out=w_out, b_out=b_out, norm1_gain=norm1_gain, norm1_bias=norm1_bias, w_inner=w_inner, b_inner=b_inner, w_outer=w_outer, b_outer=b_outer, norm2_gain=norm2_gain, norm2_bias=norm2_bias)


@jax.custom_vjp
def low(v):
    return lax.optimization_barrier(v.astype(jnp.bfloat16)).astype(jnp.float32)

@jax.custom_vjp
def low_back(v):
    return v

def low_keep(v):
    return (low(v), None)

def low_pass(kept, grad):
    return (grad,)

def back_keep(v):
    return (v, None)

def back_low(kept, grad):
    return (low(grad),)
low.defvjp(low_keep, low_pass)
low_back.defvjp(back_keep, back_low)
epsilon = 1e-06

def product(left, right):
    return jnp.dot(left, right, precision=lax.Precision.HIGHEST)

def segment_ids(length_row):
    bounds = jnp.cumsum(length_row)
    places = jnp.arange(SLOT, dtype=jnp.int32)
    return lax.optimization_barrier(jnp.sum((places[:, None] >= bounds[None, :]).astype(jnp.int32), axis=1))

def layer_norm(residue, gain_vector, offset):
    center = residue - lax.optimization_barrier(jnp.mean(residue, axis=-1, keepdims=True))
    spread = lax.optimization_barrier(jnp.mean(center * center, axis=-1, keepdims=True))
    return center * lax.rsqrt(spread + epsilon) * gain_vector + offset

def layer(inputs, params, same_segment):
    w_query, b_query, w_key, w_value, b_value, w_out, b_out, gain_one, bias_one, w_inner, b_inner, w_outer, b_outer, gain_two, bias_two = params
    queries = low_back(low(product(inputs, w_query) + b_query)).reshape(SLOT, HEADS, HD)
    key_rows = low_back(low(product(inputs, w_key))).reshape(SLOT, HEADS, HD)
    values = low_back(low(product(inputs, w_value) + b_value)).reshape(SLOT, HEADS, HD)
    scores = jnp.einsum('qhd,khd->hqk', queries, key_rows, precision=lax.Precision.HIGHEST) * (1.0 / math.sqrt(HD))
    scores = jnp.where(same_segment[None], low_back(scores), -1e+30)
    highest_score = lax.optimization_barrier(jnp.max(scores, axis=-1, keepdims=True))
    raised = jnp.exp(scores - highest_score)
    probability = low(raised / lax.optimization_barrier(jnp.sum(raised, axis=-1, keepdims=True)))
    context = jnp.einsum('hqk,khd->qhd', probability, values, precision=lax.Precision.HIGHEST).reshape(SLOT, D)
    context = low_back(low(context))
    residue_one = inputs + low_back(product(context, w_out)) + b_out
    normed = layer_norm(residue_one, gain_one, bias_one)
    hidden = low_back(product(low(normed), w_inner) + b_inner)
    active = low(jax.nn.gelu(hidden, approximate=False))
    residue_two = normed + low_back(product(active, w_outer)) + b_outer
    return layer_norm(residue_two, gain_two, bias_two)

def both_layers(slot_rows, length_row, params):
    segment = segment_ids(length_row)
    same_segment = segment[:, None] == segment[None, :]
    layer_one = tuple((member[0] for member in params))
    layer_two = tuple((member[1] for member in params))
    middle = low_back(low(layer(slot_rows, layer_one, same_segment)))
    return layer(middle, layer_two, same_segment)

def reference(section_ends, lengths, w_query, b_query, w_key, w_value, b_value, w_out, b_out, norm1_gain, norm1_bias, w_inner, b_inner, w_outer, b_outer, norm2_gain, norm2_bias):
    params = tuple((member.astype(jnp.float32) for member in (w_query, b_query, w_key, w_value, b_value, w_out, b_out, norm1_gain, norm1_bias, w_inner, b_inner, w_outer, b_outer, norm2_gain, norm2_bias)))
    inputs = section_ends[0].astype(jnp.float32)
    cotangent = section_ends[1].astype(jnp.float32)
    checked = jax.checkpoint(both_layers)

    def forward(slot_inputs, weights):

        def per_slot(slot_pair):
            return checked(slot_pair[0], slot_pair[1], weights)
        return lax.map(per_slot, (slot_inputs, lengths))
    outputs, pullback = jax.vjp(forward, inputs, params)
    grad_inputs, gradients = pullback(cotangent)
    results = jnp.stack([grad_inputs.astype(jnp.bfloat16), outputs.astype(jnp.bfloat16)])
    return (results, gradients[0], gradients[1], gradients[2], gradients[3], gradients[4], gradients[5], gradients[6], gradients[7], gradients[8], gradients[9], gradients[10], gradients[11], gradients[12], gradients[13], gradients[14])
```

```python
import functools
import math

import jax
import jax.numpy as jnp
from jax import lax
from jax.experimental import pallas as pl
from jax.experimental.pallas import tpu as pltpu
from jax.sharding import PartitionSpec as P

HD = 64
epsilon = 1e-06
root_half = 0.7071067811865476
inverse_root = 0.3989422804014327
BF = jnp.bfloat16
F32 = jnp.float32
RB = 128
VMEM_BYTES = 56 * 1024 * 1024

V_BQV, V_BO, V_G1, V_B1, V_BI, V_BU, V_G2, V_B2 = 0, 1, 2, 3, 4, 6, 7, 8
V_ROWS = 16
SMALL_ROWS = 32


def dot(a, b):
    return lax.dot_general(a, b, (((1,), (0,)), ((), ())), preferred_element_type=F32)


def dot_nt(a, b):
    return lax.dot_general(a, b, (((1,), (1,)), ((), ())), preferred_element_type=F32)


def dot_tn(a, b):
    return lax.dot_general(a, b, (((0,), (0,)), ((), ())), preferred_element_type=F32)


def start_fetch(use_own, own, other, held, sems):
    @pl.when(use_own)
    def _():
        for i in range(len(own)):
            pltpu.make_async_copy(own[i], held[i], sems.at[i]).start()

    @pl.when(jnp.logical_not(use_own))
    def _():
        for i in range(len(own)):
            pltpu.make_async_copy(other[i], held[i], sems.at[i]).start()


def wait_fetch(i, own, held, sems):
    pltpu.make_async_copy(own[i], held[i], sems.at[i]).wait()


def row_blocks(total, body):
    def step(i, carry):
        body(pl.ds(pl.multiple_of(i * RB, RB), RB))
        return carry

    lax.fori_loop(0, total // RB, step, 0)


def norm_rows(residue):
    center = residue - jnp.mean(residue, axis=-1, keepdims=True)
    inverse = lax.rsqrt(jnp.mean(center * center, axis=-1, keepdims=True) + epsilon)
    return center * inverse, inverse


def norm_back_rows(upstream, normal, inverse, gain):
    scaled = upstream * gain
    centred = scaled - jnp.mean(scaled, axis=-1, keepdims=True)
    return (centred - normal * jnp.mean(scaled * normal, axis=-1, keepdims=True)) * inverse


def column_sum(rows):
    return jnp.sum(rows, axis=0, keepdims=True)


def segment_bias(flags, bias):
    size = bias.shape[0]
    ends = [flags[2]]
    for i in range(3, 5):
        ends.append(ends[-1] + flags[i])
    row = lax.broadcasted_iota(jnp.int32, (1, size), 1)
    row_seg = sum((row >= e).astype(jnp.int32) for e in ends)

    def body(rows):
        col = lax.broadcasted_iota(jnp.int32, (RB, 1), 0) + rows.start
        col_seg = sum((col >= e).astype(jnp.int32) for e in ends)
        bias[rows, :] = jnp.where(col_seg == row_seg, 0.0, -1e30).astype(F32)

    row_blocks(size, body)


def attention_forward(flags, x, vec, weights, wait, outs, scratch):
    wq, wk, wv, wo = weights
    q_out, k_out, v_out, e_out, r_out, o_out, ot_out, p_out = outs
    qt_s, kh_s, vt_s, bias = scratch
    size = x.shape[0]
    width = wq.shape[1]
    heads = width // HD
    segment_bias(flags, bias)
    wait(0)
    wait(1)
    wait(2)
    for i in range(size // 256):
        rows = pl.ds(i * 256, 256)
        xb = x[rows, :]
        q = (dot(xb, wq[...]) + vec[V_BQV : V_BQV + 1, :width]).astype(BF).astype(F32) * (
            1.0 / math.sqrt(HD)
        )
        q_out[rows, :] = q.astype(BF)
        qt_s[:, rows] = q.T.astype(BF)
        k = dot(xb, wk[...]).astype(BF)
        k_out[rows, :] = k
        for h in range(heads):
            kh_s[h, rows, :] = k[:, h * HD : (h + 1) * HD]
        v = dot(xb, wv[...]) + vec[V_BQV : V_BQV + 1, width : 2 * width]
        v_out[rows, :] = v.astype(BF)
        vt_s[:, rows] = v.T.astype(BF)
    for h in range(heads):
        hs = slice(h * HD, (h + 1) * HD)
        for j in range(size // 256):
            cols = pl.ds(j * 256, 256)
            scores = dot(kh_s[h], qt_s[hs, cols]) + bias[:, cols]
            highest = jnp.max(scores, axis=0, keepdims=True)
            raised = jnp.exp(scores - highest)
            inverse = 1.0 / jnp.sum(raised, axis=0, keepdims=True)
            raised = raised.astype(BF)
            e_out[h, :, cols] = raised
            r_out[h : h + 1, cols] = inverse
            ot_out[hs, cols] = dot(vt_s[hs, :], raised) * inverse
    wait(3)
    for i in range(size // 256):
        rows = pl.ds(i * 256, 256)
        context = ot_out[:, rows].T.astype(BF)
        o_out[rows, :] = context
        p_out[rows, :] = dot(context, wo[...]).astype(BF)


def attention_first_kernel(
    flags, own, far, peer_a, peer_b, vec,
    wq, wk, wv, wo, wq2, wk2, wv2, wo2,
    x_out, q_out, k_out, v_out, e_out, r_out, o_out, ot_out, p_out,
    wq_s, wk_s, wv_s, wo_s, qt_s, kh_s, vt_s, bias, sems,
):
    first = flags[0] == 0
    held = (wq_s, wk_s, wv_s, wo_s)
    source = (wq, wk, wv, wo)
    start_fetch(first, source, (wq2, wk2, wv2, wo2), held, sems)
    half = own.shape[0]
    mine = pl.multiple_of(flags[1] * half, half)
    theirs = pl.multiple_of((1 - flags[1]) * half, half)
    x_out[pl.ds(mine, half), :] = jnp.where(first, own[...], far[...])
    x_out[pl.ds(theirs, half), :] = jnp.where(first, peer_a[...], peer_b[...])
    attention_forward(
        flags, x_out, vec, held, lambda i: wait_fetch(i, source, held, sems),
        (q_out, k_out, v_out, e_out, r_out, o_out, ot_out, p_out), (qt_s, kh_s, vt_s, bias),
    )


def attention_next_kernel(
    flags, normal_one, part_a, part_b, vec_prev, vec,
    wq, wk, wv, wo, wq2, wk2, wv2, wo2,
    n2_out, i2_out, x_out, q_out, k_out, v_out, e_out, r_out, o_out, ot_out, p_out,
    wq_s, wk_s, wv_s, wo_s, qt_s, kh_s, vt_s, bias, sems,
):
    held = (wq_s, wk_s, wv_s, wo_s)
    source = (wq, wk, wv, wo)
    start_fetch(flags[0] == 1, source, (wq2, wk2, wv2, wo2), held, sems)

    def body(rows):
        normal, inverse, output = second_norm(normal_one, part_a, part_b, vec_prev, rows)
        n2_out[rows, :] = normal
        i2_out[rows, :] = inverse
        x_out[rows, :] = output.astype(BF)

    row_blocks(x_out.shape[0], body)
    attention_forward(
        flags, x_out, vec, held, lambda i: wait_fetch(i, source, held, sems),
        (q_out, k_out, v_out, e_out, r_out, o_out, ot_out, p_out), (qt_s, kh_s, vt_s, bias),
    )


def second_norm(normal_one, part_a, part_b, vec, rows):
    normed = normal_one[rows, :] * vec[V_G1 : V_G1 + 1, :] + vec[V_B1 : V_B1 + 1, :]
    total = part_a[rows, :].astype(F32) + part_b[rows, :].astype(F32)
    normal, inverse = norm_rows(total + vec[V_BU : V_BU + 1, :] + normed)
    return normal, inverse, normal * vec[V_G2 : V_G2 + 1, :] + vec[V_B2 : V_B2 + 1, :]


def ffn_forward_kernel(
    layer, flags, x, part_a, part_b, vec, wi, wu, wi2, wu2,
    n1_out, i1_out, n1b_out, a_out, d_out, p_out,
    wi_s, wu_s, sems,
):
    held = (wi_s, wu_s)
    source = (wi, wu)
    start_fetch(flags[0] == layer, source, (wi2, wu2), held, sems)
    size = x.shape[0]
    width = wi_s.shape[1]
    model = wi_s.shape[0]

    def first(rows):
        total = part_a[rows, :].astype(F32) + part_b[rows, :].astype(F32)
        normal, inverse = norm_rows(total + vec[V_BO : V_BO + 1, :] + x[rows, :].astype(F32))
        n1_out[rows, :] = normal
        i1_out[rows, :] = inverse
        n1b_out[rows, :] = (normal * vec[V_G1 : V_G1 + 1, :] + vec[V_B1 : V_B1 + 1, :]).astype(BF)

    row_blocks(size, first)
    wait_fetch(0, source, held, sems)
    block = 256

    def inner(rows):
        rows_in = n1b_out[rows, :]
        for j in range(width // block):
            cols = slice(j * block, (j + 1) * block)
            at = j * block
            bias = vec[V_BI + at // model : V_BI + at // model + 1, at % model : at % model + block]
            hidden = dot(rows_in, wi_s[:, cols]) + bias
            spread = 0.5 + 0.5 * lax.erf(hidden * root_half)
            a_out[rows, cols] = (hidden * spread).astype(BF)
            d_out[rows, cols] = (
                spread + hidden * jnp.exp(-0.5 * hidden * hidden) * inverse_root
            ).astype(BF)

    row_blocks(size, inner)
    wait_fetch(1, source, held, sems)
    for i in range(size // 256):
        rows = pl.ds(i * 256, 256)
        p_out[rows, :] = dot(a_out[rows, :], wu_s[...]).astype(BF)


def ffn_backward(g2, d, w, outs, wait, small):
    wi_s, wu_s = w
    gh_out, p_out = outs
    size = g2.shape[0]
    model, width = wi_s.shape
    wait(1)
    sums = [jnp.zeros((1, model), F32)] * (width // model)
    for i in range(size // 256):
        rows = pl.ds(i * 256, 256)
        gb = g2[rows, :]
        for j in range(width // 384):
            cols = slice(j * 384, (j + 1) * 384)
            gh_out[rows, cols] = (dot_nt(gb, wu_s[cols, :]) * d[rows, cols].astype(F32)).astype(BF)
    wait(0)
    for i in range(size // 256):
        rows = pl.ds(i * 256, 256)
        gh = gh_out[rows, :]
        for j in range(width // model):
            part = gh[:, j * model : (j + 1) * model].astype(F32)
            sums[j] = sums[j] + column_sum(part)
        p_out[rows, :] = dot_nt(gh, wi_s[...]).astype(BF)
    for j in range(width // model):
        small[3 + j : 4 + j, :] = sums[j]


def ffn_back_last_kernel(
    flags, normal_one, part_a, part_b, vec, own, far, peer_a, peer_b, d, wi, wu, wi2, wu2,
    y_out, g_out, gb_out, gh_out, p_out, small,
    gy_s, wi_s, wu_s, sems,
):
    held = (wi_s, wu_s)
    source = (wi, wu)
    second = flags[0] == 1
    start_fetch(second, source, (wi2, wu2), held, sems)
    half = own.shape[0]
    mine = pl.multiple_of(flags[1] * half, half)
    theirs = pl.multiple_of((1 - flags[1]) * half, half)
    gy_s[pl.ds(mine, half), :] = jnp.where(second, own[...], far[...])
    gy_s[pl.ds(theirs, half), :] = jnp.where(second, peer_a[...], peer_b[...])
    small[...] = jnp.zeros_like(small)

    def body(rows):
        normal, inverse, output = second_norm(normal_one, part_a, part_b, vec, rows)
        y_out[rows, :] = output.astype(BF)
        ffn_back_rows(gy_s[rows, :].astype(F32), normal, inverse, vec, rows, g_out, gb_out, small)

    row_blocks(y_out.shape[0], body)
    ffn_backward(gb_out, d, held, (gh_out, p_out), lambda i: wait_fetch(i, source, held, sems), small)


def ffn_back_rows(upstream, normal, inverse, vec, rows, g_out, gb_out, small):
    grad = norm_back_rows(upstream, normal, inverse, vec[V_G2 : V_G2 + 1, :])
    g_out[rows, :] = grad
    gb_out[rows, :] = grad.astype(BF)
    small[0:1, :] += column_sum(grad)
    small[1:2, :] += column_sum(upstream * normal)
    small[2:3, :] += column_sum(upstream)


def ffn_back_next_kernel(
    flags, g1, part_a, part_b, normal_two, inverse_two, vec, d, wi, wu, wi2, wu2,
    g_out, gb_out, gh_out, p_out, small,
    wi_s, wu_s, sems,
):
    held = (wi_s, wu_s)
    source = (wi, wu)
    start_fetch(flags[0] == 0, source, (wi2, wu2), held, sems)
    small[...] = jnp.zeros_like(small)

    def body(rows):
        total = part_a[rows, :].astype(F32) + part_b[rows, :].astype(F32)
        upstream = (g1[rows, :] + total).astype(BF).astype(F32)
        ffn_back_rows(
            upstream, normal_two[rows, :], inverse_two[rows, :], vec, rows, g_out, gb_out, small
        )

    row_blocks(g1.shape[0], body)
    ffn_backward(gb_out, d, held, (gh_out, p_out), lambda i: wait_fetch(i, source, held, sems), small)


def attention_back_kernel(
    layer, flags, g2, part_a, part_b, normal_one, inverse_one, vec, q, k, v, e, r, ot_f,
    wq, wk, wv, wo, wq2, wk2, wv2, wo2,
    g_out, gb_out, gqkv_out, p_out, small,
    wq_s, wk_s, wv_s, wo_s, got_s, go_s, kt_s, vh_s, qh_s, gqt_s, delta_s, sems,
):
    held = (wq_s, wk_s, wv_s, wo_s)
    source = (wq, wk, wv, wo)
    start_fetch(flags[0] == layer, source, (wq2, wk2, wv2, wo2), held, sems)
    size, model = g2.shape
    width = q.shape[1]
    heads = width // HD
    small[...] = jnp.zeros_like(small)

    def body(rows):
        total = part_a[rows, :].astype(F32) + part_b[rows, :].astype(F32)
        upstream = g2[rows, :] + total
        normal = normal_one[rows, :]
        grad = norm_back_rows(upstream, normal, inverse_one[rows, :], vec[V_G1 : V_G1 + 1, :])
        g_out[rows, :] = grad
        gb_out[rows, :] = grad.astype(BF)
        small[0:1, :] += column_sum(grad)
        small[1:2, :] += column_sum(upstream * normal)
        small[2:3, :] += column_sum(upstream)

    row_blocks(size, body)
    for i in range(size // 256):
        rows = pl.ds(i * 256, 256)
        kt_s[:, rows] = k[rows, :].astype(F32).T.astype(BF)
        for h in range(heads):
            hs = slice(h * HD, (h + 1) * HD)
            vh_s[h, rows, :] = v[rows, hs]
            qh_s[h, rows, :] = q[rows, hs]
    wait_fetch(3, source, held, sems)
    for i in range(size // 256):
        rows = pl.ds(i * 256, 256)
        got = dot_nt(gb_out[rows, :], wo_s[...]).T
        for h in range(heads):
            hs = slice(h * HD, (h + 1) * HD)
            scaled = (got[hs, :] * r[h : h + 1, rows]).astype(BF)
            got_s[hs, rows] = scaled
            scaled = scaled.astype(F32)
            delta_s[h : h + 1, rows] = column_sum(scaled * ot_f[hs, rows])
            go_s[h, rows, :] = scaled.T.astype(BF)
    for h in range(heads):
        hs = slice(h * HD, (h + 1) * HD)
        grad_v = jnp.zeros((size, HD), F32)
        grad_k = jnp.zeros((size, HD), F32)
        for j in range(size // 256):
            cols = pl.ds(j * 256, 256)
            raised = e[h, :, cols]
            grad_p = dot(vh_s[h], got_s[hs, cols]) - delta_s[h : h + 1, cols]
            grad_s = (raised.astype(F32) * grad_p).astype(BF)
            grad_v = grad_v + dot(raised, go_s[h, cols, :])
            grad_k = grad_k + dot(grad_s, qh_s[h, cols, :])
            gqt_s[hs, cols] = dot(kt_s[hs, :], grad_s) * (1.0 / math.sqrt(HD))
        gqkv_out[:, width + h * HD : width + (h + 1) * HD] = grad_k.astype(BF)
        gqkv_out[:, 2 * width + h * HD : 2 * width + (h + 1) * HD] = grad_v.astype(BF)
    wait_fetch(0, source, held, sems)
    wait_fetch(1, source, held, sems)
    wait_fetch(2, source, held, sems)
    sum_q = jnp.zeros((1, width), F32)
    sum_v = jnp.zeros((1, width), F32)
    for i in range(size // 256):
        rows = pl.ds(i * 256, 256)
        gq = gqt_s[:, rows].T.astype(BF)
        gqkv_out[rows, :width] = gq
        gk = gqkv_out[rows, width : 2 * width]
        gv = gqkv_out[rows, 2 * width :]
        sum_q = sum_q + column_sum(gq.astype(F32))
        sum_v = sum_v + column_sum(gv.astype(F32))
        p_out[rows, :] = (
            dot_nt(gq, wq_s[...]) + dot_nt(gk, wk_s[...]) + dot_nt(gv, wv_s[...])
        ).astype(BF)
    small[3:4, :width] = sum_q
    small[3:4, width:] = sum_v


def call(kernel, operands, spaces, outs, scratch, flops):
    specs = {
        "s": pl.BlockSpec(memory_space=pltpu.SMEM),
        "v": pl.BlockSpec(memory_space=pltpu.VMEM),
        "a": pl.BlockSpec(memory_space=pl.ANY),
    }
    return pl.pallas_call(
        kernel,
        out_shape=[jax.ShapeDtypeStruct(s, t) for s, t in outs],
        in_specs=[specs[c] for c in spaces],
        out_specs=[specs["v"]] * len(outs),
        scratch_shapes=scratch,
        compiler_params=pltpu.CompilerParams(vmem_limit_bytes=VMEM_BYTES),
        cost_estimate=pl.CostEstimate(flops=flops, bytes_accessed=8 << 20, transcendentals=0),
    )(*operands)


def attention_call(flags, lead, lead_spaces, weights, size, model, width, kernel, extra_outs):
    heads = width // HD
    outs = extra_outs + [
        ((size, model), BF),
        ((size, width), BF),
        ((size, width), BF),
        ((size, width), BF),
        ((heads, size, size), BF),
        ((heads, size), F32),
        ((size, width), BF),
        ((width, size), F32),
        ((size, model), BF),
    ]
    scratch = [pltpu.VMEM((model, width), BF)] * 3 + [
        pltpu.VMEM((width, model), BF),
        pltpu.VMEM((width, size), BF),
        pltpu.VMEM((heads, size, HD), BF),
        pltpu.VMEM((width, size), BF),
        pltpu.VMEM((size, size), F32),
        pltpu.SemaphoreType.DMA((4,)),
    ]
    return call(
        kernel, (flags,) + lead + weights, "s" + lead_spaces + "a" * 8, outs, scratch,
        2 * size * width * model * 4 + 4 * heads * size * size * HD,
    )


def swap(block, axis):
    return lax.ppermute(block, axis, [(0, 1), (1, 0)])


def across(block, routes):
    return lax.ppermute(
        block, ("section", "tensor"), [(a[0] * 2 + a[1], b[0] * 2 + b[1]) for a, b in routes]
    )


def reduce_rows(block, x_first):
    count = lax.axis_size("batch")
    place = lax.axis_index("batch")

    def send(rows, pairs):
        return lax.ppermute(rows, "batch", pairs)

    if count != 8:
        if count & (count - 1):
            return lax.psum(block, "batch")
        step = 1
        while step < count:
            block = block + send(block, [(i, i ^ step) for i in range(count)])
            step *= 2
        return block
    half = block.shape[0] // 2
    side = place % 2
    line = place // 2
    inward = [(0, 2), (1, 3), (6, 4), (7, 5)]
    middle = [(2, 4), (3, 5), (4, 2), (5, 3)]
    outward = [(b, a) for a, b in inward]
    edge = (line == 0) | (line == 3)

    def part(which):
        return lax.dynamic_slice_in_dim(block, which * half, half, 0)

    def join(which, mine, theirs):
        low = jnp.where(which == 0, mine, theirs)
        high = jnp.where(which == 0, theirs, mine)
        return jnp.concatenate([low, high], axis=0)

    if x_first:
        pairs = [(i, i ^ 1) for i in range(8)]
        mine = part(side) + send(part(1 - side), pairs)
        mine = mine + send(mine, inward)
        mine = mine + send(mine, middle)
        mine = jnp.where(edge, send(mine, outward), mine)
        return join(side, mine, send(mine, pairs))
    block = block + send(block, inward)
    which = (line >= 2).astype(jnp.int32)
    mine = part(which) + send(part(1 - which), middle)
    mine = mine + send(mine, [(i, i ^ 1) for i in range(2, 6)])
    block = join(which, mine, send(mine, middle))
    return jnp.where(edge, send(block, outward), block)


def pad_rows(rows, count):
    return jnp.concatenate([rows, jnp.zeros((count - rows.shape[0], rows.shape[1]), rows.dtype)], 0)


def shards(
    section_ends, lengths, w_query, b_query, w_key, w_value, b_value, w_out, b_out,
    norm1_gain, norm1_bias, w_inner, b_inner, w_outer, b_outer, norm2_gain, norm2_bias,
):
    section = lax.axis_index("section")
    tensor = lax.axis_index("tensor")
    first = section == 0
    held = section_ends[0]
    half, model = held.shape[1], held.shape[2]
    size = 2 * half
    width = w_query.shape[2]
    inner = w_inner.shape[2]
    heads = width // HD
    flags = jnp.concatenate(
        [
            jnp.stack([section, tensor]).astype(jnp.int32),
            lax.dynamic_slice_in_dim(lengths, section, 1, 0)[0],
        ]
    )

    x_peer_a = across(held[0], [((0, 0), (0, 1)), ((0, 1), (0, 0))])
    x_peer_b = across(held[1], [((0, 0), (1, 1)), ((0, 1), (1, 0))])
    x_far = across(held[1], [((0, 0), (1, 0)), ((0, 1), (1, 1))])

    attention_own = (w_query[0], w_key[0], w_value[0], w_out[0])
    ffn_own = (w_inner[0], w_outer[0])
    vec_own = pad_rows(
        jnp.concatenate(
            [
                jnp.concatenate([b_query, b_value], axis=1),
                b_out, norm1_gain, norm1_bias, b_inner.reshape(-1, model), b_outer,
                norm2_gain, norm2_bias,
            ],
            axis=0,
        ),
        V_ROWS,
    )
    vec_far = swap(vec_own, "section")
    attention_far = tuple(swap(w, "section") for w in attention_own)
    ffn_far = tuple(swap(w, "section") for w in ffn_own)
    attention_w = attention_own + attention_far
    ffn_w = ffn_own + ffn_far
    vec_one = jnp.where(first, vec_own, vec_far)
    vec_two = jnp.where(first, vec_far, vec_own)

    gy_peer_a = across(held[1], [((1, 0), (1, 1)), ((1, 1), (1, 0))])
    gy_peer_b = across(held[0], [((1, 0), (0, 1)), ((1, 1), (0, 0))])
    gy_far = across(held[0], [((1, 0), (0, 0)), ((1, 1), (0, 1))])

    def ffn_forward(layer, x, part, vec):
        return call(
            functools.partial(ffn_forward_kernel, layer),
            (flags, x, part, swap(part, "tensor"), vec) + ffn_w,
            "svvvvaaaa",
            [
                ((size, model), F32), ((size, 1), F32), ((size, model), BF),
                ((size, inner), BF), ((size, inner), BF), ((size, model), BF),
            ],
            [
                pltpu.VMEM((model, inner), BF), pltpu.VMEM((inner, model), BF),
                pltpu.SemaphoreType.DMA((2,)),
            ],
            4 * size * model * inner,
        )

    x_one, *heads_one, part = attention_call(
        flags, (held[0], x_far, x_peer_a, x_peer_b, vec_one), "vvvvv", attention_w,
        size, model, width, attention_first_kernel, [],
    )
    n1_one, i1_one, n1b_one, a_one, d_one, part = ffn_forward(0, x_one, part, vec_one)
    n2_one, i2_one, x_two, *heads_two, part = attention_call(
        flags, (n1_one, part, swap(part, "tensor"), vec_one, vec_two), "vvvvv", attention_w,
        size, model, width, attention_next_kernel, [((size, model), F32), ((size, 1), F32)],
    )
    n1_two, i1_two, n1b_two, a_two, d_two, part = ffn_forward(1, x_two, part, vec_two)

    ffn_outs = [
        ((size, model), F32), ((size, model), BF), ((size, inner), BF), ((size, model), BF),
        ((8, model), F32),
    ]
    ffn_scratch = [
        pltpu.VMEM((model, inner), BF), pltpu.VMEM((inner, model), BF),
        pltpu.SemaphoreType.DMA((2,)),
    ]

    def reduce_pair(first_left, first_right, second_left, second_right, small, x_first):
        def product(left, right):
            return lax.dot_general(
                left, right, (((0,), (0,)), ((), ())), preferred_element_type=F32
            ).astype(BF)

        def both(pairs):
            return jnp.concatenate([product(*p) for p in pairs] + [small], axis=0)

        one, two = zip(first_left, first_right), zip(second_left, second_right)
        one, two = list(one), list(two)
        sent = [
            (jnp.where(first, b[0], a[0]), jnp.where(first, b[1], a[1])) for a, b in zip(one, two)
        ]
        kept = [
            (jnp.where(first, a[0], b[0]), jnp.where(first, a[1], b[1])) for a, b in zip(one, two)
        ]
        got = swap(both(sent), "section")
        return reduce_rows(both(kept) + got, x_first)

    def ffn_reduce(a, gb, gh, n1b, small, x_first):
        return reduce_pair(
            (a,), (gb,), (gh,), (n1b,), pad_rows(small.astype(BF), SMALL_ROWS), x_first
        )

    def attention_back(layer, g2, part, n1, i1, vec, saved):
        q, k, v, e, r, o, ot_f = saved
        return call(
            functools.partial(attention_back_kernel, layer),
            (flags, g2, part, swap(part, "tensor"), n1, i1, vec, q, k, v, e, r, ot_f) + attention_w,
            "s" + "v" * 12 + "a" * 8,
            [
                ((size, model), F32), ((size, model), BF), ((size, 3 * width), BF),
                ((size, model), BF), ((8, model), F32),
            ],
            [pltpu.VMEM((model, width), BF)] * 3
            + [
                pltpu.VMEM((width, model), BF),
                pltpu.VMEM((width, size), BF),
                pltpu.VMEM((heads, size, HD), BF),
                pltpu.VMEM((width, size), BF),
                pltpu.VMEM((heads, size, HD), BF),
                pltpu.VMEM((heads, size, HD), BF),
                pltpu.VMEM((width, size), F32),
                pltpu.VMEM((8, size), F32),
                pltpu.SemaphoreType.DMA((4,)),
            ],
            2 * size * width * model * 4 + 8 * heads * size * size * HD,
        )

    def attention_reduce(gqkv, x, o, gb, small, x_first):
        gq, gk, gv = (gqkv[:, i * width : (i + 1) * width] for i in range(3))
        return reduce_pair(
            (gq, gk), (x, x), (gv, o), (x, gb), pad_rows(small.astype(BF), SMALL_ROWS), x_first
        )

    y_two, g2_two, g2b_two, gh_two, part, small_f2 = call(
        ffn_back_last_kernel,
        (flags, n1_two, part, swap(part, "tensor"), vec_two, held[1], gy_far, gy_peer_a, gy_peer_b,
         d_two) + ffn_w,
        "s" + "v" * 9 + "a" * 4,
        [((size, model), BF)] + ffn_outs,
        [pltpu.VMEM((size, model), BF)] + ffn_scratch,
        4 * size * model * inner,
    )
    sum_f2 = ffn_reduce(a_two, g2b_two, gh_two, n1b_two, small_f2, True)
    g1_two, g1b_two, gqkv_two, part, small_a2 = attention_back(
        1, g2_two, part, n1_two, i1_two, vec_two, heads_two
    )
    sum_a2 = attention_reduce(gqkv_two, x_two, heads_two[5], g1b_two, small_a2, False)

    g2_one, g2b_one, gh_one, part, small_f1 = call(
        ffn_back_next_kernel,
        (flags, g1_two, part, swap(part, "tensor"), n2_one, i2_one, vec_one, d_one) + ffn_w,
        "s" + "v" * 7 + "a" * 4,
        ffn_outs,
        ffn_scratch,
        4 * size * model * inner,
    )
    sum_f1 = ffn_reduce(a_one, g2b_one, gh_one, n1b_one, small_f1, False)
    g1_one, g1b_one, gqkv_one, part, small_a1 = attention_back(
        0, g2_one, part, n1_one, i1_one, vec_one, heads_one
    )
    sum_a1 = attention_reduce(gqkv_one, x_one, heads_one[5], g1b_one, small_a1, True)

    part_mine = lax.dynamic_slice_in_dim(part, tensor * half, half, 0)
    part_theirs = lax.dynamic_slice_in_dim(part, (1 - tensor) * half, half, 0)
    total = part_mine.astype(F32) + swap(part_theirs, "tensor").astype(F32)
    gx = (lax.dynamic_slice_in_dim(g1_one, tensor * half, half, 0) + total).astype(BF)
    y_mine = lax.dynamic_slice_in_dim(y_two, tensor * half, half, 0)
    y_far = lax.ppermute(y_mine, "section", [(0, 1)])
    gx_far = lax.ppermute(gx, "section", [(1, 0)])
    section_results = jnp.stack(
        [jnp.where(first, gx, y_far), jnp.where(first, gx_far, y_mine)], axis=0
    )[None]

    def exchange(sum_one, sum_two):
        far_two = lax.ppermute(sum_two, "section", [(0, 1)])
        far_one = lax.ppermute(sum_one, "section", [(1, 0)])
        return (
            jnp.where(first, sum_one, far_two).astype(F32),
            jnp.where(first, far_one, sum_two).astype(F32),
        )

    ffn_first, ffn_second = exchange(sum_f1, sum_f2)
    att_first, att_second = exchange(sum_a1, sum_a2)
    small_f = ffn_first[inner:]
    small_a = att_first[2 * width :]
    return (
        section_results,
        att_first[:width].T[None],
        small_a[3:4, :width],
        att_first[width : 2 * width].T[None],
        att_second[:width].T[None],
        small_a[3:4, width:],
        att_second[width : 2 * width][None],
        small_a[0:1],
        small_a[1:2],
        small_a[2:3],
        ffn_second[:inner].T[None],
        small_f[3 : 3 + inner // model].reshape(1, inner),
        ffn_first[:inner][None],
        small_f[0:1],
        small_f[1:2],
        small_f[2:3],
    )


def solution(mesh):
    in_specs = (
        P("section", "batch", "tensor", None),
        P("batch", None),
        P("section", None, "tensor"),
        P("section", "tensor"),
        P("section", None, "tensor"),
        P("section", None, "tensor"),
        P("section", "tensor"),
        P("section", "tensor", None),
        P("section", None),
        P("section", None),
        P("section", None),
        P("section", None, "tensor"),
        P("section", "tensor"),
        P("section", "tensor", None),
        P("section", None),
        P("section", None),
        P("section", None),
    )
    out_specs = (
        P("section", "batch", "tensor", None),
        P("section", None, "tensor"),
        P("section", "tensor"),
        P("section", None, "tensor"),
        P("section", None, "tensor"),
        P("section", "tensor"),
        P("section", "tensor", None),
        P("section", None),
        P("section", None),
        P("section", None),
        P("section", None, "tensor"),
        P("section", "tensor"),
        P("section", "tensor", None),
        P("section", None),
        P("section", None),
        P("section", None),
    )
    return jax.shard_map(shards, mesh=mesh, in_specs=in_specs, out_specs=out_specs, check_vma=False)
```

```python
import functools
import math

import jax
import jax.numpy as jnp
from jax import lax
from jax.experimental import pallas as pl
from jax.experimental.pallas import tpu as pltpu
from jax.sharding import PartitionSpec as P

HD = 64
epsilon = 1e-06
root_half = 0.7071067811865476
inverse_root = 0.3989422804014327
BF = jnp.bfloat16
F32 = jnp.float32
RB = 128
VMEM_BYTES = 56 * 1024 * 1024

V_BQV, V_BO, V_G1, V_B1, V_BI, V_BU, V_G2, V_B2 = 0, 1, 2, 3, 4, 6, 7, 8
V_ROWS = 16


def dot(a, b):
    return lax.dot_general(a, b, (((1,), (0,)), ((), ())), preferred_element_type=F32)


def dot_nt(a, b):
    return lax.dot_general(a, b, (((1,), (1,)), ((), ())), preferred_element_type=F32)


def dot_tn(a, b):
    return lax.dot_general(a, b, (((0,), (0,)), ((), ())), preferred_element_type=F32)


def start_fetch(use_own, own, other, held, sems):
    @pl.when(use_own)
    def _():
        for i in range(len(own)):
            pltpu.make_async_copy(own[i], held[i], sems.at[i]).start()

    @pl.when(jnp.logical_not(use_own))
    def _():
        for i in range(len(own)):
            pltpu.make_async_copy(other[i], held[i], sems.at[i]).start()


def wait_fetch(i, own, held, sems):
    pltpu.make_async_copy(own[i], held[i], sems.at[i]).wait()


def row_blocks(total, body):
    def step(i, carry):
        body(pl.ds(pl.multiple_of(i * RB, RB), RB))
        return carry

    lax.fori_loop(0, total // RB, step, 0)


def loop(count, body, unroll=1):
    def step(i, carry):
        for j in range(unroll):
            body(i * unroll + j)
        return carry

    lax.fori_loop(0, count // unroll, step, 0)


def part_of(i, step):
    return pl.ds(i * step if isinstance(i, int) else pl.multiple_of(i * step, step), step)


def norm_rows(residue):
    center = residue - jnp.mean(residue, axis=-1, keepdims=True)
    inverse = lax.rsqrt(jnp.mean(center * center, axis=-1, keepdims=True) + epsilon)
    return center * inverse, inverse


def norm_back_rows(upstream, normal, inverse, gain):
    scaled = upstream * gain
    centred = scaled - jnp.mean(scaled, axis=-1, keepdims=True)
    return (centred - normal * jnp.mean(scaled * normal, axis=-1, keepdims=True)) * inverse


def column_sum(rows):
    return jnp.sum(rows, axis=0, keepdims=True)


def segment_bias(flags, bias):
    size = bias.shape[0]
    ends = [flags[2]]
    for i in range(3, 5):
        ends.append(ends[-1] + flags[i])
    row = lax.broadcasted_iota(jnp.int32, (1, size), 1)
    row_seg = sum((row >= e).astype(jnp.int32) for e in ends)

    def body(rows):
        col = lax.broadcasted_iota(jnp.int32, (RB, 1), 0) + rows.start
        col_seg = sum((col >= e).astype(jnp.int32) for e in ends)
        bias[rows, :] = jnp.where(col_seg == row_seg, 0.0, -1e30).astype(F32)

    row_blocks(size, body)


def attention_forward(flags, x, vec, weights, wait, outs, scratch):
    wq, wk, wv, wo = weights
    q_out, k_out, v_out, e_out, r_out, o_out, ot_out, *p_outs = outs
    qt_s, kh_s, vt_s, bias = scratch
    size = x.shape[0]
    width = wq.shape[1]
    heads = width // HD
    segment_bias(flags, bias)
    wait(0)
    wait(1)
    wait(2)

    def project(i):
        rows = part_of(i, 256)
        xb = x[rows, :]
        q = (dot(xb, wq[...]) + vec[V_BQV : V_BQV + 1, :width]).astype(BF).astype(F32) * (
            1.0 / math.sqrt(HD)
        )
        q_out[rows, :] = q.astype(BF)
        qt_s[:, rows] = q.T.astype(BF)
        k = dot(xb, wk[...]).astype(BF)
        k_out[rows, :] = k
        for h in range(heads):
            kh_s[h, rows, :] = k[:, h * HD : (h + 1) * HD]
        v = dot(xb, wv[...]) + vec[V_BQV : V_BQV + 1, width : 2 * width]
        v_out[rows, :] = v.astype(BF)
        vt_s[:, rows] = v.T.astype(BF)

    loop(size // 256, project)

    def attend(h):
        hs = part_of(h, HD)
        for j in range(size // 256):
            cols = pl.ds(j * 256, 256)
            scores = dot(kh_s[h], qt_s[hs, cols]) + bias[:, cols]
            highest = jnp.max(scores, axis=0, keepdims=True)
            raised = jnp.exp(scores - highest)
            inverse = 1.0 / jnp.sum(raised, axis=0, keepdims=True)
            raised = raised.astype(BF)
            e_out[h, :, cols] = raised
            r_out[h, :, cols] = inverse
            ot_out[hs, cols] = dot(vt_s[hs, :], raised) * inverse

    loop(heads, attend, 2)
    wait(3)

    for i, p_out in enumerate(p_outs):
        rows = part_of(i, size // 2)
        context = ot_out[:, rows].T.astype(BF)
        o_out[rows, :] = context
        p_out[...] = dot(context, wo[...]).astype(BF)


def attention_first_kernel(
    flags, own, far, peer_a, peer_b, vec,
    wq, wk, wv, wo, wq2, wk2, wv2, wo2,
    x_out, q_out, k_out, v_out, e_out, r_out, o_out, ot_out, p_out, p_out2,
    wq_s, wk_s, wv_s, wo_s, qt_s, kh_s, vt_s, bias, sems,
):
    first = flags[0] == 0
    held = (wq_s, wk_s, wv_s, wo_s)
    source = (wq, wk, wv, wo)
    start_fetch(first, source, (wq2, wk2, wv2, wo2), held, sems)
    half = own.shape[0]
    mine = pl.multiple_of(flags[1] * half, half)
    theirs = pl.multiple_of((1 - flags[1]) * half, half)
    x_out[pl.ds(mine, half), :] = jnp.where(first, own[...], far[...])
    x_out[pl.ds(theirs, half), :] = jnp.where(first, peer_a[...], peer_b[...])
    attention_forward(
        flags, x_out, vec, held, lambda i: wait_fetch(i, source, held, sems),
        (q_out, k_out, v_out, e_out, r_out, o_out, ot_out, p_out, p_out2), (qt_s, kh_s, vt_s, bias),
    )


def attention_next_kernel(
    flags, normal_one, part_a, part_a2, part_b, part_b2, vec_prev, vec,
    wq, wk, wv, wo, wq2, wk2, wv2, wo2,
    n2_out, i2_out, x_out, q_out, k_out, v_out, e_out, r_out, o_out, ot_out, p_out, p_out2,
    wq_s, wk_s, wv_s, wo_s, qt_s, kh_s, vt_s, bias, sems,
):
    held = (wq_s, wk_s, wv_s, wo_s)
    source = (wq, wk, wv, wo)
    start_fetch(flags[0] == 1, source, (wq2, wk2, wv2, wo2), held, sems)

    half = part_a.shape[0]
    for c, (one, two) in enumerate(((part_a, part_b), (part_a2, part_b2))):

        def body(rows, c=c, one=one, two=two):
            place = pl.ds(rows.start + c * half, RB)
            normal, inverse, output = second_norm(normal_one[place, :], one, two, vec_prev, rows)
            n2_out[place, :] = normal
            i2_out[place, :] = inverse
            x_out[place, :] = output.astype(BF)

        row_blocks(half, body)
    attention_forward(
        flags, x_out, vec, held, lambda i: wait_fetch(i, source, held, sems),
        (q_out, k_out, v_out, e_out, r_out, o_out, ot_out, p_out, p_out2), (qt_s, kh_s, vt_s, bias),
    )


def second_norm(normal_one, part_a, part_b, vec, rows):
    normed = normal_one * vec[V_G1 : V_G1 + 1, :] + vec[V_B1 : V_B1 + 1, :]
    total = part_a[rows, :].astype(F32) + part_b[rows, :].astype(F32)
    normal, inverse = norm_rows(total + vec[V_BU : V_BU + 1, :] + normed)
    return normal, inverse, normal * vec[V_G2 : V_G2 + 1, :] + vec[V_B2 : V_B2 + 1, :]


def ffn_forward_kernel(
    layer, flags, x, part_a, part_b, vec, wi, wu, wi2, wu2,
    n1_out, i1_out, n1b_out, a_out, d_out, p_out,
    wi_s, wu_s, sems,
):
    held = (wi_s, wu_s)
    source = (wi, wu)
    start_fetch(flags[0] == layer, source, (wi2, wu2), held, sems)
    size = x.shape[0]
    width = wi_s.shape[1]
    model = wi_s.shape[0]

    def first(rows):
        total = part_a[rows, :].astype(F32) + part_b[rows, :].astype(F32)
        normal, inverse = norm_rows(total + vec[V_BO : V_BO + 1, :] + x[rows, :].astype(F32))
        n1_out[rows, :] = normal
        i1_out[rows, :] = inverse
        n1b_out[rows, :] = (normal * vec[V_G1 : V_G1 + 1, :] + vec[V_B1 : V_B1 + 1, :]).astype(BF)

    row_blocks(size, first)
    wait_fetch(0, source, held, sems)
    block = 256

    def inner(rows):
        rows_in = n1b_out[rows, :]
        for j in range(width // block):
            cols = slice(j * block, (j + 1) * block)
            at = j * block
            bias = vec[V_BI + at // model : V_BI + at // model + 1, at % model : at % model + block]
            hidden = dot(rows_in, wi_s[:, cols]) + bias
            spread = 0.5 + 0.5 * lax.erf(hidden * root_half)
            a_out[rows, cols] = (hidden * spread).astype(BF)
            d_out[rows, cols] = (
                spread + hidden * jnp.exp(-0.5 * hidden * hidden) * inverse_root
            ).astype(BF)

    row_blocks(size, inner)
    wait_fetch(1, source, held, sems)

    def outer(i):
        rows = part_of(i, 256)
        p_out[rows, :] = dot(a_out[rows, :], wu_s[...]).astype(BF)

    loop(size // 256, outer)


def ffn_backward(g2, d, w, outs, wait, small):
    wi_s, wu_s = w
    gh_out, p_out = outs
    size = g2.shape[0]
    model, width = wi_s.shape
    wait(1)
    block = 384

    def hidden(i):
        rows = part_of(i, 256)
        gb = g2[rows, :]
        for j in range(width // block):
            cols = slice(j * block, (j + 1) * block)
            gh = (dot_nt(gb, wu_s[cols, :]) * d[rows, cols].astype(F32)).astype(BF)
            gh_out[rows, cols] = gh
            at = j * block
            small[3 + at // model : 4 + at // model, at % model : at % model + block] += column_sum(
                gh.astype(F32)
            )

    loop(size // 256, hidden)
    wait(0)

    def inner(i):
        rows = part_of(i, 256)
        p_out[rows, :] = dot_nt(gh_out[rows, :], wi_s[...]).astype(BF)

    loop(size // 256, inner)


def ffn_back_last_kernel(
    chunk, flags, normal_one, part_a, part_b, vec, own, far, peer_a, peer_b, d, small_in,
    wi, wu, wi2, wu2,
    y_out, g_out, gb_out, gh_out, p_out, small,
    gy_s, wi_s, wu_s, sems,
):
    held = (wi_s, wu_s)
    source = (wi, wu)
    second = flags[0] == 1
    start_fetch(second, source, (wi2, wu2), held, sems)
    here = flags[1] == chunk
    gy_s[...] = jnp.where(
        here,
        jnp.where(second, own[...], far[...]),
        jnp.where(second, peer_a[...], peer_b[...]),
    )
    small[...] = small_in[...]

    def body(rows):
        normal, inverse, output = second_norm(normal_one[rows, :], part_a, part_b, vec, rows)
        y_out[rows, :] = output.astype(BF)
        ffn_back_rows(gy_s[rows, :].astype(F32), normal, inverse, vec, rows, g_out, gb_out, small)

    row_blocks(y_out.shape[0], body)
    ffn_backward(gb_out, d, held, (gh_out, p_out), lambda i: wait_fetch(i, source, held, sems), small)


def ffn_back_rows(upstream, normal, inverse, vec, rows, g_out, gb_out, small):
    grad = norm_back_rows(upstream, normal, inverse, vec[V_G2 : V_G2 + 1, :])
    g_out[rows, :] = grad
    gb_out[rows, :] = grad.astype(BF)
    small[0:1, :] += column_sum(grad)
    small[1:2, :] += column_sum(upstream * normal)
    small[2:3, :] += column_sum(upstream)


def ffn_back_next_kernel(
    flags, g1, part_a, part_b, normal_two, inverse_two, vec, d, small_in, wi, wu, wi2, wu2,
    g_out, gb_out, gh_out, p_out, small,
    wi_s, wu_s, sems,
):
    held = (wi_s, wu_s)
    source = (wi, wu)
    start_fetch(flags[0] == 0, source, (wi2, wu2), held, sems)
    small[...] = small_in[...]

    def body(rows):
        total = part_a[rows, :].astype(F32) + part_b[rows, :].astype(F32)
        upstream = (g1[rows, :] + total).astype(BF).astype(F32)
        ffn_back_rows(
            upstream, normal_two[rows, :], inverse_two[rows, :], vec, rows, g_out, gb_out, small
        )

    row_blocks(g1.shape[0], body)
    ffn_backward(gb_out, d, held, (gh_out, p_out), lambda i: wait_fetch(i, source, held, sems), small)


def attention_back_kernel(
    layer, flags, g2, part_a, part_a2, part_b, part_b2, normal_one, inverse_one, vec,
    q, k, v, e, r, ot_f,
    wq, wk, wv, wo, wq2, wk2, wv2, wo2,
    g_out, gb_out, gqkv_out, p_out, p_out2, small,
    wq_s, wk_s, wv_s, wo_s, got_s, go_s, kt_s, vh_s, qh_s, gqt_s, sems,
):
    held = (wq_s, wk_s, wv_s, wo_s)
    source = (wq, wk, wv, wo)
    start_fetch(flags[0] == layer, source, (wq2, wk2, wv2, wo2), held, sems)
    size, model = g2.shape
    width = q.shape[1]
    heads = width // HD
    small[...] = jnp.zeros_like(small)

    half = size // 2
    for c, (one, two) in enumerate(((part_a, part_b), (part_a2, part_b2))):

        def body(rows, c=c, one=one, two=two):
            place = pl.ds(rows.start + c * half, RB)
            upstream = g2[place, :] + (one[rows, :].astype(F32) + two[rows, :].astype(F32))
            normal = normal_one[place, :]
            grad = norm_back_rows(upstream, normal, inverse_one[place, :], vec[V_G1 : V_G1 + 1, :])
            g_out[place, :] = grad
            gb_out[place, :] = grad.astype(BF)
            small[0:1, :] += column_sum(grad)
            small[1:2, :] += column_sum(upstream * normal)
            small[2:3, :] += column_sum(upstream)

        row_blocks(half, body)

    def split(i):
        rows = part_of(i, 256)
        kt_s[:, rows] = k[rows, :].astype(F32).T.astype(BF)
        for h in range(heads):
            hs = slice(h * HD, (h + 1) * HD)
            vh_s[h, rows, :] = v[rows, hs]
            qh_s[h, rows, :] = q[rows, hs]

    loop(size // 256, split)
    wait_fetch(3, source, held, sems)

    def context(i):
        rows = part_of(i, 256)
        gqt_s[:, rows] = dot_nt(gb_out[rows, :], wo_s[...]).T

    loop(size // 256, context)

    def attend(h):
        hs = part_of(h, HD)
        scaled = (gqt_s[hs, :] * r[h]).astype(BF)
        got_s[...] = scaled
        scaled = scaled.astype(F32)
        delta = column_sum(scaled * ot_f[hs, :])
        go_s[...] = scaled.T.astype(BF)
        grad_v = jnp.zeros((size, HD), F32)
        grad_k = jnp.zeros((size, HD), F32)
        for j in range(size // 256):
            cols = pl.ds(j * 256, 256)
            raised = e[h, :, cols]
            grad_p = dot(vh_s[h], got_s[:, cols]) - delta[:, j * 256 : (j + 1) * 256]
            grad_s = (raised.astype(F32) * grad_p).astype(BF)
            grad_v = grad_v + dot(raised, go_s[cols, :])
            grad_k = grad_k + dot(grad_s, qh_s[h, cols, :])
            gqt_s[hs, cols] = dot(kt_s[hs, :], grad_s) * (1.0 / math.sqrt(HD))
        vh_s[h] = grad_v.astype(BF)
        qh_s[h] = grad_k.astype(BF)

    loop(heads, attend, 2)
    for i in range(3):
        wait_fetch(i, source, held, sems)

    for i, p in enumerate((p_out, p_out2)):
        rows = pl.ds(i * half, half)
        gq = gqt_s[:, rows].T.astype(BF)
        gk = jnp.concatenate([qh_s[h, rows, :] for h in range(heads)], axis=1)
        gv = jnp.concatenate([vh_s[h, rows, :] for h in range(heads)], axis=1)
        gqkv_out[rows, :width] = gq
        gqkv_out[rows, width : 2 * width] = gk
        gqkv_out[rows, 2 * width :] = gv
        small[3:4, :width] += column_sum(gq.astype(F32))
        small[3:4, width:] += column_sum(gv.astype(F32))
        p[...] = (
            dot_nt(gq, wq_s[...]) + dot_nt(gk, wk_s[...]) + dot_nt(gv, wv_s[...])
        ).astype(BF)


HEAVY, LIGHT = 20, 0
PAD = 16


def unit_slot(flags, second, j):
    return 2 * (flags[0] ^ second) + (flags[6] ^ j)


def send_units(held, outs, sems):
    copies = []
    for u, units in enumerate(held):
        for i in range(4):
            copy = pltpu.make_async_copy(units.at[i], outs[4 * u + i], sems.at[4 * u + i])
            copy.start()
            copies.append(copy)
    for copy in copies:
        copy.wait()


def ffn_product_kernel(flags, a, gb, gh, n1b, small, *refs):
    outs, held, sems = refs[:8], refs[8:10], refs[10]
    model = gb.shape[1]
    block = model // 2
    extra = jnp.concatenate([small[...], jnp.zeros((PAD - 8, model), F32)], axis=0).astype(BF)
    for i in range(2):

        def products(j, i=i):
            outer, inside = unit_slot(flags, 0, j), unit_slot(flags, 1, j)
            held[i][outer, :block, :] = dot_tn(a[:, part_of(2 * j + i, block)], gb[...]).astype(BF)
            held[i][inside, :block, :] = dot_tn(
                n1b[:, i * block : (i + 1) * block], gh[:, part_of(j, model)]
            ).astype(BF)

        loop(2, products)
    for i in range(4):
        held[0][i, block:, :] = extra
    send_units(held, outs, sems)


def attention_product_kernel(flags, x, gqkv, o, gb, small, *refs):
    outs, held, sems = refs[:4], refs[4], refs[5]
    model = gb.shape[1]
    width = o.shape[1]

    def products(i):
        held[unit_slot(flags, i // 2, i % 2), :model, :] = dot_tn(
            x[...], gqkv[:, part_of(i, width)]
        ).astype(BF)

    loop(3, products)
    slot = unit_slot(flags, 1, 1)
    for i in range(2):
        held[slot, i * width : (i + 1) * width, :] = dot_tn(
            o[...], gb[:, i * width : (i + 1) * width]
        ).astype(BF)
    extra = jnp.concatenate([small[:, :width], small[:, width:]], axis=0).astype(BF)
    for i in range(4):
        held[i, model:, :] = extra
    send_units((held,), outs, sems)


def fetch_sums(flags, refs, held, sems):
    def copies(layer):
        for u, units in enumerate(held):
            for far in range(2):
                for beside in range(2):
                    slot = 2 * (flags[0] ^ far) + (flags[6] ^ beside)
                    i = 2 * far + beside
                    yield pltpu.make_async_copy(
                        refs[8 * u + 4 * layer + i], units.at[slot], sems.at[4 * u + i]
                    )

    for layer in range(2):

        @pl.when(flags[0] == layer)
        def _(layer=layer):
            for copy in copies(layer):
                copy.start()

    for copy in copies(0):
        copy.wait()


def ffn_finish_kernel(flags, *refs):
    sums, (outer, inside, small) = refs[:16], refs[16:19]
    held, sems = refs[19:21], refs[21]
    fetch_sums(flags, sums, held, sems)
    model = outer.shape[1]
    block = model // 2
    for u in range(2):
        for j in range(2):
            at = j * model + u * block
            outer[at : at + block, :] = held[u][j, :block, :].astype(F32)
            inside[u * block : (u + 1) * block, j * model : (j + 1) * model] = held[u][
                2 + j, :block, :
            ].astype(F32)
    small[...] = held[0][0, block : block + PAD, :].astype(F32)


def attention_finish_kernel(flags, *refs):
    sums, (q, k, v, out, small) = refs[:8], refs[8:13]
    held, sems = refs[13], refs[14]
    fetch_sums(flags, sums, (held,), sems)
    model, width = q.shape
    q[...] = held[0, :model, :].astype(F32)
    k[...] = held[1, :model, :].astype(F32)
    v[...] = held[2, :model, :].astype(F32)
    for i in range(2):
        out[:, i * width : (i + 1) * width] = held[3, i * width : (i + 1) * width, :].astype(F32)
    small[:, :width] = held[0, model : model + 8, :].astype(F32)
    small[:, width:] = held[0, model + 8 : model + 16, :].astype(F32)


def call(
    kernel, operands, spaces, outs, scratch, flops, after=(), out_space="v", chunk=0, before=(),
    weight=LIGHT,
):
    count = len(operands)
    out_space = out_space * len(outs) if len(out_space) == 1 else out_space
    passed = [i for i, c in enumerate(out_space) if c == "c" and before]
    extra = [before[i] for i in passed] + list(after)

    def body(*refs):
        kernel(*refs[:count], *refs[count + len(extra) :])

    def spec(letter, shape):
        if letter == "c":
            return pl.BlockSpec((shape[0] // 2, shape[1]), lambda i: (chunk, 0))
        return pl.BlockSpec(memory_space={"s": pltpu.SMEM, "v": pltpu.VMEM, "a": pl.ANY}[letter])

    return pl.pallas_call(
        body,
        grid=(1,) if "c" in spaces else (),
        out_shape=[jax.ShapeDtypeStruct(s, t) for s, t in outs],
        in_specs=[spec(c, x.shape) for c, x in zip(spaces, operands)]
        + [pl.BlockSpec(memory_space=pl.ANY)] * len(extra),
        out_specs=[spec(c, s) for c, (s, _) in zip(out_space, outs)],
        scratch_shapes=scratch,
        input_output_aliases={count + i: o for i, o in enumerate(passed)},
        compiler_params=pltpu.CompilerParams(vmem_limit_bytes=VMEM_BYTES),
        cost_estimate=pl.CostEstimate(
            flops=flops * weight, bytes_accessed=(8 << 20) * weight, transcendentals=0
        ),
    )(*operands, *extra)


def attention_call(flags, lead, lead_spaces, weights, size, model, width, kernel, extra_outs):
    heads = width // HD
    outs = extra_outs + [
        ((size, model), BF),
        ((size, width), BF),
        ((size, width), BF),
        ((size, width), BF),
        ((heads, size, size), BF),
        ((heads, 1, size), F32),
        ((size, width), BF),
        ((width, size), F32),
        ((size // 2, model), BF),
        ((size // 2, model), BF),
    ]
    scratch = [pltpu.VMEM((model, width), BF)] * 3 + [
        pltpu.VMEM((width, model), BF),
        pltpu.VMEM((width, size), BF),
        pltpu.VMEM((heads, size, HD), BF),
        pltpu.VMEM((width, size), BF),
        pltpu.VMEM((size, size), F32),
        pltpu.SemaphoreType.DMA((4,)),
    ]
    return call(
        kernel, (flags,) + lead + weights, "s" + lead_spaces + "a" * 8, outs, scratch,
        2 * size * width * model * 4 + 4 * heads * size * size * HD, weight=HEAVY,
    )


def swap(block, axis):
    return lax.ppermute(block, axis, [(0, 1), (1, 0)])


def across(block, routes):
    return lax.ppermute(
        block, ("section", "tensor"), [(a[0] * 2 + a[1], b[0] * 2 + b[1]) for a, b in routes]
    )


def batch_pairs():
    return [(i, i ^ 1) for i in range(lax.axis_size("batch"))]


def pair_swap(block):
    return lax.ppermute(block, "batch", batch_pairs())


def timed(block, token):
    return block if token is None else block + token[7:8, : block.shape[1]].astype(BF)


def line_in(mine, token=None):
    return timed(mine + lax.ppermute(mine, "batch", [(0, 2), (1, 3), (6, 4), (7, 5)]), token)


def line_middle(mine, token=None):
    return timed(mine + lax.ppermute(mine, "batch", [(2, 4), (3, 5), (4, 2), (5, 3)]), token)


def line_out(mine, token=None):
    line = lax.axis_index("batch") // 2
    got = lax.ppermute(mine, "batch", [(2, 0), (3, 1), (4, 6), (5, 7)])
    return timed(jnp.where((line == 0) | (line == 3), got, mine), token)


def line_stages():
    count = lax.axis_size("batch")
    if count == 8:
        return line_in, line_middle, line_out

    def rest(mine, token=None):
        if count & (count - 1):
            lines = [list(range(i, count, 2)) for i in range(2)]
            return lax.psum(mine, "batch", axis_index_groups=lines)
        step = 2
        while step < count:
            mine = mine + lax.ppermute(mine, "batch", [(i, i ^ step) for i in range(count)])
            step *= 2
        return mine

    return rest, lambda mine, token=None: mine, lambda mine, token=None: mine


def pad_rows(rows, count):
    return jnp.concatenate([rows, jnp.zeros((count - rows.shape[0], rows.shape[1]), rows.dtype)], 0)


def shards(
    section_ends, lengths, w_query, b_query, w_key, w_value, b_value, w_out, b_out,
    norm1_gain, norm1_bias, w_inner, b_inner, w_outer, b_outer, norm2_gain, norm2_bias,
):
    section = lax.axis_index("section")
    tensor = lax.axis_index("tensor")
    first = section == 0
    held = section_ends[0]
    half, model = held.shape[1], held.shape[2]
    size = 2 * half
    width = w_query.shape[2]
    inner = w_inner.shape[2]
    heads = width // HD
    flags = jnp.concatenate(
        [
            jnp.stack([section, tensor]).astype(jnp.int32),
            lax.dynamic_slice_in_dim(lengths, section, 1, 0)[0],
            (lax.axis_index("batch") % 2).astype(jnp.int32)[None],
        ]
    )

    x_peer_a = across(held[0], [((0, 0), (0, 1)), ((0, 1), (0, 0))])
    x_peer_b = across(held[1], [((0, 0), (1, 1)), ((0, 1), (1, 0))])
    x_far = across(held[1], [((0, 0), (1, 0)), ((0, 1), (1, 1))])

    attention_own = (w_query[0], w_key[0], w_value[0], w_out[0])
    ffn_own = (w_inner[0], w_outer[0])
    vec_own = pad_rows(
        jnp.concatenate(
            [
                jnp.concatenate([b_query, b_value], axis=1),
                b_out, norm1_gain, norm1_bias, b_inner.reshape(-1, model), b_outer,
                norm2_gain, norm2_bias,
            ],
            axis=0,
        ),
        V_ROWS,
    )
    vec_far = swap(vec_own, "section")
    attention_far = tuple(swap(w, "section") for w in attention_own)
    ffn_far = tuple(swap(w, "section") for w in ffn_own)
    attention_w = attention_own + attention_far
    ffn_w = ffn_own + ffn_far
    vec_one = jnp.where(first, vec_own, vec_far)
    vec_two = jnp.where(first, vec_far, vec_own)

    gy_peer_a = across(held[1], [((1, 0), (1, 1)), ((1, 1), (1, 0))])
    gy_peer_b = across(held[0], [((1, 0), (0, 1)), ((1, 1), (0, 0))])
    gy_far = across(held[0], [((1, 0), (0, 0)), ((1, 1), (0, 1))])

    def send(parts):
        return [swap(part, "tensor") for part in parts]

    def ffn_forward(layer, x, parts, vec, after=()):
        outs = ()
        sums = []
        for c, (part, got) in enumerate(zip(parts, send(parts))):
            outs = call(
                functools.partial(ffn_forward_kernel, layer),
                (flags, x, part, got, vec) + ffn_w,
                "scvvvaaaa",
                [
                    ((size, model), F32), ((size, 1), F32), ((size, model), BF),
                    ((size, inner), BF), ((size, inner), BF), ((half, model), BF),
                ],
                [
                    pltpu.VMEM((model, inner), BF), pltpu.VMEM((inner, model), BF),
                    pltpu.SemaphoreType.DMA((2,)),
                ],
                2 * size * model * inner, after, "cccccv", c, outs,
            )
            sums.append(outs[-1])
        return *outs[:-1], sums

    x_one, *heads_one, part, part2 = attention_call(
        flags, (held[0], x_far, x_peer_a, x_peer_b, vec_one), "vvvvv", attention_w,
        size, model, width, attention_first_kernel, [],
    )
    n1_one, i1_one, n1b_one, a_one, d_one, parts = ffn_forward(
        0, x_one, (part, part2), vec_one, (gy_peer_a, gy_peer_b, gy_far)
    )
    n2_one, i2_one, x_two, *heads_two, part, part2 = attention_call(
        flags, (n1_one, *parts, *send(parts), vec_one, vec_two), "vvvvvvv", attention_w,
        size, model, width, attention_next_kernel, [((size, model), F32), ((size, 1), F32)],
    )
    n1_two, i1_two, n1b_two, a_two, d_two, parts = ffn_forward(1, x_two, (part, part2), vec_two)

    ffn_outs = [
        ((size, model), F32), ((size, model), BF), ((size, inner), BF), ((half, model), BF),
        ((8, model), F32),
    ]
    ffn_scratch = [
        pltpu.VMEM((model, inner), BF), pltpu.VMEM((inner, model), BF),
        pltpu.SemaphoreType.DMA((2,)),
    ]

    stage_in, stage_middle, stage_out = line_stages()

    def spread(ours_mine, ours_next, theirs_mine, theirs_next):
        return (
            ours_mine + swap(theirs_mine, "section"),
            ours_next + swap(theirs_next, "section"),
        )

    def ffn_spread(a, gb, gh, n1b, small, after=()):
        shapes = [(model // 2 + PAD, model), (model // 2, model)]
        outs = call(
            ffn_product_kernel, (flags, a, gb, gh, n1b, small), "svvvvv",
            [(shape, BF) for shape in shapes for _ in range(4)],
            [pltpu.VMEM((4,) + shape, BF) for shape in shapes] + [pltpu.SemaphoreType.DMA((8,))],
            4 * size * model * inner, after, "a",
        )
        return spread(*outs[:4]), spread(*outs[4:])

    def attention_spread(gqkv, x, o, gb, small, after=()):
        shape = (model + PAD, width)
        outs = call(
            attention_product_kernel, (flags, x, gqkv, o, gb, small), "svvvvv",
            [(shape, BF)] * 4, [pltpu.VMEM((4,) + shape, BF), pltpu.SemaphoreType.DMA((4,))],
            8 * size * model * width, after, "a",
        )
        return spread(*outs)

    def collect(unit, token=None):
        return timed(unit[0] + pair_swap(unit[1]), token)

    def both_sides(mine):
        return mine, pair_swap(mine)

    def share(both, route):
        return tuple(both) + tuple(lax.ppermute(part, "section", [route]) for part in both)

    def attention_back(layer, g2, parts, n1, i1, vec, saved, after):
        q, k, v, e, r, o, ot_f = saved
        *outs, part, part2, small = call(
            functools.partial(attention_back_kernel, layer),
            (flags, g2, *parts, *send(parts), n1, i1, vec, q, k, v, e, r, ot_f) + attention_w,
            "s" + "v" * 14 + "a" * 8,
            [
                ((size, model), F32), ((size, model), BF), ((size, 3 * width), BF),
                ((half, model), BF), ((half, model), BF), ((8, model), F32),
            ],
            [pltpu.VMEM((model, width), BF)] * 3
            + [
                pltpu.VMEM((width, model), BF),
                pltpu.VMEM((HD, size), BF),
                pltpu.VMEM((size, HD), BF),
                pltpu.VMEM((width, size), BF),
                pltpu.VMEM((heads, size, HD), BF),
                pltpu.VMEM((heads, size, HD), BF),
                pltpu.VMEM((width, size), F32),
                pltpu.SemaphoreType.DMA((4,)),
            ],
            2 * size * width * model * 4 + 8 * heads * size * size * HD,
            after, weight=HEAVY,
        )
        return *outs, [part, part2], small

    outs = ()
    small_f2 = jnp.zeros((8, model), F32)
    sums = []
    for c, (part, got) in enumerate(zip(parts, send(parts))):
        outs = call(
            functools.partial(ffn_back_last_kernel, c),
            (flags, n1_two, part, got, vec_two, held[1], gy_far, gy_peer_a, gy_peer_b,
             d_two, small_f2) + ffn_w,
            "sc" + "v" * 7 + "cv" + "a" * 4,
            [((size, model), BF)] + ffn_outs,
            [pltpu.VMEM((half, model), BF)] + ffn_scratch,
            2 * size * model * inner, (), "ccccvv", c, outs,
        )
        sums.append(outs[-2])
        small_f2 = outs[-1]
    y_two, g2_two, g2b_two, gh_two = outs[:4]
    f2a, f2b = ffn_spread(a_two, g2b_two, gh_two, n1b_two, small_f2)
    g1_two, g1b_two, gqkv_two, parts, small_a2 = attention_back(
        1, g2_two, sums, n1_two, i1_two, vec_two, heads_two, (f2a[1], f2b[1])
    )
    f2a, f2b = collect(f2a, small_a2), collect(f2b, small_a2)
    a2 = attention_spread(gqkv_two, x_two, heads_two[5], g1b_two, small_a2)

    outs = ()
    small_f1 = jnp.zeros((8, model), F32)
    sums, tokens = [], []
    for c, (part, got) in enumerate(zip(parts, send(parts))):
        outs = call(
            ffn_back_next_kernel,
            (flags, g1_two, part, got, n2_one, i2_one, vec_one, d_one, small_f1) + ffn_w,
            "scvvccvcv" + "a" * 4,
            ffn_outs,
            ffn_scratch,
            2 * size * model * inner, ((), (a2[1],))[c], "cccvv", c, outs,
        )
        sums.append(outs[-2])
        small_f1 = outs[-1]
        tokens.append(small_f1)
    g2_one, g2b_one, gh_one = outs[:3]
    f2a, f2b = stage_in(f2a, tokens[0]), stage_in(f2b, tokens[1])
    a2 = collect(a2, tokens[1])
    f1a, f1b = ffn_spread(a_one, g2b_one, gh_one, n1b_one, small_f1)
    g1_one, g1b_one, gqkv_one, parts, small_a1 = attention_back(
        0, g2_one, sums, n1_one, i1_one, vec_one, heads_one, (f1a[1], f1b[1])
    )
    f2a, f2b = stage_middle(f2a, small_a1), stage_middle(f2b, small_a1)
    a2 = stage_in(a2, small_a1)
    f1a, f1b = collect(f1a, small_a1), collect(f1b, small_a1)
    a1 = attention_spread(gqkv_one, x_one, heads_one[5], g1b_one, small_a1)
    f2a, f2b = stage_out(f2a), stage_out(f2b)
    a2 = stage_middle(a2)
    f1a, f1b = stage_in(f1a), stage_in(f1b)
    a1 = collect(a1)
    a2 = stage_out(a2)
    f1a, f1b = stage_middle(f1a), stage_middle(f1b)
    a1 = stage_in(a1)
    f1a, f1b = stage_out(f1a), stage_out(f1b)
    a1 = stage_middle(a1)
    a1 = stage_out(a1)

    part_mine = jnp.where(tensor == 0, parts[0], parts[1])
    part_theirs = jnp.where(tensor == 0, parts[1], parts[0])
    total = part_mine.astype(F32) + swap(part_theirs, "tensor").astype(F32)
    gx = (lax.dynamic_slice_in_dim(g1_one, tensor * half, half, 0) + total).astype(BF)
    y_mine = lax.dynamic_slice_in_dim(y_two, tensor * half, half, 0)
    y_far = lax.ppermute(y_mine, "section", [(0, 1)])
    gx_far = lax.ppermute(gx, "section", [(1, 0)])
    section_results = jnp.stack(
        [jnp.where(first, gx, y_far), jnp.where(first, gx_far, y_mine)], axis=0
    )[None]

    def finish(kernel, units, outs):
        sums = ()
        for one, two in units:
            sums += share(one, (1, 0)) + share(two, (0, 1))
        held = [pltpu.VMEM((4,) + one[0].shape, BF) for one, _ in units]
        return call(
            kernel, (flags,) + sums, "s" + "a" * len(sums), [(shape, F32) for shape in outs],
            held + [pltpu.SemaphoreType.DMA((4 * len(held),))], size * model,
        )

    grad_outer, grad_inner, small_f = finish(
        ffn_finish_kernel, [(both_sides(f1a), both_sides(f2a)), (both_sides(f1b), both_sides(f2b))],
        [(inner, model), (model, inner), (PAD, model)]
    )
    grad_q, grad_k, grad_v, grad_out, small_a = finish(
        attention_finish_kernel, [(both_sides(a1), both_sides(a2))],
        [(model, width)] * 3 + [(width, model), (8, model)],
    )
    return (
        section_results,
        grad_q[None],
        small_a[3:4, :width],
        grad_k[None],
        grad_v[None],
        small_a[3:4, width:],
        grad_out[None],
        small_a[0:1],
        small_a[1:2],
        small_a[2:3],
        grad_inner[None],
        small_f[3 : 3 + inner // model].reshape(1, inner),
        grad_outer[None],
        small_f[0:1],
        small_f[1:2],
        small_f[2:3],
    )


def solution(mesh):
    in_specs = (
        P("section", "batch", "tensor", None),
        P("batch", None),
        P("section", None, "tensor"),
        P("section", "tensor"),
        P("section", None, "tensor"),
        P("section", None, "tensor"),
        P("section", "tensor"),
        P("section", "tensor", None),
        P("section", None),
        P("section", None),
        P("section", None),
        P("section", None, "tensor"),
        P("section", "tensor"),
        P("section", "tensor", None),
        P("section", None),
        P("section", None),
        P("section", None),
    )
    out_specs = (
        P("section", "batch", "tensor", None),
        P("section", None, "tensor"),
        P("section", "tensor"),
        P("section", None, "tensor"),
        P("section", None, "tensor"),
        P("section", "tensor"),
        P("section", "tensor", None),
        P("section", None),
        P("section", None),
        P("section", None),
        P("section", None, "tensor"),
        P("section", "tensor"),
        P("section", "tensor", None),
        P("section", None),
        P("section", None),
        P("section", None),
    )
    return jax.shard_map(shards, mesh=mesh, in_specs=in_specs, out_specs=out_specs, check_vma=False)
```

```python
import functools
import math

import jax
import jax.numpy as jnp
from jax import lax
from jax.experimental import pallas as pl
from jax.experimental.pallas import tpu as pltpu
from jax.sharding import PartitionSpec as P

HD = 64
epsilon = 1e-06
root_half = 0.7071067811865476
inverse_root = 0.3989422804014327
BF = jnp.bfloat16
F32 = jnp.float32
RB = 128
VMEM_BYTES = 56 * 1024 * 1024

V_BQV, V_BO, V_G1, V_B1, V_BI, V_BU, V_G2, V_B2 = 0, 1, 2, 3, 4, 6, 7, 8
V_ROWS = 16


def dot(a, b):
    return lax.dot_general(a, b, (((1,), (0,)), ((), ())), preferred_element_type=F32)


def dot_nt(a, b):
    return lax.dot_general(a, b, (((1,), (1,)), ((), ())), preferred_element_type=F32)


def dot_tn(a, b):
    return lax.dot_general(a, b, (((0,), (0,)), ((), ())), preferred_element_type=F32)


def start_fetch(use_own, own, other, held, sems):
    @pl.when(use_own)
    def _():
        for i in range(len(own)):
            pltpu.make_async_copy(own[i], held[i], sems.at[i]).start()

    @pl.when(jnp.logical_not(use_own))
    def _():
        for i in range(len(own)):
            pltpu.make_async_copy(other[i], held[i], sems.at[i]).start()


def wait_fetch(i, own, held, sems):
    pltpu.make_async_copy(own[i], held[i], sems.at[i]).wait()


def row_blocks(total, body):
    def step(i, carry):
        body(pl.ds(pl.multiple_of(i * RB, RB), RB))
        return carry

    lax.fori_loop(0, total // RB, step, 0)


def loop(count, body, unroll=1):
    def step(i, carry):
        for j in range(unroll):
            body(i * unroll + j)
        return carry

    lax.fori_loop(0, count // unroll, step, 0)


def part_of(i, step):
    return pl.ds(i * step if isinstance(i, int) else pl.multiple_of(i * step, step), step)


def norm_rows(residue):
    center = residue - jnp.mean(residue, axis=-1, keepdims=True)
    inverse = lax.rsqrt(jnp.mean(center * center, axis=-1, keepdims=True) + epsilon)
    return center * inverse, inverse


def norm_back_rows(upstream, normal, inverse, gain):
    scaled = upstream * gain
    centred = scaled - jnp.mean(scaled, axis=-1, keepdims=True)
    return (centred - normal * jnp.mean(scaled * normal, axis=-1, keepdims=True)) * inverse


def column_sum(rows):
    return jnp.sum(rows, axis=0, keepdims=True)


def segment_bias(flags, bias):
    size = bias.shape[0]
    ends = [flags[2]]
    for i in range(3, 5):
        ends.append(ends[-1] + flags[i])
    row = lax.broadcasted_iota(jnp.int32, (1, size), 1)
    row_seg = sum((row >= e).astype(jnp.int32) for e in ends)

    def body(rows):
        col = lax.broadcasted_iota(jnp.int32, (RB, 1), 0) + rows.start
        col_seg = sum((col >= e).astype(jnp.int32) for e in ends)
        bias[rows, :] = jnp.where(col_seg == row_seg, 0.0, -1e30).astype(F32)

    row_blocks(size, body)


def attention_forward(flags, x, vec, weights, wait, outs, scratch):
    wq, wk, wv, wo = weights
    q_out, k_out, v_out, e_out, r_out, o_out, ot_out, *p_outs = outs
    qt_s, kh_s, vt_s, bias = scratch
    size = x.shape[0]
    width = wq.shape[1]
    heads = width // HD
    segment_bias(flags, bias)
    wait(0)
    wait(1)
    wait(2)

    def project(i):
        rows = part_of(i, 256)
        xb = x[rows, :]
        q = (dot(xb, wq[...]) + vec[V_BQV : V_BQV + 1, :width]).astype(BF).astype(F32) * (
            1.0 / math.sqrt(HD)
        )
        q_out[rows, :] = q.astype(BF)
        qt_s[:, rows] = q.T.astype(BF)
        k = dot(xb, wk[...]).astype(BF)
        k_out[rows, :] = k
        for h in range(heads):
            kh_s[h, rows, :] = k[:, h * HD : (h + 1) * HD]
        v = dot(xb, wv[...]) + vec[V_BQV : V_BQV + 1, width : 2 * width]
        v_out[rows, :] = v.astype(BF)
        vt_s[:, rows] = v.T.astype(BF)

    loop(size // 256, project)

    def attend(h):
        hs = part_of(h, HD)
        for j in range(size // 256):
            cols = pl.ds(j * 256, 256)
            scores = dot(kh_s[h], qt_s[hs, cols]) + bias[:, cols]
            highest = jnp.max(scores, axis=0, keepdims=True)
            raised = jnp.exp(scores - highest)
            inverse = 1.0 / jnp.sum(raised, axis=0, keepdims=True)
            raised = raised.astype(BF)
            e_out[h, :, cols] = raised
            r_out[h, :, cols] = inverse
            ot_out[hs, cols] = dot(vt_s[hs, :], raised) * inverse

    loop(heads, attend, 2)
    wait(3)

    for i, p_out in enumerate(p_outs):
        rows = part_of(i, size // 2)
        context = ot_out[:, rows].T.astype(BF)
        o_out[rows, :] = context
        p_out[...] = dot(context, wo[...]).astype(BF)


def attention_first_kernel(
    flags, own, far, peer_a, peer_b, vec,
    wq, wk, wv, wo, wq2, wk2, wv2, wo2,
    x_out, q_out, k_out, v_out, e_out, r_out, o_out, ot_out, p_out, p_out2,
    wq_s, wk_s, wv_s, wo_s, qt_s, kh_s, vt_s, bias, sems,
):
    first = flags[0] == 0
    held = (wq_s, wk_s, wv_s, wo_s)
    source = (wq, wk, wv, wo)
    start_fetch(first, source, (wq2, wk2, wv2, wo2), held, sems)
    half = own.shape[0]
    mine = pl.multiple_of(flags[1] * half, half)
    theirs = pl.multiple_of((1 - flags[1]) * half, half)
    x_out[pl.ds(mine, half), :] = jnp.where(first, own[...], far[...])
    x_out[pl.ds(theirs, half), :] = jnp.where(first, peer_a[...], peer_b[...])
    attention_forward(
        flags, x_out, vec, held, lambda i: wait_fetch(i, source, held, sems),
        (q_out, k_out, v_out, e_out, r_out, o_out, ot_out, p_out, p_out2), (qt_s, kh_s, vt_s, bias),
    )


def attention_next_kernel(
    flags, normal_one, part_a, part_a2, part_b, part_b2, vec_prev, vec,
    wq, wk, wv, wo, wq2, wk2, wv2, wo2,
    n2_out, i2_out, x_out, q_out, k_out, v_out, e_out, r_out, o_out, ot_out, p_out, p_out2,
    wq_s, wk_s, wv_s, wo_s, qt_s, kh_s, vt_s, bias, sems,
):
    held = (wq_s, wk_s, wv_s, wo_s)
    source = (wq, wk, wv, wo)
    start_fetch(flags[0] == 1, source, (wq2, wk2, wv2, wo2), held, sems)

    half = part_a.shape[0]
    for c, (one, two) in enumerate(((part_a, part_b), (part_a2, part_b2))):

        def body(rows, c=c, one=one, two=two):
            place = pl.ds(rows.start + c * half, RB)
            normal, inverse, output = second_norm(normal_one[place, :], one, two, vec_prev, rows)
            n2_out[place, :] = normal
            i2_out[place, :] = inverse
            x_out[place, :] = output.astype(BF)

        row_blocks(half, body)
    attention_forward(
        flags, x_out, vec, held, lambda i: wait_fetch(i, source, held, sems),
        (q_out, k_out, v_out, e_out, r_out, o_out, ot_out, p_out, p_out2), (qt_s, kh_s, vt_s, bias),
    )


def second_norm(normal_one, part_a, part_b, vec, rows):
    normed = normal_one * vec[V_G1 : V_G1 + 1, :] + vec[V_B1 : V_B1 + 1, :]
    total = part_a[rows, :].astype(F32) + part_b[rows, :].astype(F32)
    normal, inverse = norm_rows(total + vec[V_BU : V_BU + 1, :] + normed)
    return normal, inverse, normal * vec[V_G2 : V_G2 + 1, :] + vec[V_B2 : V_B2 + 1, :]


def ffn_forward_kernel(
    layer, flags, x, part_a, part_b, vec, wi, wu, wi2, wu2,
    n1_out, i1_out, n1b_out, a_out, d_out, p_out,
    wi_s, wu_s, sems,
):
    held = (wi_s, wu_s)
    source = (wi, wu)
    start_fetch(flags[0] == layer, source, (wi2, wu2), held, sems)
    size = x.shape[0]
    width = wi_s.shape[1]
    model = wi_s.shape[0]

    def first(rows):
        total = part_a[rows, :].astype(F32) + part_b[rows, :].astype(F32)
        normal, inverse = norm_rows(total + vec[V_BO : V_BO + 1, :] + x[rows, :].astype(F32))
        n1_out[rows, :] = normal
        i1_out[rows, :] = inverse
        n1b_out[rows, :] = (normal * vec[V_G1 : V_G1 + 1, :] + vec[V_B1 : V_B1 + 1, :]).astype(BF)

    row_blocks(size, first)
    wait_fetch(0, source, held, sems)
    block = 256

    def inner(rows):
        rows_in = n1b_out[rows, :]
        for j in range(width // block):
            cols = slice(j * block, (j + 1) * block)
            at = j * block
            bias = vec[V_BI + at // model : V_BI + at // model + 1, at % model : at % model + block]
            hidden = dot(rows_in, wi_s[:, cols]) + bias
            spread = 0.5 + 0.5 * lax.erf(hidden * root_half)
            a_out[rows, cols] = (hidden * spread).astype(BF)
            d_out[rows, cols] = (
                spread + hidden * jnp.exp(-0.5 * hidden * hidden) * inverse_root
            ).astype(BF)

    row_blocks(size, inner)
    wait_fetch(1, source, held, sems)

    def outer(i):
        rows = part_of(i, 256)
        p_out[rows, :] = dot(a_out[rows, :], wu_s[...]).astype(BF)

    loop(size // 256, outer)


def ffn_backward(g2, d, w, outs, wait, small):
    wi_s, wu_s = w
    gh_out, p_out = outs
    size = g2.shape[0]
    model, width = wi_s.shape
    wait(1)
    block = 384

    def hidden(i):
        rows = part_of(i, 256)
        gb = g2[rows, :]
        for j in range(width // block):
            cols = slice(j * block, (j + 1) * block)
            gh = (dot_nt(gb, wu_s[cols, :]) * d[rows, cols].astype(F32)).astype(BF)
            gh_out[rows, cols] = gh
            at = j * block
            small[3 + at // model : 4 + at // model, at % model : at % model + block] += column_sum(
                gh.astype(F32)
            )

    loop(size // 256, hidden)
    wait(0)

    def inner(i):
        rows = part_of(i, 256)
        p_out[rows, :] = dot_nt(gh_out[rows, :], wi_s[...]).astype(BF)

    loop(size // 256, inner)


def ffn_back_last_kernel(
    chunk, flags, normal_one, part_a, part_b, vec, own, far, peer_a, peer_b, d, small_in,
    wi, wu, wi2, wu2,
    y_out, g_out, gb_out, gh_out, p_out, small,
    gy_s, wi_s, wu_s, sems,
):
    held = (wi_s, wu_s)
    source = (wi, wu)
    second = flags[0] == 1
    start_fetch(second, source, (wi2, wu2), held, sems)
    here = flags[1] == chunk
    gy_s[...] = jnp.where(
        here,
        jnp.where(second, own[...], far[...]),
        jnp.where(second, peer_a[...], peer_b[...]),
    )
    small[...] = small_in[...]

    def body(rows):
        normal, inverse, output = second_norm(normal_one[rows, :], part_a, part_b, vec, rows)
        y_out[rows, :] = output.astype(BF)
        ffn_back_rows(gy_s[rows, :].astype(F32), normal, inverse, vec, rows, g_out, gb_out, small)

    row_blocks(y_out.shape[0], body)
    ffn_backward(gb_out, d, held, (gh_out, p_out), lambda i: wait_fetch(i, source, held, sems), small)


def ffn_back_rows(upstream, normal, inverse, vec, rows, g_out, gb_out, small):
    grad = norm_back_rows(upstream, normal, inverse, vec[V_G2 : V_G2 + 1, :])
    g_out[rows, :] = grad
    gb_out[rows, :] = grad.astype(BF)
    small[0:1, :] += column_sum(grad)
    small[1:2, :] += column_sum(upstream * normal)
    small[2:3, :] += column_sum(upstream)


def ffn_back_next_kernel(
    flags, g1, part_a, part_b, normal_two, inverse_two, vec, d, small_in, wi, wu, wi2, wu2,
    g_out, gb_out, gh_out, p_out, small,
    wi_s, wu_s, sems,
):
    held = (wi_s, wu_s)
    source = (wi, wu)
    start_fetch(flags[0] == 0, source, (wi2, wu2), held, sems)
    small[...] = small_in[...]

    def body(rows):
        total = part_a[rows, :].astype(F32) + part_b[rows, :].astype(F32)
        upstream = (g1[rows, :] + total).astype(BF).astype(F32)
        ffn_back_rows(
            upstream, normal_two[rows, :], inverse_two[rows, :], vec, rows, g_out, gb_out, small
        )

    row_blocks(g1.shape[0], body)
    ffn_backward(gb_out, d, held, (gh_out, p_out), lambda i: wait_fetch(i, source, held, sems), small)


def attention_back_kernel(
    layer, flags, g2, part_a, part_a2, part_b, part_b2, normal_one, inverse_one, vec,
    q, k, v, e, r, ot_f,
    wq, wk, wv, wo, wq2, wk2, wv2, wo2,
    g_out, gb_out, gqkv_out, p_out, p_out2, small,
    wq_s, wk_s, wv_s, wo_s, got_s, go_s, kt_s, vh_s, qh_s, gqt_s, sems,
):
    held = (wq_s, wk_s, wv_s, wo_s)
    source = (wq, wk, wv, wo)
    start_fetch(flags[0] == layer, source, (wq2, wk2, wv2, wo2), held, sems)
    size, model = g2.shape
    width = q.shape[1]
    heads = width // HD
    small[...] = jnp.zeros_like(small)

    half = size // 2
    for c, (one, two) in enumerate(((part_a, part_b), (part_a2, part_b2))):

        def body(rows, c=c, one=one, two=two):
            place = pl.ds(rows.start + c * half, RB)
            upstream = g2[place, :] + (one[rows, :].astype(F32) + two[rows, :].astype(F32))
            normal = normal_one[place, :]
            grad = norm_back_rows(upstream, normal, inverse_one[place, :], vec[V_G1 : V_G1 + 1, :])
            g_out[place, :] = grad
            gb_out[place, :] = grad.astype(BF)
            small[0:1, :] += column_sum(grad)
            small[1:2, :] += column_sum(upstream * normal)
            small[2:3, :] += column_sum(upstream)

        row_blocks(half, body)

    def split(i):
        rows = part_of(i, 256)
        kt_s[:, rows] = k[rows, :].astype(F32).T.astype(BF)
        for h in range(heads):
            hs = slice(h * HD, (h + 1) * HD)
            vh_s[h, rows, :] = v[rows, hs]
            qh_s[h, rows, :] = q[rows, hs]

    loop(size // 256, split)
    wait_fetch(3, source, held, sems)

    def context(i):
        rows = part_of(i, 256)
        gqt_s[:, rows] = dot_nt(gb_out[rows, :], wo_s[...]).T

    loop(size // 256, context)

    def attend(h):
        hs = part_of(h, HD)
        scaled = (gqt_s[hs, :] * r[h]).astype(BF)
        got_s[...] = scaled
        scaled = scaled.astype(F32)
        delta = column_sum(scaled * ot_f[hs, :])
        go_s[...] = scaled.T.astype(BF)
        grad_v = jnp.zeros((size, HD), F32)
        grad_k = jnp.zeros((size, HD), F32)
        for j in range(size // 256):
            cols = pl.ds(j * 256, 256)
            raised = e[h, :, cols]
            grad_p = dot(vh_s[h], got_s[:, cols]) - delta[:, j * 256 : (j + 1) * 256]
            grad_s = (raised.astype(F32) * grad_p).astype(BF)
            grad_v = grad_v + dot(raised, go_s[cols, :])
            grad_k = grad_k + dot(grad_s, qh_s[h, cols, :])
            gqt_s[hs, cols] = dot(kt_s[hs, :], grad_s) * (1.0 / math.sqrt(HD))
        vh_s[h] = grad_v.astype(BF)
        qh_s[h] = grad_k.astype(BF)

    loop(heads, attend, 2)
    for i in range(3):
        wait_fetch(i, source, held, sems)

    for i, p in enumerate((p_out, p_out2)):
        rows = pl.ds(i * half, half)
        gq = gqt_s[:, rows].T.astype(BF)
        gk = jnp.concatenate([qh_s[h, rows, :] for h in range(heads)], axis=1)
        gv = jnp.concatenate([vh_s[h, rows, :] for h in range(heads)], axis=1)
        gqkv_out[rows, :width] = gq
        gqkv_out[rows, width : 2 * width] = gk
        gqkv_out[rows, 2 * width :] = gv
        small[3:4, :width] += column_sum(gq.astype(F32))
        small[3:4, width:] += column_sum(gv.astype(F32))
        p[...] = (
            dot_nt(gq, wq_s[...]) + dot_nt(gk, wk_s[...]) + dot_nt(gv, wv_s[...])
        ).astype(BF)


HEAVY, LIGHT = 20, 0
PAD = 16
UNITS = (2, 2)
ORDER = (
    "KC2a", "KC2b", "KWF2", "KD2", "KWA2", "a2gn", "f2gn", "KC1a", "KC1b", "KWF1", "f2aa1", "KD1",
    "f2ba1", "KWA1", "f2aa2", "f1gn", "a2a1", "f2ba2", "a1gn", "f2aa3", "f1aa1", "a2a2", "f2ba3",
    "f1ba1", "f2aa4", "f1aa2", "a2a3", "a1a1", "f2ba4", "f1ba2", "f1aa3", "a2a4", "a1a2", "f1ba3",
    "f1aa4", "a1a3", "f1ba4", "a1a4", "finF", "finA",
)


def send_both(held, outs, sems):
    copies = [pltpu.make_async_copy(held.at[i], outs[i], sems.at[i]) for i in range(2)]
    for copy in copies:
        copy.start()
    for copy in copies:
        copy.wait()


def ffn_rows(units, block):
    if units == 1:
        return (2 * block + PAD,), lambda i, half: half * (2 * block + PAD) + i * block
    return (block + PAD, block), lambda i, half: i * 2 * (block + PAD) + half * (block + PAD * (1 - i))


def ffn_product_kernel(units, flags, a, gb, gh, n1b, small, ours, theirs, held, sems):
    model = gb.shape[1]
    block = model // 2
    extra = jnp.concatenate([small[...], jnp.zeros((PAD - 8, model), F32)], axis=0).astype(BF)
    sizes, start = ffn_rows(units, block)
    for i in range(2):

        def products(j, i=i):
            here = pl.ds(pl.multiple_of(start(i, flags[6] ^ j), 16), block)
            held[flags[0], here, :] = dot_tn(a[:, part_of(2 * j + i, block)], gb[...]).astype(BF)
            held[1 - flags[0], here, :] = dot_tn(
                n1b[:, i * block : (i + 1) * block], gh[:, part_of(j, model)]
            ).astype(BF)

        loop(2, products)
    for i in range(2):
        for half in range(2):
            at = (half + 1) * sizes[0]
            held[i, at - PAD : at, :] = extra
    send_both(held, (ours, theirs), sems)


def attention_product_kernel(flags, x, gqkv, o, gb, small, ours, theirs, held, sems):
    model = gb.shape[1]
    width = o.shape[1]
    rows = model + PAD

    def products(i):
        here = pl.ds(pl.multiple_of((flags[6] ^ (i % 2)) * rows, 16), model)
        held[flags[0] ^ (i // 2), here, :] = dot_tn(x[...], gqkv[:, part_of(i, width)]).astype(BF)

    loop(3, products)
    base = pl.multiple_of((flags[6] ^ 1) * rows, 16)
    for i in range(2):
        held[1 - flags[0], pl.ds(base + i * width, width), :] = dot_tn(
            o[...], gb[:, i * width : (i + 1) * width]
        ).astype(BF)
    extra = jnp.concatenate([small[:, :width], small[:, width:]], axis=0).astype(BF)
    for i in range(2):
        for half in range(2):
            held[i, half * rows + model : (half + 1) * rows, :] = extra
    send_both(held, (ours, theirs), sems)


def fetch_sums(flags, layers, held, sems):
    def copies(layer):
        pieces = layers[layer]
        for u, (sums, row, rows, at) in enumerate(pieces):
            for far in range(2):
                for beside in range(2):
                    slot = 2 * (flags[0] ^ far) + (flags[6] ^ beside)
                    i = 2 * far + beside
                    yield pltpu.make_async_copy(
                        sums[i].at[pl.ds(row, rows), :],
                        held.at[slot, pl.ds(at, rows), :],
                        sems.at[4 * u + i],
                    )

    for layer in range(2):

        @pl.when(flags[0] == layer)
        def _(layer=layer):
            for copy in copies(layer):
                copy.start()
            for copy in copies(layer):
                copy.wait()


def ffn_finish_kernel(units, flags, *refs):
    counts = [4 * n for n in units]
    sums = refs[: sum(counts)]
    outer, inside, bias_outer, gain, bias, bias_inner, held, sems = refs[sum(counts) :]
    model = outer.shape[1]
    block = model // 2
    layers = []
    for n, mine in zip(units, (sums[: counts[0]], sums[counts[0] :])):
        if n == 1:
            layers.append([(mine, 0, 2 * block + PAD, 0)])
        else:
            layers.append(
                [
                    (mine[:4], 0, block, 0),
                    (mine[4:], 0, block, block),
                    (mine[:4], block, PAD, 2 * block),
                ]
            )
    fetch_sums(flags, layers, held, sems)
    for j in range(2):
        outer[j * model : (j + 1) * model, :] = held[j, :model, :].astype(F32)
        inside[:, j * model : (j + 1) * model] = held[2 + j, :model, :].astype(F32)
    small = held[0, model : model + PAD, :].astype(F32)
    for i, out in enumerate((bias_outer, gain, bias)):
        out[...] = small[i : i + 1, :]
    for i in range(bias_inner.shape[1] // model):
        bias_inner[:, i * model : (i + 1) * model] = small[3 + i : 4 + i, :]


def attention_finish_kernel(flags, *refs):
    sums, (q, k, v, out, bias_out, gain, bias, bias_q, bias_v) = refs[:8], refs[8:17]
    held, sems = refs[17], refs[18]
    model, width = q.shape
    rows = model + PAD
    fetch_sums(flags, [[(sums[:4], 0, rows, 0)], [(sums[4:], 0, rows, 0)]], held, sems)
    q[...] = held[0, :model, :].astype(F32)
    k[...] = held[1, :model, :].astype(F32)
    v[...] = held[2, :model, :].astype(F32)
    for i in range(2):
        out[:, i * width : (i + 1) * width] = held[3, i * width : (i + 1) * width, :].astype(F32)
    left = held[0, model : model + PAD, :].astype(F32)
    for i, row in enumerate((bias_out, gain, bias)):
        row[:, :width] = left[i : i + 1, :]
        row[:, width:] = left[8 + i : 9 + i, :]
    bias_q[...] = left[3:4, :]
    bias_v[...] = left[11:12, :]


def ordered(array, after):
    return lax.optimization_barrier((array,) + tuple(after))[0] if after else array


def call(
    kernel, operands, spaces, outs, scratch, flops, after=(), out_space="v", chunk=0, before=(),
    weight=LIGHT,
):
    count = len(operands)
    out_space = out_space * len(outs) if len(out_space) == 1 else out_space
    passed = [i for i, c in enumerate(out_space) if c == "c" and before]
    extra = [before[i] for i in passed]
    operands = (ordered(operands[0], after),) + tuple(operands[1:])

    def body(*refs):
        kernel(*refs[:count], *refs[count + len(extra) :])

    def spec(letter, shape):
        if letter == "c":
            return pl.BlockSpec((shape[0] // 2, shape[1]), lambda i: (chunk, 0))
        return pl.BlockSpec(memory_space={"s": pltpu.SMEM, "v": pltpu.VMEM, "a": pl.ANY}[letter])

    return pl.pallas_call(
        body,
        grid=(1,) if "c" in spaces else (),
        out_shape=[jax.ShapeDtypeStruct(s, t) for s, t in outs],
        in_specs=[spec(c, x.shape) for c, x in zip(spaces, operands)]
        + [pl.BlockSpec(memory_space=pl.ANY)] * len(extra),
        out_specs=[spec(c, s) for c, (s, _) in zip(out_space, outs)],
        scratch_shapes=scratch,
        input_output_aliases={count + i: o for i, o in enumerate(passed)},
        compiler_params=pltpu.CompilerParams(vmem_limit_bytes=VMEM_BYTES),
        cost_estimate=pl.CostEstimate(
            flops=flops * weight, bytes_accessed=(8 << 20) * weight, transcendentals=0
        ),
    )(*operands, *extra)


def attention_call(flags, lead, lead_spaces, weights, size, model, width, kernel, extra_outs):
    heads = width // HD
    outs = extra_outs + [
        ((size, model), BF),
        ((size, width), BF),
        ((size, width), BF),
        ((size, width), BF),
        ((heads, size, size), BF),
        ((heads, 1, size), F32),
        ((size, width), BF),
        ((width, size), F32),
        ((size // 2, model), BF),
        ((size // 2, model), BF),
    ]
    scratch = [pltpu.VMEM((model, width), BF)] * 3 + [
        pltpu.VMEM((width, model), BF),
        pltpu.VMEM((width, size), BF),
        pltpu.VMEM((heads, size, HD), BF),
        pltpu.VMEM((width, size), BF),
        pltpu.VMEM((size, size), F32),
        pltpu.SemaphoreType.DMA((4,)),
    ]
    return call(
        kernel, (flags,) + lead + weights, "s" + lead_spaces + "a" * 8, outs, scratch,
        2 * size * width * model * 4 + 4 * heads * size * size * HD, weight=HEAVY,
    )


def swap(block, axis):
    return lax.ppermute(block, axis, [(0, 1), (1, 0)])


def across(block, routes):
    return lax.ppermute(
        block, ("section", "tensor"), [(a[0] * 2 + a[1], b[0] * 2 + b[1]) for a, b in routes]
    )


def batch_pairs():
    return [(i, i ^ 1) for i in range(lax.axis_size("batch"))]


def pair_swap(block):
    return lax.ppermute(block, "batch", batch_pairs())


def line_end():
    line = lax.axis_index("batch") // 2
    return (line == 0) | (line == 3)


STAGES = (
    ("in", ((0, 2), (1, 3), (6, 4), (7, 5))),
    ("middle", ((2, 4), (3, 5), (4, 2), (5, 3))),
    ("out", ((2, 0), (3, 1), (4, 6), (5, 7))),
)


def rest_of_line(mine):
    count = lax.axis_size("batch")
    if count & (count - 1):
        lines = [list(range(i, count, 2)) for i in range(2)]
        return lax.psum(mine, "batch", axis_index_groups=lines)
    step = 2
    while step < count:
        mine = mine + lax.ppermute(mine, "batch", [(i, i ^ step) for i in range(count)])
        step *= 2
    return mine


def pad_rows(rows, count):
    return jnp.concatenate([rows, jnp.zeros((count - rows.shape[0], rows.shape[1]), rows.dtype)], 0)


def shards(
    section_ends, lengths, w_query, b_query, w_key, w_value, b_value, w_out, b_out,
    norm1_gain, norm1_bias, w_inner, b_inner, w_outer, b_outer, norm2_gain, norm2_bias,
):
    section = lax.axis_index("section")
    tensor = lax.axis_index("tensor")
    first = section == 0
    held = section_ends[0]
    half, model = held.shape[1], held.shape[2]
    size = 2 * half
    width = w_query.shape[2]
    inner = w_inner.shape[2]
    heads = width // HD
    flags = jnp.concatenate(
        [
            jnp.stack([section, tensor]).astype(jnp.int32),
            lax.dynamic_slice_in_dim(lengths, section, 1, 0)[0],
            (lax.axis_index("batch") % 2).astype(jnp.int32)[None],
        ]
    )

    x_peer_a = across(held[0], [((0, 0), (0, 1)), ((0, 1), (0, 0))])
    x_peer_b = across(held[1], [((0, 0), (1, 1)), ((0, 1), (1, 0))])
    x_far = across(held[1], [((0, 0), (1, 0)), ((0, 1), (1, 1))])

    attention_own = (w_query[0], w_key[0], w_value[0], w_out[0])
    ffn_own = (w_inner[0], w_outer[0])
    vec_own = pad_rows(
        jnp.concatenate(
            [
                jnp.concatenate([b_query, b_value], axis=1),
                b_out, norm1_gain, norm1_bias, b_inner.reshape(-1, model), b_outer,
                norm2_gain, norm2_bias,
            ],
            axis=0,
        ),
        V_ROWS,
    )
    vec_far = swap(vec_own, "section")
    attention_far = tuple(swap(w, "section") for w in attention_own)
    ffn_far = tuple(swap(w, "section") for w in ffn_own)
    attention_w = attention_own + attention_far
    ffn_w = ffn_own + ffn_far
    vec_one = jnp.where(first, vec_own, vec_far)
    vec_two = jnp.where(first, vec_far, vec_own)

    gy_peer_a = across(held[1], [((1, 0), (1, 1)), ((1, 1), (1, 0))])
    gy_peer_b = across(held[0], [((1, 0), (0, 1)), ((1, 1), (0, 0))])
    gy_far = across(held[0], [((1, 0), (0, 0)), ((1, 1), (0, 1))])

    def send(parts):
        return [swap(part, "tensor") for part in parts]

    def ffn_forward(layer, x, parts, vec, after=()):
        outs = ()
        sums = []
        for c, (part, got) in enumerate(zip(parts, send(parts))):
            outs = call(
                functools.partial(ffn_forward_kernel, layer),
                (flags, x, part, got, vec) + ffn_w,
                "scvvvaaaa",
                [
                    ((size, model), F32), ((size, 1), F32), ((size, model), BF),
                    ((size, inner), BF), ((size, inner), BF), ((half, model), BF),
                ],
                [
                    pltpu.VMEM((model, inner), BF), pltpu.VMEM((inner, model), BF),
                    pltpu.SemaphoreType.DMA((2,)),
                ],
                2 * size * model * inner, after, "cccccv", c, outs,
            )
            sums.append(outs[-1])
        return *outs[:-1], sums

    x_one, *heads_one, part, part2 = attention_call(
        flags, (held[0], x_far, x_peer_a, x_peer_b, vec_one), "vvvvv", attention_w,
        size, model, width, attention_first_kernel, [],
    )
    n1_one, i1_one, n1b_one, a_one, d_one, parts = ffn_forward(
        0, x_one, (part, part2), vec_one, (gy_peer_a, gy_peer_b, gy_far)
    )
    n2_one, i2_one, x_two, *heads_two, part, part2 = attention_call(
        flags, (n1_one, *parts, *send(parts), vec_one, vec_two), "vvvvvvv", attention_w,
        size, model, width, attention_next_kernel, [((size, model), F32), ((size, 1), F32)],
    )
    n1_two, i1_two, n1b_two, a_two, d_two, parts_two = ffn_forward(1, x_two, (part, part2), vec_two)

    ffn_outs = [
        ((size, model), F32), ((size, model), BF), ((size, inner), BF), ((half, model), BF),
        ((8, model), F32),
    ]
    ffn_scratch = [
        pltpu.VMEM((model, inner), BF), pltpu.VMEM((inner, model), BF),
        pltpu.SemaphoreType.DMA((2,)),
    ]

    def attention_back(layer, g2, parts, got, n1, i1, vec, saved, after):
        q, k, v, e, r, o, ot_f = saved
        *outs, part, part2, small = call(
            functools.partial(attention_back_kernel, layer),
            (flags, g2, *parts, *got, n1, i1, vec, q, k, v, e, r, ot_f) + attention_w,
            "s" + "v" * 14 + "a" * 8,
            [
                ((size, model), F32), ((size, model), BF), ((size, 3 * width), BF),
                ((half, model), BF), ((half, model), BF), ((8, model), F32),
            ],
            [pltpu.VMEM((model, width), BF)] * 3
            + [
                pltpu.VMEM((width, model), BF),
                pltpu.VMEM((HD, size), BF),
                pltpu.VMEM((size, HD), BF),
                pltpu.VMEM((width, size), BF),
                pltpu.VMEM((heads, size, HD), BF),
                pltpu.VMEM((heads, size, HD), BF),
                pltpu.VMEM((width, size), F32),
                pltpu.SemaphoreType.DMA((4,)),
            ],
            2 * size * width * model * 4 + 8 * heads * size * size * HD,
            after, weight=HEAVY,
        )
        return *outs, [part, part2], small

    state = {}
    last = ()
    chunked = [()]

    def add(groups, arrays, shapes):
        sums = []
        for group, (rows, _) in zip(groups, shapes):
            terms = [arrays[i][row : row + rows] for i, row in group]
            sums.append(sum(terms[1:], ordered(terms[0], last)))
        return sums

    def back_last(c):
        part = parts_two[c]
        outs = call(
            functools.partial(ffn_back_last_kernel, c),
            (flags, n1_two, part, got_two[c], vec_two, held[1], gy_far, gy_peer_a, gy_peer_b,
             d_two, small_zero if c == 0 else state["small_f2"]) + ffn_w,
            "sc" + "v" * 7 + "cv" + "a" * 4,
            [((size, model), BF)] + ffn_outs,
            [pltpu.VMEM((half, model), BF)] + ffn_scratch,
            2 * size * model * inner, last, "ccccvv", c, chunked[0],
        )
        chunked[0] = outs if c == 0 else ()
        state["small_f2"] = outs[-1]
        state["y_two"], state["g2_two"], state["g2b_two"], state["gh_two"] = outs[:4]
        state.setdefault("sums_two", []).append(outs[-2])
        state.setdefault("sums_two_got", []).append(swap(outs[-2], "tensor"))
        return outs[-1]

    def back_next(c):
        outs = call(
            ffn_back_next_kernel,
            (flags, state["g1_two"], state["p4_two"][c], state["p4_two_got"][c], n2_one, i2_one,
             vec_one, d_one, small_zero if c == 0 else state["small_f1"]) + ffn_w,
            "scvvccvcv" + "a" * 4,
            ffn_outs,
            ffn_scratch,
            2 * size * model * inner, last, "cccvv", c, chunked[0],
        )
        chunked[0] = outs if c == 0 else ()
        state["small_f1"] = outs[-1]
        state["g2_one"], state["g2b_one"], state["gh_one"] = outs[:3]
        state.setdefault("sums_one", []).append(outs[-2])
        state.setdefault("sums_one_got", []).append(swap(outs[-2], "tensor"))
        return outs[-1]

    def back_attention(name, layer, *rest):
        grad, rows, gqkv, parts, small = attention_back(
            layer, state["g2_" + name], state["sums_" + name], state["sums_" + name + "_got"],
            *rest, last,
        )
        state["g1_" + name], state["g1b_" + name], state["gqkv_" + name] = grad, rows, gqkv
        state["p4_" + name], state["small_a_" + name] = parts, small
        if name == "two":
            state["p4_two_got"] = send(parts)
        return small

    def put(base, ours, theirs):
        state[base] = ours
        state[base + "_got"] = swap(theirs, "section")

    def ffn_products(base, units, a, gb, gh, n1b, small):
        rows = 2 * (model + PAD)
        ours, theirs = call(
            functools.partial(ffn_product_kernel, units), (flags, a, gb, gh, n1b, small), "svvvvv",
            [((rows, model), BF)] * 2,
            [pltpu.VMEM((2, rows, model), BF), pltpu.SemaphoreType.DMA((2,))],
            4 * size * model * inner, last, "a",
        )
        put(base, ours, theirs)
        return ours

    def attention_products(base, gqkv, x, o, gb, small):
        rows = 2 * (model + PAD)
        ours, theirs = call(
            attention_product_kernel, (flags, x, gqkv, o, gb, small), "svvvvv",
            [((rows, width), BF)] * 2,
            [pltpu.VMEM((2, rows, width), BF), pltpu.SemaphoreType.DMA((2,))],
            8 * size * model * width, last, "a",
        )
        put(base, ours, theirs)
        return ours

    units = {}
    for base, count in (("f1", UNITS[0]), ("f2", UNITS[1])):
        row = 0
        for name, rows in zip("ab", ffn_rows(count, model // 2)[0]):
            units[base + name] = (base, row, rows, model)
            row += 2 * rows
    for base in ("a1", "a2"):
        units[base] = (base, 0, model + PAD, width)

    def give(base):
        names = [n for n in units if units[n][0] == base]
        outs = add(
            [[(0, units[n][1] + units[n][2]), (1, units[n][1] + units[n][2])] for n in names],
            (state[base], state[base + "_got"]),
            [units[n][2:] for n in names],
        )
        for n, out in zip(names, outs):
            state[n + "x"] = pair_swap(out)
        return outs[0]

    def step(name, stage):
        base, row, rows, columns = units[name]
        shape = (rows, columns)
        if stage == 0:
            (mine,) = add(
                [[(0, row), (1, row), (2, 0)]],
                (state[base], state[base + "_got"], state[name + "x"]), [shape],
            )
        elif lax.axis_size("batch") != 8:
            mine = rest_of_line(state[name]) if stage == 1 else state[name]
        elif stage < 3:
            (mine,) = add([[(0, 0), (1, 0)]], (state[name], state[name + "s"]), [shape])
        else:
            mine = jnp.where(at_end, state[name + "s"], ordered(state[name], last))
        state[name] = mine
        if stage < 3:
            state[name + "s"] = lax.ppermute(mine, "batch", STAGES[stage][1]) if lax.axis_size("batch") == 8 else None
        else:
            both = (mine, pair_swap(mine))
            route = (1, 0) if base[1] == "1" else (0, 1)
            state[name] = both + tuple(lax.ppermute(b, "section", [route]) for b in both)
        return mine

    def finish_ffn():
        sums = sum((state[n] for n in sorted(units) if n[0] == "f"), ())
        outs = call(
            functools.partial(ffn_finish_kernel, UNITS), (flags,) + sums, "s" + "a" * len(sums),
            [((inner, model), F32), ((model, inner), F32)] + [((1, model), F32)] * 3
            + [((1, inner), F32)],
            [pltpu.VMEM((4, model + PAD, model), BF), pltpu.SemaphoreType.DMA((12,))],
            size * model, last,
        )
        state["ffn"] = outs
        return outs[-1]

    def finish_attention():
        outs = call(
            attention_finish_kernel, (flags,) + state["a1"] + state["a2"], "s" + "a" * 8,
            [((model, width), F32)] * 3 + [((width, model), F32)] + [((1, model), F32)] * 3
            + [((1, width), F32)] * 2,
            [pltpu.VMEM((4, model + PAD, width), BF), pltpu.SemaphoreType.DMA((4,))],
            size * model, last,
        )
        state["attention"] = outs
        return outs[-1]

    at_end = line_end()
    small_zero = jnp.zeros((8, model), F32)
    got_two = send(parts_two)
    tasks = {
        "KC2a": lambda: back_last(0),
        "KC2b": lambda: back_last(1),
        "KWF2": lambda: ffn_products(
            "f2", UNITS[1], a_two, state["g2b_two"], state["gh_two"], n1b_two, state["small_f2"]
        ),
        "KD2": lambda: back_attention("two", 1, n1_two, i1_two, vec_two, heads_two),
        "KWA2": lambda: attention_products(
            "a2", state["gqkv_two"], x_two, heads_two[5], state["g1b_two"], state["small_a_two"]
        ),
        "KC1a": lambda: back_next(0),
        "KC1b": lambda: back_next(1),
        "KWF1": lambda: ffn_products(
            "f1", UNITS[0], a_one, state["g2b_one"], state["gh_one"], n1b_one, state["small_f1"]
        ),
        "KD1": lambda: back_attention("one", 0, n1_one, i1_one, vec_one, heads_one),
        "KWA1": lambda: attention_products(
            "a1", state["gqkv_one"], x_one, heads_one[5], state["g1b_one"], state["small_a_one"]
        ),
        "finF": finish_ffn,
        "finA": finish_attention,
    }
    for base in ("f1", "f2", "a1", "a2"):
        tasks[base + "gn"] = functools.partial(give, base)
    for name in units:
        for stage in range(4):
            tasks[name + "a" + str(stage + 1)] = functools.partial(step, name, stage)
    for name in ORDER:
        last = (tasks[name](),)

    part_one, part_one2 = state["p4_one"]
    part_mine = jnp.where(tensor == 0, part_one, part_one2)
    part_theirs = jnp.where(tensor == 0, part_one2, part_one)
    total = part_mine.astype(F32) + swap(part_theirs, "tensor").astype(F32)
    gx = (lax.dynamic_slice_in_dim(state["g1_one"], tensor * half, half, 0) + total).astype(BF)
    y_mine = lax.dynamic_slice_in_dim(state["y_two"], tensor * half, half, 0)
    y_far = lax.ppermute(y_mine, "section", [(0, 1)])
    gx_far = lax.ppermute(gx, "section", [(1, 0)])
    section_results = jnp.stack(
        [jnp.where(first, gx, y_far), jnp.where(first, gx_far, y_mine)], axis=0
    )[None]
    grad_outer, grad_inner, bias_outer, gain_two, bias_two, bias_inner = state["ffn"]
    grad_q, grad_k, grad_v, grad_out, bias_out, gain_one, bias_one, bias_q, bias_v = state["attention"]
    return (
        section_results,
        grad_q[None],
        bias_q,
        grad_k[None],
        grad_v[None],
        bias_v,
        grad_out[None],
        bias_out,
        gain_one,
        bias_one,
        grad_inner[None],
        bias_inner,
        grad_outer[None],
        bias_outer,
        gain_two,
        bias_two,
    )


def solution(mesh):
    in_specs = (
        P("section", "batch", "tensor", None),
        P("batch", None),
        P("section", None, "tensor"),
        P("section", "tensor"),
        P("section", None, "tensor"),
        P("section", None, "tensor"),
        P("section", "tensor"),
        P("section", "tensor", None),
        P("section", None),
        P("section", None),
        P("section", None),
        P("section", None, "tensor"),
        P("section", "tensor"),
        P("section", "tensor", None),
        P("section", None),
        P("section", None),
        P("section", None),
    )
    out_specs = (
        P("section", "batch", "tensor", None),
        P("section", None, "tensor"),
        P("section", "tensor"),
        P("section", None, "tensor"),
        P("section", None, "tensor"),
        P("section", "tensor"),
        P("section", "tensor", None),
        P("section", None),
        P("section", None),
        P("section", None),
        P("section", None, "tensor"),
        P("section", "tensor"),
        P("section", "tensor", None),
        P("section", None),
        P("section", None),
        P("section", None),
    )
    return jax.shard_map(shards, mesh=mesh, in_specs=in_specs, out_specs=out_specs, check_vma=False)
```

```python
import functools
import math

import jax
import jax.numpy as jnp
from jax import lax
from jax.experimental import pallas as pl
from jax.experimental.pallas import tpu as pltpu
from jax.sharding import PartitionSpec as P

HD = 64
epsilon = 1e-06
root_half = 0.7071067811865476
inverse_root = 0.3989422804014327
BF = jnp.bfloat16
F32 = jnp.float32
RB = 128
VMEM_BYTES = 56 * 1024 * 1024

V_BQV, V_BO, V_G1, V_B1, V_BI, V_BU, V_G2, V_B2 = 0, 1, 2, 3, 4, 6, 7, 8
V_ROWS = 16


def dot(a, b):
    return lax.dot_general(a, b, (((1,), (0,)), ((), ())), preferred_element_type=F32)


def dot_nt(a, b):
    return lax.dot_general(a, b, (((1,), (1,)), ((), ())), preferred_element_type=F32)


def dot_tn(a, b):
    return lax.dot_general(a, b, (((0,), (0,)), ((), ())), preferred_element_type=F32)


def start_fetch(use_own, own, other, held, sems):
    @pl.when(use_own)
    def _():
        for i in range(len(own)):
            pltpu.make_async_copy(own[i], held[i], sems.at[i]).start()

    @pl.when(jnp.logical_not(use_own))
    def _():
        for i in range(len(own)):
            pltpu.make_async_copy(other[i], held[i], sems.at[i]).start()


def wait_fetch(i, own, held, sems):
    pltpu.make_async_copy(own[i], held[i], sems.at[i]).wait()


def row_blocks(total, body):
    def step(i, carry):
        body(pl.ds(pl.multiple_of(i * RB, RB), RB))
        return carry

    lax.fori_loop(0, total // RB, step, 0)


def loop(count, body, unroll=1):
    def step(i, carry):
        for j in range(unroll):
            body(i * unroll + j)
        return carry

    lax.fori_loop(0, count // unroll, step, 0)


def part_of(i, step):
    return pl.ds(i * step if isinstance(i, int) else pl.multiple_of(i * step, step), step)


def norm_rows(residue):
    center = residue - jnp.mean(residue, axis=-1, keepdims=True)
    inverse = lax.rsqrt(jnp.mean(center * center, axis=-1, keepdims=True) + epsilon)
    return center * inverse, inverse


def norm_back_rows(upstream, normal, inverse, gain):
    scaled = upstream * gain
    centred = scaled - jnp.mean(scaled, axis=-1, keepdims=True)
    return (centred - normal * jnp.mean(scaled * normal, axis=-1, keepdims=True)) * inverse


def column_sum(rows):
    return jnp.sum(rows, axis=0, keepdims=True)


def segment_bias(flags, bias):
    size = bias.shape[0]
    ends = [flags[2]]
    for i in range(3, 5):
        ends.append(ends[-1] + flags[i])
    row = lax.broadcasted_iota(jnp.int32, (1, size), 1)
    row_seg = sum((row >= e).astype(jnp.int32) for e in ends)

    def body(rows):
        col = lax.broadcasted_iota(jnp.int32, (RB, 1), 0) + rows.start
        col_seg = sum((col >= e).astype(jnp.int32) for e in ends)
        bias[rows, :] = jnp.where(col_seg == row_seg, 0.0, -1e30).astype(F32)

    row_blocks(size, body)


def attention_forward(flags, x, vec, weights, wait, outs, scratch):
    wq, wk, wv, wo = weights
    q_out, k_out, v_out, e_out, r_out, o_out, ot_out, *p_outs = outs
    qt_s, kh_s, vt_s, bias = scratch
    size = x.shape[0]
    width = wq.shape[1]
    heads = width // HD
    segment_bias(flags, bias)
    wait(0)
    wait(1)
    wait(2)

    def project(i):
        rows = part_of(i, 256)
        xb = x[rows, :]
        q = (dot(xb, wq[...]) + vec[V_BQV : V_BQV + 1, :width]).astype(BF).astype(F32) * (
            1.0 / math.sqrt(HD)
        )
        q_out[rows, :] = q.astype(BF)
        qt_s[:, rows] = q.T.astype(BF)
        k = dot(xb, wk[...]).astype(BF)
        k_out[rows, :] = k
        for h in range(heads):
            kh_s[h, rows, :] = k[:, h * HD : (h + 1) * HD]
        v = dot(xb, wv[...]) + vec[V_BQV : V_BQV + 1, width : 2 * width]
        v_out[rows, :] = v.astype(BF)
        vt_s[:, rows] = v.T.astype(BF)

    loop(size // 256, project)

    def attend(h):
        hs = part_of(h, HD)
        for j in range(size // 256):
            cols = pl.ds(j * 256, 256)
            scores = dot(kh_s[h], qt_s[hs, cols]) + bias[:, cols]
            highest = jnp.max(scores, axis=0, keepdims=True)
            raised = jnp.exp(scores - highest)
            inverse = 1.0 / jnp.sum(raised, axis=0, keepdims=True)
            raised = raised.astype(BF)
            e_out[h, :, cols] = raised
            r_out[h, :, cols] = inverse
            ot_out[hs, cols] = dot(vt_s[hs, :], raised) * inverse

    loop(heads, attend, 2)
    wait(3)

    for i, p_out in enumerate(p_outs):
        rows = part_of(i, size // 2)
        context = ot_out[:, rows].T.astype(BF)
        o_out[rows, :] = context
        p_out[...] = dot(context, wo[...]).astype(BF)


def attention_first_kernel(
    flags, own, far, peer_a, peer_b, vec,
    wq, wk, wv, wo, wq2, wk2, wv2, wo2,
    x_out, q_out, k_out, v_out, e_out, r_out, o_out, ot_out, p_out, p_out2,
    wq_s, wk_s, wv_s, wo_s, qt_s, kh_s, vt_s, bias, sems,
):
    first = flags[0] == 0
    held = (wq_s, wk_s, wv_s, wo_s)
    source = (wq, wk, wv, wo)
    start_fetch(first, source, (wq2, wk2, wv2, wo2), held, sems)
    half = own.shape[0]
    mine = pl.multiple_of(flags[1] * half, half)
    theirs = pl.multiple_of((1 - flags[1]) * half, half)
    x_out[pl.ds(mine, half), :] = jnp.where(first, own[...], far[...])
    x_out[pl.ds(theirs, half), :] = jnp.where(first, peer_a[...], peer_b[...])
    attention_forward(
        flags, x_out, vec, held, lambda i: wait_fetch(i, source, held, sems),
        (q_out, k_out, v_out, e_out, r_out, o_out, ot_out, p_out, p_out2), (qt_s, kh_s, vt_s, bias),
    )


def attention_next_kernel(
    flags, normal_one, part_a, part_a2, part_b, part_b2, vec_prev, vec,
    wq, wk, wv, wo, wq2, wk2, wv2, wo2,
    n2_out, i2_out, x_out, q_out, k_out, v_out, e_out, r_out, o_out, ot_out, p_out, p_out2,
    wq_s, wk_s, wv_s, wo_s, qt_s, kh_s, vt_s, bias, sems,
):
    held = (wq_s, wk_s, wv_s, wo_s)
    source = (wq, wk, wv, wo)
    start_fetch(flags[0] == 1, source, (wq2, wk2, wv2, wo2), held, sems)

    half = part_a.shape[0]
    for c, (one, two) in enumerate(((part_a, part_b), (part_a2, part_b2))):

        def body(rows, c=c, one=one, two=two):
            place = pl.ds(rows.start + c * half, RB)
            normal, inverse, output = second_norm(normal_one[place, :], one, two, vec_prev, rows)
            n2_out[place, :] = normal
            i2_out[place, :] = inverse
            x_out[place, :] = output.astype(BF)

        row_blocks(half, body)
    attention_forward(
        flags, x_out, vec, held, lambda i: wait_fetch(i, source, held, sems),
        (q_out, k_out, v_out, e_out, r_out, o_out, ot_out, p_out, p_out2), (qt_s, kh_s, vt_s, bias),
    )


def second_norm(normal_one, part_a, part_b, vec, rows):
    normed = normal_one * vec[V_G1 : V_G1 + 1, :] + vec[V_B1 : V_B1 + 1, :]
    total = part_a[rows, :].astype(F32) + part_b[rows, :].astype(F32)
    normal, inverse = norm_rows(total + vec[V_BU : V_BU + 1, :] + normed)
    return normal, inverse, normal * vec[V_G2 : V_G2 + 1, :] + vec[V_B2 : V_B2 + 1, :]


def ffn_forward_kernel(
    layer, flags, x, part_a, part_b, vec, wi, wu, wi2, wu2,
    n1_out, i1_out, n1b_out, a_out, d_out, p_out,
    wi_s, wu_s, sems,
):
    held = (wi_s, wu_s)
    source = (wi, wu)
    start_fetch(flags[0] == layer, source, (wi2, wu2), held, sems)
    size = x.shape[0]
    width = wi_s.shape[1]
    model = wi_s.shape[0]

    def first(rows):
        total = part_a[rows, :].astype(F32) + part_b[rows, :].astype(F32)
        normal, inverse = norm_rows(total + vec[V_BO : V_BO + 1, :] + x[rows, :].astype(F32))
        n1_out[rows, :] = normal
        i1_out[rows, :] = inverse
        n1b_out[rows, :] = (normal * vec[V_G1 : V_G1 + 1, :] + vec[V_B1 : V_B1 + 1, :]).astype(BF)

    row_blocks(size, first)
    wait_fetch(0, source, held, sems)
    block = 256

    def inner(rows):
        rows_in = n1b_out[rows, :]
        for j in range(width // block):
            cols = slice(j * block, (j + 1) * block)
            at = j * block
            bias = vec[V_BI + at // model : V_BI + at // model + 1, at % model : at % model + block]
            hidden = dot(rows_in, wi_s[:, cols]) + bias
            spread = 0.5 + 0.5 * lax.erf(hidden * root_half)
            a_out[rows, cols] = (hidden * spread).astype(BF)
            d_out[rows, cols] = (
                spread + hidden * jnp.exp(-0.5 * hidden * hidden) * inverse_root
            ).astype(BF)

    row_blocks(size, inner)
    wait_fetch(1, source, held, sems)

    def outer(i):
        rows = part_of(i, 256)
        p_out[rows, :] = dot(a_out[rows, :], wu_s[...]).astype(BF)

    loop(size // 256, outer)


def ffn_backward(g2, d, w, outs, wait, small):
    wi_s, wu_s = w
    gh_out, p_out = outs
    size = g2.shape[0]
    model, width = wi_s.shape
    wait(1)
    block = 384

    def hidden(i):
        rows = part_of(i, 256)
        gb = g2[rows, :]
        for j in range(width // block):
            cols = slice(j * block, (j + 1) * block)
            gh = (dot_nt(gb, wu_s[cols, :]) * d[rows, cols].astype(F32)).astype(BF)
            gh_out[rows, cols] = gh
            at = j * block
            small[3 + at // model : 4 + at // model, at % model : at % model + block] += column_sum(
                gh.astype(F32)
            )

    loop(size // 256, hidden)
    wait(0)

    def inner(i):
        rows = part_of(i, 256)
        p_out[rows, :] = dot_nt(gh_out[rows, :], wi_s[...]).astype(BF)

    loop(size // 256, inner)


def ffn_back_last_kernel(
    chunk, flags, normal_one, part_a, part_b, vec, own, far, peer_a, peer_b, d, small_in,
    wi, wu, wi2, wu2,
    y_out, g_out, gb_out, gh_out, p_out, small,
    gy_s, wi_s, wu_s, sems,
):
    held = (wi_s, wu_s)
    source = (wi, wu)
    second = flags[0] == 1
    start_fetch(second, source, (wi2, wu2), held, sems)
    here = flags[1] == chunk
    gy_s[...] = jnp.where(
        here,
        jnp.where(second, own[...], far[...]),
        jnp.where(second, peer_a[...], peer_b[...]),
    )
    small[...] = small_in[...]

    def body(rows):
        normal, inverse, output = second_norm(normal_one[rows, :], part_a, part_b, vec, rows)
        y_out[rows, :] = output.astype(BF)
        ffn_back_rows(gy_s[rows, :].astype(F32), normal, inverse, vec, rows, g_out, gb_out, small)

    row_blocks(y_out.shape[0], body)
    ffn_backward(gb_out, d, held, (gh_out, p_out), lambda i: wait_fetch(i, source, held, sems), small)


def ffn_back_rows(upstream, normal, inverse, vec, rows, g_out, gb_out, small):
    grad = norm_back_rows(upstream, normal, inverse, vec[V_G2 : V_G2 + 1, :])
    g_out[rows, :] = grad
    gb_out[rows, :] = grad.astype(BF)
    small[0:1, :] += column_sum(grad)
    small[1:2, :] += column_sum(upstream * normal)
    small[2:3, :] += column_sum(upstream)


def ffn_back_next_kernel(
    flags, g1, part_a, part_b, normal_two, inverse_two, vec, d, small_in, wi, wu, wi2, wu2,
    g_out, gb_out, gh_out, p_out, small,
    wi_s, wu_s, sems,
):
    held = (wi_s, wu_s)
    source = (wi, wu)
    start_fetch(flags[0] == 0, source, (wi2, wu2), held, sems)
    small[...] = small_in[...]

    def body(rows):
        total = part_a[rows, :].astype(F32) + part_b[rows, :].astype(F32)
        upstream = (g1[rows, :] + total).astype(BF).astype(F32)
        ffn_back_rows(
            upstream, normal_two[rows, :], inverse_two[rows, :], vec, rows, g_out, gb_out, small
        )

    row_blocks(g1.shape[0], body)
    ffn_backward(gb_out, d, held, (gh_out, p_out), lambda i: wait_fetch(i, source, held, sems), small)


def attention_back_kernel(
    layer, flags, g2, part_a, part_a2, part_b, part_b2, normal_one, inverse_one, vec,
    q, k, v, e, r, ot_f,
    wq, wk, wv, wo, wq2, wk2, wv2, wo2,
    g_out, gb_out, gqkv_out, p_out, p_out2, small,
    wq_s, wk_s, wv_s, wo_s, got_s, go_s, kt_s, vh_s, qh_s, gqt_s, sems,
):
    held = (wq_s, wk_s, wv_s, wo_s)
    source = (wq, wk, wv, wo)
    start_fetch(flags[0] == layer, source, (wq2, wk2, wv2, wo2), held, sems)
    size, model = g2.shape
    width = q.shape[1]
    heads = width // HD
    small[...] = jnp.zeros_like(small)

    half = size // 2
    for c, (one, two) in enumerate(((part_a, part_b), (part_a2, part_b2))):

        def body(rows, c=c, one=one, two=two):
            place = pl.ds(rows.start + c * half, RB)
            upstream = g2[place, :] + (one[rows, :].astype(F32) + two[rows, :].astype(F32))
            normal = normal_one[place, :]
            grad = norm_back_rows(upstream, normal, inverse_one[place, :], vec[V_G1 : V_G1 + 1, :])
            g_out[place, :] = grad
            gb_out[place, :] = grad.astype(BF)
            small[0:1, :] += column_sum(grad)
            small[1:2, :] += column_sum(upstream * normal)
            small[2:3, :] += column_sum(upstream)

        row_blocks(half, body)

    def split(i):
        rows = part_of(i, 256)
        kt_s[:, rows] = k[rows, :].astype(F32).T.astype(BF)
        for h in range(heads):
            hs = slice(h * HD, (h + 1) * HD)
            vh_s[h, rows, :] = v[rows, hs]
            qh_s[h, rows, :] = q[rows, hs]

    loop(size // 256, split)
    wait_fetch(3, source, held, sems)

    def context(i):
        rows = part_of(i, 256)
        gqt_s[:, rows] = dot_nt(gb_out[rows, :], wo_s[...]).T

    loop(size // 256, context)

    def attend(h):
        hs = part_of(h, HD)
        scaled = (gqt_s[hs, :] * r[h]).astype(BF)
        got_s[...] = scaled
        scaled = scaled.astype(F32)
        delta = column_sum(scaled * ot_f[hs, :])
        go_s[...] = scaled.T.astype(BF)
        grad_v = jnp.zeros((size, HD), F32)
        grad_k = jnp.zeros((size, HD), F32)
        for j in range(size // 256):
            cols = pl.ds(j * 256, 256)
            raised = e[h, :, cols]
            grad_p = dot(vh_s[h], got_s[:, cols]) - delta[:, j * 256 : (j + 1) * 256]
            grad_s = (raised.astype(F32) * grad_p).astype(BF)
            grad_v = grad_v + dot(raised, go_s[cols, :])
            grad_k = grad_k + dot(grad_s, qh_s[h, cols, :])
            gqt_s[hs, cols] = dot(kt_s[hs, :], grad_s) * (1.0 / math.sqrt(HD))
        vh_s[h] = grad_v.astype(BF)
        qh_s[h] = grad_k.astype(BF)

    loop(heads, attend, 2)
    for i in range(3):
        wait_fetch(i, source, held, sems)

    for i, p in enumerate((p_out, p_out2)):
        rows = pl.ds(i * half, half)
        gq = gqt_s[:, rows].T.astype(BF)
        gk = jnp.concatenate([qh_s[h, rows, :] for h in range(heads)], axis=1)
        gv = jnp.concatenate([vh_s[h, rows, :] for h in range(heads)], axis=1)
        gqkv_out[rows, :width] = gq
        gqkv_out[rows, width : 2 * width] = gk
        gqkv_out[rows, 2 * width :] = gv
        small[3:4, :width] += column_sum(gq.astype(F32))
        small[3:4, width:] += column_sum(gv.astype(F32))
        p[...] = (
            dot_nt(gq, wq_s[...]) + dot_nt(gk, wk_s[...]) + dot_nt(gv, wv_s[...])
        ).astype(BF)


HEAVY, LIGHT = 20, 0
PAD = 16
UNITS = (2, 2)
ORDER = (
    "KC2a", "KC2b", "KWF2", "KD2", "KWA2", "a2gn", "f2gn", "KC1a", "f2ba1", "KC1b", "KWF1",
    "f2aa1", "KD1", "KWA1", "f2aa2", "f1gn", "a2a1", "f2ba2", "a1gn", "f2aa3", "f1aa1", "a2a2",
    "f2ba3", "f1ba1", "f2aa4", "f1aa2", "a2a3", "f2ba4", "a1a1", "f1aa3", "f1ba2", "a2a4", "a1a2",
    "f1ba3", "f1aa4", "a1a3", "f1ba4", "finF", "a1a4", "finA",
)


def send_both(held, outs, sems):
    copies = [pltpu.make_async_copy(held.at[i], outs[i], sems.at[i]) for i in range(2)]
    for copy in copies:
        copy.start()
    for copy in copies:
        copy.wait()


def ffn_rows(units, block):
    if units == 1:
        return (2 * block + PAD,), lambda i, half: half * (2 * block + PAD) + i * block
    return (block + PAD, block), lambda i, half: i * 2 * (block + PAD) + half * (block + PAD * (1 - i))


def ffn_product_kernel(units, flags, a, gb, gh, n1b, small, ours, theirs, held, sems):
    model = gb.shape[1]
    block = model // 2
    extra = jnp.concatenate([small[...], jnp.zeros((PAD - 8, model), F32)], axis=0).astype(BF)
    sizes, start = ffn_rows(units, block)
    for i in range(2):

        def products(j, i=i):
            here = pl.ds(pl.multiple_of(start(i, flags[6] ^ j), 16), block)
            held[flags[0], here, :] = dot_tn(a[:, part_of(2 * j + i, block)], gb[...]).astype(BF)
            held[1 - flags[0], here, :] = dot_tn(
                n1b[:, i * block : (i + 1) * block], gh[:, part_of(j, model)]
            ).astype(BF)

        loop(2, products)
    for i in range(2):
        for half in range(2):
            at = (half + 1) * sizes[0]
            held[i, at - PAD : at, :] = extra
    send_both(held, (ours, theirs), sems)


def attention_product_kernel(flags, x, gqkv, o, gb, small, ours, theirs, held, sems):
    model = gb.shape[1]
    width = o.shape[1]
    rows = model + PAD

    def products(i):
        here = pl.ds(pl.multiple_of((flags[6] ^ (i % 2)) * rows, 16), model)
        held[flags[0] ^ (i // 2), here, :] = dot_tn(x[...], gqkv[:, part_of(i, width)]).astype(BF)

    loop(3, products)
    base = pl.multiple_of((flags[6] ^ 1) * rows, 16)
    for i in range(2):
        held[1 - flags[0], pl.ds(base + i * width, width), :] = dot_tn(
            o[...], gb[:, i * width : (i + 1) * width]
        ).astype(BF)
    extra = jnp.concatenate([small[:, :width], small[:, width:]], axis=0).astype(BF)
    for i in range(2):
        for half in range(2):
            held[i, half * rows + model : (half + 1) * rows, :] = extra
    send_both(held, (ours, theirs), sems)


def fetch_sums(flags, layers, held, sems):
    def copies(layer):
        pieces = layers[layer]
        for u, (sums, row, rows, at) in enumerate(pieces):
            for far in range(2):
                for beside in range(2):
                    slot = 2 * (flags[0] ^ far) + (flags[6] ^ beside)
                    i = 2 * far + beside
                    yield pltpu.make_async_copy(
                        sums[i].at[pl.ds(row, rows), :],
                        held.at[slot, pl.ds(at, rows), :],
                        sems.at[4 * u + i],
                    )

    for layer in range(2):

        @pl.when(flags[0] == layer)
        def _(layer=layer):
            for copy in copies(layer):
                copy.start()
            for copy in copies(layer):
                copy.wait()


def ffn_finish_kernel(units, flags, *refs):
    counts = [4 * n for n in units]
    sums = refs[: sum(counts)]
    outer, inside, bias_outer, gain, bias, bias_inner, held, sems = refs[sum(counts) :]
    model = outer.shape[1]
    block = model // 2
    layers = []
    for n, mine in zip(units, (sums[: counts[0]], sums[counts[0] :])):
        if n == 1:
            layers.append([(mine, 0, 2 * block + PAD, 0)])
        else:
            layers.append(
                [
                    (mine[:4], 0, block, 0),
                    (mine[4:], 0, block, block),
                    (mine[:4], block, PAD, 2 * block),
                ]
            )
    fetch_sums(flags, layers, held, sems)
    for j in range(2):
        outer[j * model : (j + 1) * model, :] = held[j, :model, :].astype(F32)
        inside[:, j * model : (j + 1) * model] = held[2 + j, :model, :].astype(F32)
    small = held[0, model : model + PAD, :].astype(F32)
    for i, out in enumerate((bias_outer, gain, bias)):
        out[...] = small[i : i + 1, :]
    for i in range(bias_inner.shape[1] // model):
        bias_inner[:, i * model : (i + 1) * model] = small[3 + i : 4 + i, :]


def attention_finish_kernel(flags, *refs):
    sums, (q, k, v, out, bias_out, gain, bias, bias_q, bias_v) = refs[:8], refs[8:17]
    held, sems = refs[17], refs[18]
    model, width = q.shape
    rows = model + PAD
    fetch_sums(flags, [[(sums[:4], 0, rows, 0)], [(sums[4:], 0, rows, 0)]], held, sems)
    q[...] = held[0, :model, :].astype(F32)
    k[...] = held[1, :model, :].astype(F32)
    v[...] = held[2, :model, :].astype(F32)
    for i in range(2):
        out[:, i * width : (i + 1) * width] = held[3, i * width : (i + 1) * width, :].astype(F32)
    left = held[0, model : model + PAD, :].astype(F32)
    for i, row in enumerate((bias_out, gain, bias)):
        row[:, :width] = left[i : i + 1, :]
        row[:, width:] = left[8 + i : 9 + i, :]
    bias_q[...] = left[3:4, :]
    bias_v[...] = left[11:12, :]


def ordered(array, after):
    return lax.optimization_barrier((array,) + tuple(after))[0] if after else array


def call(
    kernel, operands, spaces, outs, scratch, flops, after=(), out_space="v", chunk=0, before=(),
    weight=LIGHT,
):
    count = len(operands)
    out_space = out_space * len(outs) if len(out_space) == 1 else out_space
    passed = [i for i, c in enumerate(out_space) if c == "c" and before]
    extra = [before[i] for i in passed]
    operands = (ordered(operands[0], after),) + tuple(operands[1:])

    def body(*refs):
        kernel(*refs[:count], *refs[count + len(extra) :])

    def spec(letter, shape):
        if letter == "c":
            return pl.BlockSpec((shape[0] // 2, shape[1]), lambda i: (chunk, 0))
        return pl.BlockSpec(memory_space={"s": pltpu.SMEM, "v": pltpu.VMEM, "a": pl.ANY}[letter])

    return pl.pallas_call(
        body,
        grid=(1,) if "c" in spaces else (),
        out_shape=[jax.ShapeDtypeStruct(s, t) for s, t in outs],
        in_specs=[spec(c, x.shape) for c, x in zip(spaces, operands)]
        + [pl.BlockSpec(memory_space=pl.ANY)] * len(extra),
        out_specs=[spec(c, s) for c, (s, _) in zip(out_space, outs)],
        scratch_shapes=scratch,
        input_output_aliases={count + i: o for i, o in enumerate(passed)},
        compiler_params=pltpu.CompilerParams(vmem_limit_bytes=VMEM_BYTES),
        cost_estimate=pl.CostEstimate(
            flops=flops * weight, bytes_accessed=(8 << 20) * weight, transcendentals=0
        ),
    )(*operands, *extra)


def attention_call(
    flags, lead, lead_spaces, weights, size, model, width, kernel, extra_outs, after=()
):
    heads = width // HD
    outs = extra_outs + [
        ((size, model), BF),
        ((size, width), BF),
        ((size, width), BF),
        ((size, width), BF),
        ((heads, size, size), BF),
        ((heads, 1, size), F32),
        ((size, width), BF),
        ((width, size), F32),
        ((size // 2, model), BF),
        ((size // 2, model), BF),
    ]
    scratch = [pltpu.VMEM((model, width), BF)] * 3 + [
        pltpu.VMEM((width, model), BF),
        pltpu.VMEM((width, size), BF),
        pltpu.VMEM((heads, size, HD), BF),
        pltpu.VMEM((width, size), BF),
        pltpu.VMEM((size, size), F32),
        pltpu.SemaphoreType.DMA((4,)),
    ]
    return call(
        kernel, (flags,) + lead + weights, "s" + lead_spaces + "a" * 8, outs, scratch,
        2 * size * width * model * 4 + 4 * heads * size * size * HD, after, weight=HEAVY,
    )


def swap(block, axis):
    return lax.ppermute(block, axis, [(0, 1), (1, 0)])


def across(block, routes):
    return lax.ppermute(
        block, ("section", "tensor"), [(a[0] * 2 + a[1], b[0] * 2 + b[1]) for a, b in routes]
    )


def batch_pairs():
    return [(i, i ^ 1) for i in range(lax.axis_size("batch"))]


def pair_swap(block):
    return lax.ppermute(block, "batch", batch_pairs())


def line_end():
    line = lax.axis_index("batch") // 2
    return (line == 0) | (line == 3)


STAGES = (
    ("in", ((0, 2), (1, 3), (6, 4), (7, 5))),
    ("middle", ((2, 4), (3, 5), (4, 2), (5, 3))),
    ("out", ((2, 0), (3, 1), (4, 6), (5, 7))),
)


def rest_of_line(mine):
    count = lax.axis_size("batch")
    if count & (count - 1):
        lines = [list(range(i, count, 2)) for i in range(2)]
        return lax.psum(mine, "batch", axis_index_groups=lines)
    step = 2
    while step < count:
        mine = mine + lax.ppermute(mine, "batch", [(i, i ^ step) for i in range(count)])
        step *= 2
    return mine


def pad_rows(rows, count):
    return jnp.concatenate([rows, jnp.zeros((count - rows.shape[0], rows.shape[1]), rows.dtype)], 0)


def shards(
    section_ends, lengths, w_query, b_query, w_key, w_value, b_value, w_out, b_out,
    norm1_gain, norm1_bias, w_inner, b_inner, w_outer, b_outer, norm2_gain, norm2_bias,
):
    section = lax.axis_index("section")
    tensor = lax.axis_index("tensor")
    first = section == 0
    held = section_ends[0]
    half, model = held.shape[1], held.shape[2]
    size = 2 * half
    width = w_query.shape[2]
    inner = w_inner.shape[2]
    heads = width // HD
    flags = jnp.concatenate(
        [
            jnp.stack([section, tensor]).astype(jnp.int32),
            lax.dynamic_slice_in_dim(lengths, section, 1, 0)[0],
            (lax.axis_index("batch") % 2).astype(jnp.int32)[None],
        ]
    )

    x_peer_a = across(held[0], [((0, 0), (0, 1)), ((0, 1), (0, 0))])
    x_peer_b = across(held[1], [((0, 0), (1, 1)), ((0, 1), (1, 0))])
    x_far = across(held[1], [((0, 0), (1, 0)), ((0, 1), (1, 1))])

    attention_own = (w_query[0], w_key[0], w_value[0], w_out[0])
    ffn_own = (w_inner[0], w_outer[0])
    vec_own = pad_rows(
        jnp.concatenate(
            [
                jnp.concatenate([b_query, b_value], axis=1),
                b_out, norm1_gain, norm1_bias, b_inner.reshape(-1, model), b_outer,
                norm2_gain, norm2_bias,
            ],
            axis=0,
        ),
        V_ROWS,
    )
    vec_far = swap(vec_own, "section")
    attention_far = tuple(swap(w, "section") for w in attention_own)
    ffn_far = tuple(swap(w, "section") for w in ffn_own)
    attention_w = attention_own + attention_far
    ffn_w = ffn_own + ffn_far
    vec_one = jnp.where(first, vec_own, vec_far)
    vec_two = jnp.where(first, vec_far, vec_own)

    def send(parts):
        return [swap(part, "tensor") for part in parts]

    def ffn_forward(layer, x, parts, vec, after=()):
        outs = ()
        sums = []
        for c, (part, got) in enumerate(zip(parts, send(parts))):
            outs = call(
                functools.partial(ffn_forward_kernel, layer),
                (flags, x, part, got, vec) + ffn_w,
                "scvvvaaaa",
                [
                    ((size, model), F32), ((size, 1), F32), ((size, model), BF),
                    ((size, inner), BF), ((size, inner), BF), ((half, model), BF),
                ],
                [
                    pltpu.VMEM((model, inner), BF), pltpu.VMEM((inner, model), BF),
                    pltpu.SemaphoreType.DMA((2,)),
                ],
                2 * size * model * inner, after, "cccccv", c, outs,
            )
            sums.append(outs[-1])
        return *outs[:-1], sums

    x_one, *heads_one, part, part2 = attention_call(
        flags, (held[0], x_far, x_peer_a, x_peer_b, vec_one), "vvvvv", attention_w,
        size, model, width, attention_first_kernel, [], ffn_far,
    )
    n1_one, i1_one, n1b_one, a_one, d_one, parts = ffn_forward(
        0, x_one, (part, part2), vec_one
    )
    later = [ordered(held[i], (n1b_one,)) for i in range(2)]
    gy_peer_a = across(later[1], [((1, 0), (1, 1)), ((1, 1), (1, 0))])
    gy_peer_b = across(later[0], [((1, 0), (0, 1)), ((1, 1), (0, 0))])
    gy_far = across(later[0], [((1, 0), (0, 0)), ((1, 1), (0, 1))])

    n2_one, i2_one, x_two, *heads_two, part, part2 = attention_call(
        flags, (n1_one, *parts, *send(parts), vec_one, vec_two), "vvvvvvv", attention_w,
        size, model, width, attention_next_kernel, [((size, model), F32), ((size, 1), F32)],
    )
    n1_two, i1_two, n1b_two, a_two, d_two, parts_two = ffn_forward(
        1, x_two, (part, part2), vec_two, (gy_peer_a, gy_peer_b, gy_far)
    )

    ffn_outs = [
        ((size, model), F32), ((size, model), BF), ((size, inner), BF), ((half, model), BF),
        ((8, model), F32),
    ]
    ffn_scratch = [
        pltpu.VMEM((model, inner), BF), pltpu.VMEM((inner, model), BF),
        pltpu.SemaphoreType.DMA((2,)),
    ]

    def attention_back(layer, g2, parts, got, n1, i1, vec, saved, after):
        q, k, v, e, r, o, ot_f = saved
        *outs, part, part2, small = call(
            functools.partial(attention_back_kernel, layer),
            (flags, g2, *parts, *got, n1, i1, vec, q, k, v, e, r, ot_f) + attention_w,
            "s" + "v" * 14 + "a" * 8,
            [
                ((size, model), F32), ((size, model), BF), ((size, 3 * width), BF),
                ((half, model), BF), ((half, model), BF), ((8, model), F32),
            ],
            [pltpu.VMEM((model, width), BF)] * 3
            + [
                pltpu.VMEM((width, model), BF),
                pltpu.VMEM((HD, size), BF),
                pltpu.VMEM((size, HD), BF),
                pltpu.VMEM((width, size), BF),
                pltpu.VMEM((heads, size, HD), BF),
                pltpu.VMEM((heads, size, HD), BF),
                pltpu.VMEM((width, size), F32),
                pltpu.SemaphoreType.DMA((4,)),
            ],
            2 * size * width * model * 4 + 8 * heads * size * size * HD,
            after, weight=HEAVY,
        )
        return *outs, [part, part2], small

    state = {}
    last = ()
    chunked = [()]

    def add(groups, arrays, shapes):
        sums = []
        for group, (rows, _) in zip(groups, shapes):
            terms = [arrays[i][row : row + rows] for i, row in group]
            sums.append(sum(terms[1:], ordered(terms[0], last)))
        return sums

    def back_last(c):
        part = parts_two[c]
        outs = call(
            functools.partial(ffn_back_last_kernel, c),
            (flags, n1_two, part, got_two[c], vec_two, held[1], gy_far, gy_peer_a, gy_peer_b,
             d_two, small_zero if c == 0 else state["small_f2"]) + ffn_w,
            "sc" + "v" * 7 + "cv" + "a" * 4,
            [((size, model), BF)] + ffn_outs,
            [pltpu.VMEM((half, model), BF)] + ffn_scratch,
            2 * size * model * inner, last, "ccccvv", c, chunked[0],
        )
        chunked[0] = outs if c == 0 else ()
        state["small_f2"] = outs[-1]
        state["y_two"], state["g2_two"], state["g2b_two"], state["gh_two"] = outs[:4]
        state.setdefault("sums_two", []).append(outs[-2])
        state.setdefault("sums_two_got", []).append(swap(outs[-2], "tensor"))
        return outs[-1]

    def back_next(c):
        outs = call(
            ffn_back_next_kernel,
            (flags, state["g1_two"], state["p4_two"][c], state["p4_two_got"][c], n2_one, i2_one,
             vec_one, d_one, small_zero if c == 0 else state["small_f1"]) + ffn_w,
            "scvvccvcv" + "a" * 4,
            ffn_outs,
            ffn_scratch,
            2 * size * model * inner, last, "cccvv", c, chunked[0],
        )
        chunked[0] = outs if c == 0 else ()
        state["small_f1"] = outs[-1]
        state["g2_one"], state["g2b_one"], state["gh_one"] = outs[:3]
        state.setdefault("sums_one", []).append(outs[-2])
        state.setdefault("sums_one_got", []).append(swap(outs[-2], "tensor"))
        return outs[-1]

    def back_attention(name, layer, *rest):
        grad, rows, gqkv, parts, small = attention_back(
            layer, state["g2_" + name], state["sums_" + name], state["sums_" + name + "_got"],
            *rest, last,
        )
        state["g1_" + name], state["g1b_" + name], state["gqkv_" + name] = grad, rows, gqkv
        state["p4_" + name], state["small_a_" + name] = parts, small
        if name == "two":
            state["p4_two_got"] = send(parts)
        return small

    def put(base, ours, theirs):
        state[base] = ours
        state[base + "_got"] = swap(theirs, "section")

    def ffn_products(base, units, a, gb, gh, n1b, small):
        rows = 2 * (model + PAD)
        ours, theirs = call(
            functools.partial(ffn_product_kernel, units), (flags, a, gb, gh, n1b, small), "svvvvv",
            [((rows, model), BF)] * 2,
            [pltpu.VMEM((2, rows, model), BF), pltpu.SemaphoreType.DMA((2,))],
            4 * size * model * inner, last, "a",
        )
        put(base, ours, theirs)
        return ours

    def attention_products(base, gqkv, x, o, gb, small):
        rows = 2 * (model + PAD)
        ours, theirs = call(
            attention_product_kernel, (flags, x, gqkv, o, gb, small), "svvvvv",
            [((rows, width), BF)] * 2,
            [pltpu.VMEM((2, rows, width), BF), pltpu.SemaphoreType.DMA((2,))],
            8 * size * model * width, last, "a",
        )
        put(base, ours, theirs)
        return ours

    units = {}
    for base, count in (("f1", UNITS[0]), ("f2", UNITS[1])):
        row = 0
        for name, rows in zip("ab", ffn_rows(count, model // 2)[0]):
            units[base + name] = (base, row, rows, model)
            row += 2 * rows
    for base in ("a1", "a2"):
        units[base] = (base, 0, model + PAD, width)

    def give(base):
        names = [n for n in units if units[n][0] == base]
        outs = add(
            [[(0, units[n][1] + units[n][2]), (1, units[n][1] + units[n][2])] for n in names],
            (state[base], state[base + "_got"]),
            [units[n][2:] for n in names],
        )
        for n, out in zip(names, outs):
            state[n + "x"] = pair_swap(out)
        return outs[0]

    def step(name, stage):
        base, row, rows, columns = units[name]
        shape = (rows, columns)
        if stage == 0:
            (mine,) = add(
                [[(0, row), (1, row), (2, 0)]],
                (state[base], state[base + "_got"], state[name + "x"]), [shape],
            )
        elif lax.axis_size("batch") != 8:
            mine = rest_of_line(state[name]) if stage == 1 else state[name]
        elif stage < 3:
            (mine,) = add([[(0, 0), (1, 0)]], (state[name], state[name + "s"]), [shape])
        else:
            mine = jnp.where(at_end, state[name + "s"], ordered(state[name], last))
        state[name] = mine
        if stage < 3:
            state[name + "s"] = lax.ppermute(mine, "batch", STAGES[stage][1]) if lax.axis_size("batch") == 8 else None
        else:
            both = (mine, pair_swap(mine))
            route = (1, 0) if base[1] == "1" else (0, 1)
            state[name] = both + tuple(lax.ppermute(b, "section", [route]) for b in both)
        return mine

    def finish_ffn():
        sums = sum((state[n] for n in sorted(units) if n[0] == "f"), ())
        outs = call(
            functools.partial(ffn_finish_kernel, UNITS), (flags,) + sums, "s" + "a" * len(sums),
            [((inner, model), F32), ((model, inner), F32)] + [((1, model), F32)] * 3
            + [((1, inner), F32)],
            [pltpu.VMEM((4, model + PAD, model), BF), pltpu.SemaphoreType.DMA((12,))],
            size * model, last,
        )
        state["ffn"] = outs
        return outs[-1]

    def finish_attention():
        outs = call(
            attention_finish_kernel, (flags,) + state["a1"] + state["a2"], "s" + "a" * 8,
            [((model, width), F32)] * 3 + [((width, model), F32)] + [((1, model), F32)] * 3
            + [((1, width), F32)] * 2,
            [pltpu.VMEM((4, model + PAD, width), BF), pltpu.SemaphoreType.DMA((4,))],
            size * model, last,
        )
        state["attention"] = outs
        return outs[-1]

    at_end = line_end()
    small_zero = jnp.zeros((8, model), F32)
    got_two = send(parts_two)
    tasks = {
        "KC2a": lambda: back_last(0),
        "KC2b": lambda: back_last(1),
        "KWF2": lambda: ffn_products(
            "f2", UNITS[1], a_two, state["g2b_two"], state["gh_two"], n1b_two, state["small_f2"]
        ),
        "KD2": lambda: back_attention("two", 1, n1_two, i1_two, vec_two, heads_two),
        "KWA2": lambda: attention_products(
            "a2", state["gqkv_two"], x_two, heads_two[5], state["g1b_two"], state["small_a_two"]
        ),
        "KC1a": lambda: back_next(0),
        "KC1b": lambda: back_next(1),
        "KWF1": lambda: ffn_products(
            "f1", UNITS[0], a_one, state["g2b_one"], state["gh_one"], n1b_one, state["small_f1"]
        ),
        "KD1": lambda: back_attention("one", 0, n1_one, i1_one, vec_one, heads_one),
        "KWA1": lambda: attention_products(
            "a1", state["gqkv_one"], x_one, heads_one[5], state["g1b_one"], state["small_a_one"]
        ),
        "finF": finish_ffn,
        "finA": finish_attention,
    }
    for base in ("f1", "f2", "a1", "a2"):
        tasks[base + "gn"] = functools.partial(give, base)
    for name in units:
        for stage in range(4):
            tasks[name + "a" + str(stage + 1)] = functools.partial(step, name, stage)
    for name in ORDER:
        last = (tasks[name](),)

    part_one, part_one2 = state["p4_one"]
    part_mine = jnp.where(tensor == 0, part_one, part_one2)
    part_theirs = jnp.where(tensor == 0, part_one2, part_one)
    total = part_mine.astype(F32) + swap(part_theirs, "tensor").astype(F32)
    gx = (lax.dynamic_slice_in_dim(state["g1_one"], tensor * half, half, 0) + total).astype(BF)
    y_mine = lax.dynamic_slice_in_dim(state["y_two"], tensor * half, half, 0)
    y_far = lax.ppermute(y_mine, "section", [(0, 1)])
    gx_far = lax.ppermute(gx, "section", [(1, 0)])
    section_results = jnp.stack(
        [jnp.where(first, gx, y_far), jnp.where(first, gx_far, y_mine)], axis=0
    )[None]
    grad_outer, grad_inner, bias_outer, gain_two, bias_two, bias_inner = state["ffn"]
    grad_q, grad_k, grad_v, grad_out, bias_out, gain_one, bias_one, bias_q, bias_v = state["attention"]
    return (
        section_results,
        grad_q[None],
        bias_q,
        grad_k[None],
        grad_v[None],
        bias_v,
        grad_out[None],
        bias_out,
        gain_one,
        bias_one,
        grad_inner[None],
        bias_inner,
        grad_outer[None],
        bias_outer,
        gain_two,
        bias_two,
    )


def solution(mesh):
    in_specs = (
        P("section", "batch", "tensor", None),
        P("batch", None),
        P("section", None, "tensor"),
        P("section", "tensor"),
        P("section", None, "tensor"),
        P("section", None, "tensor"),
        P("section", "tensor"),
        P("section", "tensor", None),
        P("section", None),
        P("section", None),
        P("section", None),
        P("section", None, "tensor"),
        P("section", "tensor"),
        P("section", "tensor", None),
        P("section", None),
        P("section", None),
        P("section", None),
    )
    out_specs = (
        P("section", "batch", "tensor", None),
        P("section", None, "tensor"),
        P("section", "tensor"),
        P("section", None, "tensor"),
        P("section", None, "tensor"),
        P("section", "tensor"),
        P("section", "tensor", None),
        P("section", None),
        P("section", None),
        P("section", None),
        P("section", None, "tensor"),
        P("section", "tensor"),
        P("section", "tensor", None),
        P("section", None),
        P("section", None),
        P("section", None),
    )
    return jax.shard_map(shards, mesh=mesh, in_specs=in_specs, out_specs=out_specs, check_vma=False)
```

```python
import functools
import math

import jax
import jax.numpy as jnp
from jax import lax
from jax.experimental import pallas as pl
from jax.experimental.pallas import tpu as pltpu
from jax.sharding import PartitionSpec as P

HD = 64
epsilon = 1e-06
root_half = 0.7071067811865476
inverse_root = 0.3989422804014327
BF = jnp.bfloat16
F32 = jnp.float32
RB = 128
VMEM_BYTES = 56 * 1024 * 1024

V_BQV, V_BO, V_G1, V_B1, V_BI, V_BU, V_G2, V_B2 = 0, 1, 2, 3, 4, 6, 7, 8
V_ROWS = 16


def dot(a, b):
    return lax.dot_general(a, b, (((1,), (0,)), ((), ())), preferred_element_type=F32)


def dot_nt(a, b):
    return lax.dot_general(a, b, (((1,), (1,)), ((), ())), preferred_element_type=F32)


def dot_tn(a, b):
    return lax.dot_general(a, b, (((0,), (0,)), ((), ())), preferred_element_type=F32)


def start_fetch(use_own, own, other, held, sems):
    @pl.when(use_own)
    def _():
        for i in range(len(own)):
            pltpu.make_async_copy(own[i], held[i], sems.at[i]).start()

    @pl.when(jnp.logical_not(use_own))
    def _():
        for i in range(len(own)):
            pltpu.make_async_copy(other[i], held[i], sems.at[i]).start()


def wait_fetch(i, own, held, sems):
    pltpu.make_async_copy(own[i], held[i], sems.at[i]).wait()


def row_blocks(total, body):
    def step(i, carry):
        body(pl.ds(pl.multiple_of(i * RB, RB), RB))
        return carry

    lax.fori_loop(0, total // RB, step, 0)


def loop(count, body, unroll=1):
    def step(i, carry):
        for j in range(unroll):
            body(i * unroll + j)
        return carry

    lax.fori_loop(0, count // unroll, step, 0)


def part_of(i, step):
    return pl.ds(i * step if isinstance(i, int) else pl.multiple_of(i * step, step), step)


def norm_rows(residue):
    center = residue - jnp.mean(residue, axis=-1, keepdims=True)
    inverse = lax.rsqrt(jnp.mean(center * center, axis=-1, keepdims=True) + epsilon)
    return center * inverse, inverse


def norm_back_rows(upstream, normal, inverse, gain):
    scaled = upstream * gain
    centred = scaled - jnp.mean(scaled, axis=-1, keepdims=True)
    return (centred - normal * jnp.mean(scaled * normal, axis=-1, keepdims=True)) * inverse


def column_sum(rows):
    return jnp.sum(rows, axis=0, keepdims=True)


def segment_bias(flags, bias):
    size = bias.shape[0]
    ends = [flags[2]]
    for i in range(3, 5):
        ends.append(ends[-1] + flags[i])
    row = lax.broadcasted_iota(jnp.int32, (1, size), 1)
    row_seg = sum((row >= e).astype(jnp.int32) for e in ends)

    def body(rows):
        col = lax.broadcasted_iota(jnp.int32, (RB, 1), 0) + rows.start
        col_seg = sum((col >= e).astype(jnp.int32) for e in ends)
        bias[rows, :] = jnp.where(col_seg == row_seg, 0.0, -1e30).astype(F32)

    row_blocks(size, body)


def attention_forward(flags, x, vec, weights, wait, outs, scratch):
    wq, wk, wv, wo = weights
    q_out, k_out, v_out, e_out, r_out, o_out, ot_out, *p_outs = outs
    qt_s, kh_s, vt_s, bias = scratch
    size = x.shape[0]
    width = wq.shape[1]
    heads = width // HD
    segment_bias(flags, bias)
    wait(0)
    wait(1)
    wait(2)

    def project(i):
        rows = part_of(i, 256)
        xb = x[rows, :]
        q = (dot(xb, wq[...]) + vec[V_BQV : V_BQV + 1, :width]).astype(BF).astype(F32) * (
            1.0 / math.sqrt(HD)
        )
        q_out[rows, :] = q.astype(BF)
        qt_s[:, rows] = q.T.astype(BF)
        k = dot(xb, wk[...]).astype(BF)
        k_out[rows, :] = k
        for h in range(heads):
            kh_s[h, rows, :] = k[:, h * HD : (h + 1) * HD]
        v = dot(xb, wv[...]) + vec[V_BQV : V_BQV + 1, width : 2 * width]
        v_out[rows, :] = v.astype(BF)
        vt_s[:, rows] = v.T.astype(BF)

    loop(size // 256, project)

    def attend(h):
        hs = part_of(h, HD)
        for j in range(size // 256):
            cols = pl.ds(j * 256, 256)
            scores = dot(kh_s[h], qt_s[hs, cols]) + bias[:, cols]
            highest = jnp.max(scores, axis=0, keepdims=True)
            raised = jnp.exp(scores - highest)
            inverse = 1.0 / jnp.sum(raised, axis=0, keepdims=True)
            raised = raised.astype(BF)
            e_out[h, :, cols] = raised
            r_out[h, :, cols] = inverse
            ot_out[hs, cols] = dot(vt_s[hs, :], raised) * inverse

    loop(heads, attend, 2)
    wait(3)

    for i, p_out in enumerate(p_outs):
        rows = part_of(i, size // 2)
        context = ot_out[:, rows].T.astype(BF)
        o_out[rows, :] = context
        p_out[...] = dot(context, wo[...]).astype(BF)


def attention_first_kernel(
    flags, own, far, peer_a, peer_b, vec,
    wq, wk, wv, wo, wq2, wk2, wv2, wo2,
    x_out, q_out, k_out, v_out, e_out, r_out, o_out, ot_out, p_out, p_out2,
    wq_s, wk_s, wv_s, wo_s, qt_s, kh_s, vt_s, bias, sems,
):
    first = flags[0] == 0
    held = (wq_s, wk_s, wv_s, wo_s)
    source = (wq, wk, wv, wo)
    start_fetch(first, source, (wq2, wk2, wv2, wo2), held, sems)
    half = own.shape[0]
    mine = pl.multiple_of(flags[1] * half, half)
    theirs = pl.multiple_of((1 - flags[1]) * half, half)
    x_out[pl.ds(mine, half), :] = jnp.where(first, own[...], far[...])
    x_out[pl.ds(theirs, half), :] = jnp.where(first, peer_a[...], peer_b[...])
    attention_forward(
        flags, x_out, vec, held, lambda i: wait_fetch(i, source, held, sems),
        (q_out, k_out, v_out, e_out, r_out, o_out, ot_out, p_out, p_out2), (qt_s, kh_s, vt_s, bias),
    )


def attention_next_kernel(
    flags, normal_one, part_a, part_a2, part_b, part_b2, vec_prev, vec,
    wq, wk, wv, wo, wq2, wk2, wv2, wo2,
    n2_out, i2_out, x_out, q_out, k_out, v_out, e_out, r_out, o_out, ot_out, p_out, p_out2,
    wq_s, wk_s, wv_s, wo_s, qt_s, kh_s, vt_s, bias, sems,
):
    held = (wq_s, wk_s, wv_s, wo_s)
    source = (wq, wk, wv, wo)
    start_fetch(flags[0] == 1, source, (wq2, wk2, wv2, wo2), held, sems)

    half = part_a.shape[0]
    for c, (one, two) in enumerate(((part_a, part_b), (part_a2, part_b2))):

        def body(rows, c=c, one=one, two=two):
            place = pl.ds(rows.start + c * half, RB)
            normal, inverse, output = second_norm(normal_one[place, :], one, two, vec_prev, rows)
            n2_out[place, :] = normal
            i2_out[place, :] = inverse
            x_out[place, :] = output.astype(BF)

        row_blocks(half, body)
    attention_forward(
        flags, x_out, vec, held, lambda i: wait_fetch(i, source, held, sems),
        (q_out, k_out, v_out, e_out, r_out, o_out, ot_out, p_out, p_out2), (qt_s, kh_s, vt_s, bias),
    )


def second_norm(normal_one, part_a, part_b, vec, rows):
    normed = normal_one * vec[V_G1 : V_G1 + 1, :] + vec[V_B1 : V_B1 + 1, :]
    total = part_a[rows, :].astype(F32) + part_b[rows, :].astype(F32)
    normal, inverse = norm_rows(total + vec[V_BU : V_BU + 1, :] + normed)
    return normal, inverse, normal * vec[V_G2 : V_G2 + 1, :] + vec[V_B2 : V_B2 + 1, :]


def ffn_forward_kernel(
    layer, flags, x, part_a, part_b, vec, wi, wu, wi2, wu2,
    n1_out, i1_out, n1b_out, a_out, d_out, p_out,
    wi_s, wu_s, sems,
):
    held = (wi_s, wu_s)
    source = (wi, wu)
    start_fetch(flags[0] == layer, source, (wi2, wu2), held, sems)
    size = x.shape[0]
    width = wi_s.shape[1]
    model = wi_s.shape[0]

    def first(rows):
        total = part_a[rows, :].astype(F32) + part_b[rows, :].astype(F32)
        normal, inverse = norm_rows(total + vec[V_BO : V_BO + 1, :] + x[rows, :].astype(F32))
        n1_out[rows, :] = normal
        i1_out[rows, :] = inverse
        n1b_out[rows, :] = (normal * vec[V_G1 : V_G1 + 1, :] + vec[V_B1 : V_B1 + 1, :]).astype(BF)

    row_blocks(size, first)
    wait_fetch(0, source, held, sems)
    block = 256

    def inner(rows):
        rows_in = n1b_out[rows, :]
        for j in range(width // block):
            cols = slice(j * block, (j + 1) * block)
            at = j * block
            bias = vec[V_BI + at // model : V_BI + at // model + 1, at % model : at % model + block]
            hidden = dot(rows_in, wi_s[:, cols]) + bias
            spread = 0.5 + 0.5 * lax.erf(hidden * root_half)
            a_out[rows, cols] = (hidden * spread).astype(BF)
            d_out[rows, cols] = (
                spread + hidden * jnp.exp(-0.5 * hidden * hidden) * inverse_root
            ).astype(BF)

    row_blocks(size, inner)
    wait_fetch(1, source, held, sems)

    def outer(i):
        rows = part_of(i, 256)
        p_out[rows, :] = dot(a_out[rows, :], wu_s[...]).astype(BF)

    loop(size // 256, outer)


def ffn_backward(g2, d, w, outs, wait, small):
    wi_s, wu_s = w
    gh_out, p_out = outs
    size = g2.shape[0]
    model, width = wi_s.shape
    wait(1)
    block = 384

    def hidden(i):
        rows = part_of(i, 256)
        gb = g2[rows, :]
        for j in range(width // block):
            cols = slice(j * block, (j + 1) * block)
            gh = (dot_nt(gb, wu_s[cols, :]) * d[rows, cols].astype(F32)).astype(BF)
            gh_out[rows, cols] = gh
            at = j * block
            small[3 + at // model : 4 + at // model, at % model : at % model + block] += column_sum(
                gh.astype(F32)
            )

    loop(size // 256, hidden)
    wait(0)

    def inner(i):
        rows = part_of(i, 256)
        p_out[rows, :] = dot_nt(gh_out[rows, :], wi_s[...]).astype(BF)

    loop(size // 256, inner)


def ffn_back_last_kernel(
    chunk, flags, normal_one, part_a, part_b, vec, own, far, peer_a, peer_b, d, small_in,
    wi, wu, wi2, wu2,
    y_out, g_out, gb_out, gh_out, p_out, small,
    gy_s, wi_s, wu_s, sems,
):
    held = (wi_s, wu_s)
    source = (wi, wu)
    second = flags[0] == 1
    start_fetch(second, source, (wi2, wu2), held, sems)
    here = flags[1] == chunk
    gy_s[...] = jnp.where(
        here,
        jnp.where(second, own[...], far[...]),
        jnp.where(second, peer_a[...], peer_b[...]),
    )
    small[...] = small_in[...]

    def body(rows):
        normal, inverse, output = second_norm(normal_one[rows, :], part_a, part_b, vec, rows)
        y_out[rows, :] = output.astype(BF)
        ffn_back_rows(gy_s[rows, :].astype(F32), normal, inverse, vec, rows, g_out, gb_out, small)

    row_blocks(y_out.shape[0], body)
    ffn_backward(gb_out, d, held, (gh_out, p_out), lambda i: wait_fetch(i, source, held, sems), small)


def ffn_back_rows(upstream, normal, inverse, vec, rows, g_out, gb_out, small):
    grad = norm_back_rows(upstream, normal, inverse, vec[V_G2 : V_G2 + 1, :])
    g_out[rows, :] = grad
    gb_out[rows, :] = grad.astype(BF)
    small[0:1, :] += column_sum(grad)
    small[1:2, :] += column_sum(upstream * normal)
    small[2:3, :] += column_sum(upstream)


def ffn_back_next_kernel(
    flags, g1, part_a, part_b, normal_two, inverse_two, vec, d, small_in, wi, wu, wi2, wu2,
    g_out, gb_out, gh_out, p_out, small,
    wi_s, wu_s, sems,
):
    held = (wi_s, wu_s)
    source = (wi, wu)
    start_fetch(flags[0] == 0, source, (wi2, wu2), held, sems)
    small[...] = small_in[...]

    def body(rows):
        total = part_a[rows, :].astype(F32) + part_b[rows, :].astype(F32)
        upstream = (g1[rows, :] + total).astype(BF).astype(F32)
        ffn_back_rows(
            upstream, normal_two[rows, :], inverse_two[rows, :], vec, rows, g_out, gb_out, small
        )

    row_blocks(g1.shape[0], body)
    ffn_backward(gb_out, d, held, (gh_out, p_out), lambda i: wait_fetch(i, source, held, sems), small)


def attention_back_kernel(
    layer, flags, g2, part_a, part_a2, part_b, part_b2, normal_one, inverse_one, vec,
    q, k, v, e, r, ot_f,
    wq, wk, wv, wo, wq2, wk2, wv2, wo2,
    g_out, gb_out, gqkv_out, p_out, p_out2, small,
    wq_s, wk_s, wv_s, wo_s, got_s, go_s, kt_s, vh_s, qh_s, gqt_s, sems,
):
    held = (wq_s, wk_s, wv_s, wo_s)
    source = (wq, wk, wv, wo)
    start_fetch(flags[0] == layer, source, (wq2, wk2, wv2, wo2), held, sems)
    size, model = g2.shape
    width = q.shape[1]
    heads = width // HD
    small[...] = jnp.zeros_like(small)

    half = size // 2
    for c, (one, two) in enumerate(((part_a, part_b), (part_a2, part_b2))):

        def body(rows, c=c, one=one, two=two):
            place = pl.ds(rows.start + c * half, RB)
            upstream = g2[place, :] + (one[rows, :].astype(F32) + two[rows, :].astype(F32))
            normal = normal_one[place, :]
            grad = norm_back_rows(upstream, normal, inverse_one[place, :], vec[V_G1 : V_G1 + 1, :])
            g_out[place, :] = grad
            gb_out[place, :] = grad.astype(BF)
            small[0:1, :] += column_sum(grad)
            small[1:2, :] += column_sum(upstream * normal)
            small[2:3, :] += column_sum(upstream)

        row_blocks(half, body)

    def split(i):
        rows = part_of(i, 256)
        kt_s[:, rows] = k[rows, :].astype(F32).T.astype(BF)
        for h in range(heads):
            hs = slice(h * HD, (h + 1) * HD)
            vh_s[h, rows, :] = v[rows, hs]
            qh_s[h, rows, :] = q[rows, hs]

    loop(size // 256, split)
    wait_fetch(3, source, held, sems)

    def context(i):
        rows = part_of(i, 256)
        gqt_s[:, rows] = dot_nt(gb_out[rows, :], wo_s[...]).T

    loop(size // 256, context)

    def attend(h):
        hs = part_of(h, HD)
        scaled = (gqt_s[hs, :] * r[h]).astype(BF)
        got_s[...] = scaled
        scaled = scaled.astype(F32)
        delta = column_sum(scaled * ot_f[hs, :])
        go_s[...] = scaled.T.astype(BF)
        grad_v = jnp.zeros((size, HD), F32)
        grad_k = jnp.zeros((size, HD), F32)
        for j in range(size // 256):
            cols = pl.ds(j * 256, 256)
            raised = e[h, :, cols]
            grad_p = dot(vh_s[h], got_s[:, cols]) - delta[:, j * 256 : (j + 1) * 256]
            grad_s = (raised.astype(F32) * grad_p).astype(BF)
            grad_v = grad_v + dot(raised, go_s[cols, :])
            grad_k = grad_k + dot(grad_s, qh_s[h, cols, :])
            gqt_s[hs, cols] = dot(kt_s[hs, :], grad_s) * (1.0 / math.sqrt(HD))
        vh_s[h] = grad_v.astype(BF)
        qh_s[h] = grad_k.astype(BF)

    loop(heads, attend, 2)
    for i in range(3):
        wait_fetch(i, source, held, sems)

    for i, p in enumerate((p_out, p_out2)):
        rows = pl.ds(i * half, half)
        gq = gqt_s[:, rows].T.astype(BF)
        gk = jnp.concatenate([qh_s[h, rows, :] for h in range(heads)], axis=1)
        gv = jnp.concatenate([vh_s[h, rows, :] for h in range(heads)], axis=1)
        gqkv_out[rows, :width] = gq
        gqkv_out[rows, width : 2 * width] = gk
        gqkv_out[rows, 2 * width :] = gv
        small[3:4, :width] += column_sum(gq.astype(F32))
        small[3:4, width:] += column_sum(gv.astype(F32))
        p[...] = (
            dot_nt(gq, wq_s[...]) + dot_nt(gk, wk_s[...]) + dot_nt(gv, wv_s[...])
        ).astype(BF)


HEAVY, LIGHT = 20, 0
PAD = 16
ORDER = (
    "KC2a", "KC2b", "KWF2", "KD2", "KWA2", "a2gn", "f2gn", "KC1a", "f2ba1", "KC1b", "KWF1",
    "f2aa1", "KD1", "KWA1", "f2aa2", "f1gn", "a2a1", "f2ba2", "a1gn", "a2a2", "f2aa3", "f1aa1",
    "f1ba1", "f2ba3", "f2aa4", "f1aa2", "a2a3", "a1a1", "f2ba4", "f1aa3", "f1ba2", "a2a4", "a1a2",
    "f2bg", "f1ba3", "f1aa4", "a1a3", "a2g", "f1ag", "f1ba4", "f2ag", "a1a4", "f1bg", "finF",
    "a1g", "finA",
)


def send_both(held, outs, sems):
    copies = [pltpu.make_async_copy(held.at[i], outs[i], sems.at[i]) for i in range(2)]
    for copy in copies:
        copy.start()
    for copy in copies:
        copy.wait()


def ffn_rows(block):
    return (block + PAD, block), lambda i, half: i * 2 * (block + PAD) + half * (block + PAD * (1 - i))


def ffn_product_kernel(flags, a, gb, gh, n1b, small, ours, theirs, held, sems):
    model = gb.shape[1]
    block = model // 2
    extra = jnp.concatenate([small[...], jnp.zeros((PAD - 8, model), F32)], axis=0).astype(BF)
    sizes, start = ffn_rows(block)
    for i in range(2):

        def products(j, i=i):
            here = pl.ds(pl.multiple_of(start(i, flags[6] ^ j), 16), block)
            held[flags[0], here, :] = dot_tn(a[:, part_of(2 * j + i, block)], gb[...]).astype(BF)
            held[1 - flags[0], here, :] = dot_tn(
                n1b[:, i * block : (i + 1) * block], gh[:, part_of(j, model)]
            ).astype(BF)

        loop(2, products)
    for i in range(2):
        for half in range(2):
            at = (half + 1) * sizes[0]
            held[i, at - PAD : at, :] = extra
    send_both(held, (ours, theirs), sems)


def attention_product_kernel(flags, x, gqkv, o, gb, small, ours, theirs, held, sems):
    model = gb.shape[1]
    width = o.shape[1]
    rows = model + PAD

    def products(i):
        here = pl.ds(pl.multiple_of((flags[6] ^ (i % 2)) * rows, 16), model)
        held[flags[0] ^ (i // 2), here, :] = dot_tn(x[...], gqkv[:, part_of(i, width)]).astype(BF)

    loop(3, products)
    base = pl.multiple_of((flags[6] ^ 1) * rows, 16)
    for i in range(2):
        held[1 - flags[0], pl.ds(base + i * width, width), :] = dot_tn(
            o[...], gb[:, i * width : (i + 1) * width]
        ).astype(BF)
    extra = jnp.concatenate([small[:, :width], small[:, width:]], axis=0).astype(BF)
    for i in range(2):
        for half in range(2):
            held[i, half * rows + model : (half + 1) * rows, :] = extra
    send_both(held, (ours, theirs), sems)


def fetch_sums(flags, layers, held, sems):
    for layer in range(2):

        @pl.when(flags[0] == layer)
        def _(layer=layer):
            for u, (sums, row, rows, at) in enumerate(layers[layer]):
                for far in range(2):
                    for beside in range(2):
                        slot = 2 * (flags[0] ^ far) + (flags[6] ^ beside)
                        pltpu.make_async_copy(
                            sums[2 * far + beside].at[pl.ds(row, rows), :],
                            held.at[slot, pl.ds(at, rows), :],
                            sems.at[4 * u + slot],
                        ).start()

    def wait(u, slot):
        sums, row, rows, at = layers[0][u]
        pltpu.make_async_copy(
            sums[0].at[pl.ds(row, rows), :], held.at[slot, pl.ds(at, rows), :],
            sems.at[4 * u + slot],
        ).wait()

    return wait


def ffn_finish_kernel(flags, *refs):
    sums = refs[:16]
    outer, inside, bias_outer, gain, bias, bias_inner = refs[16:22]
    held, outer_s, inside_s, sems, out_sems = refs[22:]
    model = outer.shape[1]
    block = model // 2
    layers = [
        [(mine[:4], 0, block, 0), (mine[4:], 0, block, block), (mine[:4], block, PAD, 2 * block)]
        for mine in (sums[:8], sums[8:])
    ]
    wait = fetch_sums(flags, layers, held, sems)
    copies = []
    for u in range(2):
        rows = slice(u * block, (u + 1) * block)
        for j in range(2):
            at = pl.ds(j * model + u * block, block)
            wait(u, j)
            outer_s[at, :] = held[j, rows, :].astype(F32)
            copies.append((outer_s.at[at, :], outer.at[at, :]))
            columns = pl.ds(j * model, model)
            wait(u, 2 + j)
            inside_s[rows, columns] = held[2 + j, rows, :].astype(F32)
            place = pl.ds(u * block, block)
            copies.append((inside_s.at[place, columns], inside.at[place, columns]))
            for i in (len(copies) - 2, len(copies) - 1):
                pltpu.make_async_copy(*copies[i], out_sems.at[i]).start()
    for slot in range(4):
        wait(2, slot)
    small = held[0, model : model + PAD, :].astype(F32)
    for i, out in enumerate((bias_outer, gain, bias)):
        out[...] = small[i : i + 1, :]
    for i in range(bias_inner.shape[1] // model):
        bias_inner[:, i * model : (i + 1) * model] = small[3 + i : 4 + i, :]
    for i, copy in enumerate(copies):
        pltpu.make_async_copy(*copy, out_sems.at[i]).wait()


def attention_finish_kernel(flags, *refs):
    sums, (q, k, v, out, bias_out, gain, bias, bias_q, bias_v) = refs[:8], refs[8:17]
    held, sums_s, out_s, sems, out_sems = refs[17:]
    model, width = q.shape
    rows = model + PAD
    wait = fetch_sums(flags, [[(sums[:4], 0, rows, 0)], [(sums[4:], 0, rows, 0)]], held, sems)
    copies = []
    for slot, target in enumerate((q, k, v, out)):
        wait(0, slot)
        if slot < 3:
            source = sums_s.at[slot]
            source[...] = held[slot, :model, :].astype(F32)
        else:
            source = out_s
            for i in range(2):
                source[:, i * width : (i + 1) * width] = held[
                    slot, i * width : (i + 1) * width, :
                ].astype(F32)
        copies.append(pltpu.make_async_copy(source, target, out_sems.at[slot]))
        copies[-1].start()
    left = held[0, model : model + PAD, :].astype(F32)
    for i, row in enumerate((bias_out, gain, bias)):
        row[:, :width] = left[i : i + 1, :]
        row[:, width:] = left[8 + i : 9 + i, :]
    bias_q[...] = left[3:4, :]
    bias_v[...] = left[11:12, :]
    for copy in copies:
        copy.wait()


def ordered(array, after):
    return lax.optimization_barrier((array,) + tuple(after))[0] if after else array


def call(
    kernel, operands, spaces, outs, scratch, flops, after=(), out_space="v", chunk=0, before=(),
    weight=LIGHT,
):
    count = len(operands)
    out_space = out_space * len(outs) if len(out_space) == 1 else out_space
    passed = [i for i, c in enumerate(out_space) if c == "c" and before]
    extra = [before[i] for i in passed]
    operands = (ordered(operands[0], after),) + tuple(operands[1:])

    def body(*refs):
        kernel(*refs[:count], *refs[count + len(extra) :])

    def spec(letter, shape):
        if letter == "c":
            return pl.BlockSpec((shape[0] // 2, shape[1]), lambda i: (chunk, 0))
        return pl.BlockSpec(memory_space={"s": pltpu.SMEM, "v": pltpu.VMEM, "a": pl.ANY}[letter])

    return pl.pallas_call(
        body,
        grid=(1,) if "c" in spaces else (),
        out_shape=[jax.ShapeDtypeStruct(s, t) for s, t in outs],
        in_specs=[spec(c, x.shape) for c, x in zip(spaces, operands)]
        + [pl.BlockSpec(memory_space=pl.ANY)] * len(extra),
        out_specs=[spec(c, s) for c, (s, _) in zip(out_space, outs)],
        scratch_shapes=scratch,
        input_output_aliases={count + i: o for i, o in enumerate(passed)},
        compiler_params=pltpu.CompilerParams(vmem_limit_bytes=VMEM_BYTES),
        cost_estimate=pl.CostEstimate(
            flops=flops * weight, bytes_accessed=(8 << 20) * weight, transcendentals=0
        ),
    )(*operands, *extra)


def attention_call(
    flags, lead, lead_spaces, weights, size, model, width, kernel, extra_outs, after=()
):
    heads = width // HD
    outs = extra_outs + [
        ((size, model), BF),
        ((size, width), BF),
        ((size, width), BF),
        ((size, width), BF),
        ((heads, size, size), BF),
        ((heads, 1, size), F32),
        ((size, width), BF),
        ((width, size), F32),
        ((size // 2, model), BF),
        ((size // 2, model), BF),
    ]
    scratch = [pltpu.VMEM((model, width), BF)] * 3 + [
        pltpu.VMEM((width, model), BF),
        pltpu.VMEM((width, size), BF),
        pltpu.VMEM((heads, size, HD), BF),
        pltpu.VMEM((width, size), BF),
        pltpu.VMEM((size, size), F32),
        pltpu.SemaphoreType.DMA((4,)),
    ]
    return call(
        kernel, (flags,) + lead + weights, "s" + lead_spaces + "a" * 8, outs, scratch,
        2 * size * width * model * 4 + 4 * heads * size * size * HD, after, weight=HEAVY,
    )


def swap(block, axis):
    return lax.ppermute(block, axis, [(0, 1), (1, 0)])


def across(block, routes):
    return lax.ppermute(
        block, ("section", "tensor"), [(a[0] * 2 + a[1], b[0] * 2 + b[1]) for a, b in routes]
    )


def batch_pairs():
    return [(i, i ^ 1) for i in range(lax.axis_size("batch"))]


def pair_swap(block):
    return lax.ppermute(block, "batch", batch_pairs())


def line_end():
    line = lax.axis_index("batch") // 2
    return (line == 0) | (line == 3)


STAGES = (
    ("in", ((0, 2), (1, 3), (6, 4), (7, 5))),
    ("middle", ((2, 4), (3, 5), (4, 2), (5, 3))),
    ("out", ((2, 0), (3, 1), (4, 6), (5, 7))),
)


def rest_of_line(mine):
    count = lax.axis_size("batch")
    if count & (count - 1):
        lines = [list(range(i, count, 2)) for i in range(2)]
        return lax.psum(mine, "batch", axis_index_groups=lines)
    step = 2
    while step < count:
        mine = mine + lax.ppermute(mine, "batch", [(i, i ^ step) for i in range(count)])
        step *= 2
    return mine


def pad_rows(rows, count):
    return jnp.concatenate([rows, jnp.zeros((count - rows.shape[0], rows.shape[1]), rows.dtype)], 0)


def shards(
    section_ends, lengths, w_query, b_query, w_key, w_value, b_value, w_out, b_out,
    norm1_gain, norm1_bias, w_inner, b_inner, w_outer, b_outer, norm2_gain, norm2_bias,
):
    section = lax.axis_index("section")
    tensor = lax.axis_index("tensor")
    first = section == 0
    held = section_ends[0]
    half, model = held.shape[1], held.shape[2]
    size = 2 * half
    width = w_query.shape[2]
    inner = w_inner.shape[2]
    heads = width // HD
    flags = jnp.concatenate(
        [
            jnp.stack([section, tensor]).astype(jnp.int32),
            lax.dynamic_slice_in_dim(lengths, section, 1, 0)[0],
            (lax.axis_index("batch") % 2).astype(jnp.int32)[None],
        ]
    )

    x_peer_a = across(held[0], [((0, 0), (0, 1)), ((0, 1), (0, 0))])
    x_peer_b = across(held[1], [((0, 0), (1, 1)), ((0, 1), (1, 0))])
    x_far = across(held[1], [((0, 0), (1, 0)), ((0, 1), (1, 1))])

    attention_own = (w_query[0], w_key[0], w_value[0], w_out[0])
    ffn_own = (w_inner[0], w_outer[0])
    vec_own = pad_rows(
        jnp.concatenate(
            [
                jnp.concatenate([b_query, b_value], axis=1),
                b_out, norm1_gain, norm1_bias, b_inner.reshape(-1, model), b_outer,
                norm2_gain, norm2_bias,
            ],
            axis=0,
        ),
        V_ROWS,
    )
    vec_far = swap(vec_own, "section")
    attention_far = tuple(swap(w, "section") for w in attention_own)
    ffn_far = tuple(swap(w, "section") for w in ffn_own)
    attention_w = attention_own + attention_far
    ffn_w = ffn_own + ffn_far
    vec_one = jnp.where(first, vec_own, vec_far)
    vec_two = jnp.where(first, vec_far, vec_own)

    def send(parts):
        return [swap(part, "tensor") for part in parts]

    def ffn_forward(layer, x, parts, vec, after=()):
        outs = ()
        sums = []
        for c, (part, got) in enumerate(zip(parts, send(parts))):
            outs = call(
                functools.partial(ffn_forward_kernel, layer),
                (flags, x, part, got, vec) + ffn_w,
                "scvvvaaaa",
                [
                    ((size, model), F32), ((size, 1), F32), ((size, model), BF),
                    ((size, inner), BF), ((size, inner), BF), ((half, model), BF),
                ],
                [
                    pltpu.VMEM((model, inner), BF), pltpu.VMEM((inner, model), BF),
                    pltpu.SemaphoreType.DMA((2,)),
                ],
                2 * size * model * inner, after, "cccccv", c, outs,
            )
            sums.append(outs[-1])
        return *outs[:-1], sums

    x_one, *heads_one, part, part2 = attention_call(
        flags, (held[0], x_far, x_peer_a, x_peer_b, vec_one), "vvvvv", attention_w,
        size, model, width, attention_first_kernel, [], ffn_far,
    )
    n1_one, i1_one, n1b_one, a_one, d_one, parts = ffn_forward(
        0, x_one, (part, part2), vec_one
    )
    later = [ordered(held[i], (n1b_one,)) for i in range(2)]
    gy_peer_a = across(later[1], [((1, 0), (1, 1)), ((1, 1), (1, 0))])
    gy_peer_b = across(later[0], [((1, 0), (0, 1)), ((1, 1), (0, 0))])
    gy_far = across(later[0], [((1, 0), (0, 0)), ((1, 1), (0, 1))])

    n2_one, i2_one, x_two, *heads_two, part, part2 = attention_call(
        flags, (n1_one, *parts, *send(parts), vec_one, vec_two), "vvvvvvv", attention_w,
        size, model, width, attention_next_kernel, [((size, model), F32), ((size, 1), F32)],
    )
    n1_two, i1_two, n1b_two, a_two, d_two, parts_two = ffn_forward(
        1, x_two, (part, part2), vec_two, (gy_peer_a, gy_peer_b, gy_far)
    )

    ffn_outs = [
        ((size, model), F32), ((size, model), BF), ((size, inner), BF), ((half, model), BF),
        ((8, model), F32),
    ]
    ffn_scratch = [
        pltpu.VMEM((model, inner), BF), pltpu.VMEM((inner, model), BF),
        pltpu.SemaphoreType.DMA((2,)),
    ]

    def attention_back(layer, g2, parts, got, n1, i1, vec, saved, after):
        q, k, v, e, r, o, ot_f = saved
        *outs, part, part2, small = call(
            functools.partial(attention_back_kernel, layer),
            (flags, g2, *parts, *got, n1, i1, vec, q, k, v, e, r, ot_f) + attention_w,
            "s" + "v" * 14 + "a" * 8,
            [
                ((size, model), F32), ((size, model), BF), ((size, 3 * width), BF),
                ((half, model), BF), ((half, model), BF), ((8, model), F32),
            ],
            [pltpu.VMEM((model, width), BF)] * 3
            + [
                pltpu.VMEM((width, model), BF),
                pltpu.VMEM((HD, size), BF),
                pltpu.VMEM((size, HD), BF),
                pltpu.VMEM((width, size), BF),
                pltpu.VMEM((heads, size, HD), BF),
                pltpu.VMEM((heads, size, HD), BF),
                pltpu.VMEM((width, size), F32),
                pltpu.SemaphoreType.DMA((4,)),
            ],
            2 * size * width * model * 4 + 8 * heads * size * size * HD,
            after, weight=HEAVY,
        )
        return *outs, [part, part2], small

    state = {}
    last = ()
    chunked = [()]

    def add(groups, arrays, shapes):
        sums = []
        for group, (rows, _) in zip(groups, shapes):
            terms = [arrays[i][row : row + rows] for i, row in group]
            sums.append(sum(terms[1:], ordered(terms[0], last)))
        return sums

    def back_last(c):
        part = parts_two[c]
        outs = call(
            functools.partial(ffn_back_last_kernel, c),
            (flags, n1_two, part, got_two[c], vec_two, held[1], gy_far, gy_peer_a, gy_peer_b,
             d_two, small_zero if c == 0 else state["small_f2"]) + ffn_w,
            "sc" + "v" * 7 + "cv" + "a" * 4,
            [((size, model), BF)] + ffn_outs,
            [pltpu.VMEM((half, model), BF)] + ffn_scratch,
            2 * size * model * inner, last, "ccccvv", c, chunked[0],
        )
        chunked[0] = outs if c == 0 else ()
        state["small_f2"] = outs[-1]
        state["y_two"], state["g2_two"], state["g2b_two"], state["gh_two"] = outs[:4]
        state.setdefault("sums_two", []).append(outs[-2])
        state.setdefault("sums_two_got", []).append(swap(outs[-2], "tensor"))
        return outs[-1]

    def back_next(c):
        outs = call(
            ffn_back_next_kernel,
            (flags, state["g1_two"], state["p4_two"][c], state["p4_two_got"][c], n2_one, i2_one,
             vec_one, d_one, small_zero if c == 0 else state["small_f1"]) + ffn_w,
            "scvvccvcv" + "a" * 4,
            ffn_outs,
            ffn_scratch,
            2 * size * model * inner, last, "cccvv", c, chunked[0],
        )
        chunked[0] = outs if c == 0 else ()
        state["small_f1"] = outs[-1]
        state["g2_one"], state["g2b_one"], state["gh_one"] = outs[:3]
        state.setdefault("sums_one", []).append(outs[-2])
        state.setdefault("sums_one_got", []).append(swap(outs[-2], "tensor"))
        return outs[-1]

    def back_attention(name, layer, *rest):
        grad, rows, gqkv, parts, small = attention_back(
            layer, state["g2_" + name], state["sums_" + name], state["sums_" + name + "_got"],
            *rest, last,
        )
        state["g1_" + name], state["g1b_" + name], state["gqkv_" + name] = grad, rows, gqkv
        state["p4_" + name], state["small_a_" + name] = parts, small
        if name == "two":
            state["p4_two_got"] = send(parts)
        return small

    def put(base, ours, theirs):
        state[base] = ours
        state[base + "_got"] = swap(theirs, "section")

    def ffn_products(base, a, gb, gh, n1b, small):
        rows = 2 * (model + PAD)
        ours, theirs = call(
            ffn_product_kernel, (flags, a, gb, gh, n1b, small), "svvvvv",
            [((rows, model), BF)] * 2,
            [pltpu.VMEM((2, rows, model), BF), pltpu.SemaphoreType.DMA((2,))],
            4 * size * model * inner, last, "a",
        )
        put(base, ours, theirs)
        return ours

    def attention_products(base, gqkv, x, o, gb, small):
        rows = 2 * (model + PAD)
        ours, theirs = call(
            attention_product_kernel, (flags, x, gqkv, o, gb, small), "svvvvv",
            [((rows, width), BF)] * 2,
            [pltpu.VMEM((2, rows, width), BF), pltpu.SemaphoreType.DMA((2,))],
            8 * size * model * width, last, "a",
        )
        put(base, ours, theirs)
        return ours

    units = {}
    for base in ("f1", "f2"):
        row = 0
        for name, rows in zip("ab", ffn_rows(model // 2)[0]):
            units[base + name] = (base, row, rows, model)
            row += 2 * rows
    for base in ("a1", "a2"):
        units[base] = (base, 0, model + PAD, width)

    def give(base):
        names = [n for n in units if units[n][0] == base]
        outs = add(
            [[(0, units[n][1] + units[n][2]), (1, units[n][1] + units[n][2])] for n in names],
            (state[base], state[base + "_got"]),
            [units[n][2:] for n in names],
        )
        for n, out in zip(names, outs):
            state[n + "x"] = pair_swap(out)
        return outs[0]

    def step(name, stage):
        base, row, rows, columns = units[name]
        shape = (rows, columns)
        if stage == 0:
            (mine,) = add(
                [[(0, row), (1, row), (2, 0)]],
                (state[base], state[base + "_got"], state[name + "x"]), [shape],
            )
        elif lax.axis_size("batch") != 8:
            mine = rest_of_line(state[name]) if stage == 1 else state[name]
        elif stage < 3:
            (mine,) = add([[(0, 0), (1, 0)]], (state[name], state[name + "s"]), [shape])
        else:
            mine = jnp.where(at_end, state[name + "s"], ordered(state[name], last))
        state[name] = mine
        if stage < 3:
            state[name + "s"] = lax.ppermute(mine, "batch", STAGES[stage][1]) if lax.axis_size("batch") == 8 else None
        else:
            state[name] = (mine, pair_swap(mine))
        return mine

    def share(name):
        both = state[name]
        route = (1, 0) if name[1] == "1" else (0, 1)
        first_half = ordered(both[0], last)
        state[name] = both + tuple(
            lax.ppermute(part, "section", [route]) for part in (first_half, ordered(both[1], last))
        )
        return first_half

    def finish_ffn():
        sums = sum((state[n] for n in sorted(units) if n[0] == "f"), ())
        outs = call(
            ffn_finish_kernel, (flags,) + sums, "s" + "a" * len(sums),
            [((inner, model), F32), ((model, inner), F32)] + [((1, model), F32)] * 3
            + [((1, inner), F32)],
            [
                pltpu.VMEM((4, model + PAD, model), BF), pltpu.VMEM((inner, model), F32),
                pltpu.VMEM((model, inner), F32), pltpu.SemaphoreType.DMA((12,)),
                pltpu.SemaphoreType.DMA((8,)),
            ],
            size * model, last, "aavvvv",
        )
        state["ffn"] = outs
        return outs[-1]

    def finish_attention():
        outs = call(
            attention_finish_kernel, (flags,) + state["a1"] + state["a2"], "s" + "a" * 8,
            [((model, width), F32)] * 3 + [((width, model), F32)] + [((1, model), F32)] * 3
            + [((1, width), F32)] * 2,
            [
                pltpu.VMEM((4, model + PAD, width), BF), pltpu.VMEM((3, model, width), F32),
                pltpu.VMEM((width, model), F32), pltpu.SemaphoreType.DMA((4,)),
                pltpu.SemaphoreType.DMA((4,)),
            ],
            size * model, last, "aaaavvvvv",
        )
        state["attention"] = outs
        return outs[-1]

    at_end = line_end()
    small_zero = jnp.zeros((8, model), F32)
    got_two = send(parts_two)
    tasks = {
        "KC2a": lambda: back_last(0),
        "KC2b": lambda: back_last(1),
        "KWF2": lambda: ffn_products(
            "f2", a_two, state["g2b_two"], state["gh_two"], n1b_two, state["small_f2"]
        ),
        "KD2": lambda: back_attention("two", 1, n1_two, i1_two, vec_two, heads_two),
        "KWA2": lambda: attention_products(
            "a2", state["gqkv_two"], x_two, heads_two[5], state["g1b_two"], state["small_a_two"]
        ),
        "KC1a": lambda: back_next(0),
        "KC1b": lambda: back_next(1),
        "KWF1": lambda: ffn_products(
            "f1", a_one, state["g2b_one"], state["gh_one"], n1b_one, state["small_f1"]
        ),
        "KD1": lambda: back_attention("one", 0, n1_one, i1_one, vec_one, heads_one),
        "KWA1": lambda: attention_products(
            "a1", state["gqkv_one"], x_one, heads_one[5], state["g1b_one"], state["small_a_one"]
        ),
        "finF": finish_ffn,
        "finA": finish_attention,
    }
    for base in ("f1", "f2", "a1", "a2"):
        tasks[base + "gn"] = functools.partial(give, base)
    for name in units:
        for stage in range(4):
            tasks[name + "a" + str(stage + 1)] = functools.partial(step, name, stage)
        tasks[name + "g"] = functools.partial(share, name)
    for name in ORDER:
        last = (tasks[name](),)

    part_one, part_one2 = state["p4_one"]
    part_mine = jnp.where(tensor == 0, part_one, part_one2)
    part_theirs = jnp.where(tensor == 0, part_one2, part_one)
    total = part_mine.astype(F32) + swap(part_theirs, "tensor").astype(F32)
    gx = (lax.dynamic_slice_in_dim(state["g1_one"], tensor * half, half, 0) + total).astype(BF)
    y_mine = lax.dynamic_slice_in_dim(state["y_two"], tensor * half, half, 0)
    y_far = lax.ppermute(y_mine, "section", [(0, 1)])
    gx_far = lax.ppermute(gx, "section", [(1, 0)])
    section_results = jnp.stack(
        [jnp.where(first, gx, y_far), jnp.where(first, gx_far, y_mine)], axis=0
    )[None]
    grad_outer, grad_inner, bias_outer, gain_two, bias_two, bias_inner = state["ffn"]
    grad_q, grad_k, grad_v, grad_out, bias_out, gain_one, bias_one, bias_q, bias_v = state["attention"]
    return (
        section_results,
        grad_q[None],
        bias_q,
        grad_k[None],
        grad_v[None],
        bias_v,
        grad_out[None],
        bias_out,
        gain_one,
        bias_one,
        grad_inner[None],
        bias_inner,
        grad_outer[None],
        bias_outer,
        gain_two,
        bias_two,
    )


def solution(mesh):
    in_specs = (
        P("section", "batch", "tensor", None),
        P("batch", None),
        P("section", None, "tensor"),
        P("section", "tensor"),
        P("section", None, "tensor"),
        P("section", None, "tensor"),
        P("section", "tensor"),
        P("section", "tensor", None),
        P("section", None),
        P("section", None),
        P("section", None),
        P("section", None, "tensor"),
        P("section", "tensor"),
        P("section", "tensor", None),
        P("section", None),
        P("section", None),
        P("section", None),
    )
    out_specs = (
        P("section", "batch", "tensor", None),
        P("section", None, "tensor"),
        P("section", "tensor"),
        P("section", None, "tensor"),
        P("section", None, "tensor"),
        P("section", "tensor"),
        P("section", "tensor", None),
        P("section", None),
        P("section", None),
        P("section", None),
        P("section", None, "tensor"),
        P("section", "tensor"),
        P("section", "tensor", None),
        P("section", None),
        P("section", None),
        P("section", None),
    )
    return jax.shard_map(shards, mesh=mesh, in_specs=in_specs, out_specs=out_specs, check_vma=False)
```

```python
import functools
import math

import jax
import jax.numpy as jnp
from jax import lax
from jax.experimental import pallas as pl
from jax.experimental.pallas import tpu as pltpu
from jax.sharding import PartitionSpec as P

HD = 64
epsilon = 1e-06
root_half = 0.7071067811865476
inverse_root = 0.3989422804014327
BF = jnp.bfloat16
F32 = jnp.float32
RB = 128
VMEM_BYTES = 56 * 1024 * 1024

V_BQV, V_BO, V_G1, V_B1, V_BI, V_BU, V_G2, V_B2 = 0, 1, 2, 3, 4, 6, 7, 8
V_ROWS = 16


def dot(a, b):
    return lax.dot_general(a, b, (((1,), (0,)), ((), ())), preferred_element_type=F32)


def dot_nt(a, b):
    return lax.dot_general(a, b, (((1,), (1,)), ((), ())), preferred_element_type=F32)


def dot_tn(a, b):
    return lax.dot_general(a, b, (((0,), (0,)), ((), ())), preferred_element_type=F32)


def start_fetch(use_own, own, other, held, sems):
    @pl.when(use_own)
    def _():
        for i in range(len(own)):
            pltpu.make_async_copy(own[i], held[i], sems.at[i]).start()

    @pl.when(jnp.logical_not(use_own))
    def _():
        for i in range(len(own)):
            pltpu.make_async_copy(other[i], held[i], sems.at[i]).start()


def wait_fetch(i, own, held, sems):
    pltpu.make_async_copy(own[i], held[i], sems.at[i]).wait()


def row_blocks(total, body):
    def step(i, carry):
        body(pl.ds(pl.multiple_of(i * RB, RB), RB))
        return carry

    lax.fori_loop(0, total // RB, step, 0)


def loop(count, body, unroll=1):
    def step(i, carry):
        for j in range(unroll):
            body(i * unroll + j)
        return carry

    lax.fori_loop(0, count // unroll, step, 0)


def part_of(i, step):
    return pl.ds(i * step if isinstance(i, int) else pl.multiple_of(i * step, step), step)


def norm_rows(residue):
    center = residue - jnp.mean(residue, axis=-1, keepdims=True)
    inverse = lax.rsqrt(jnp.mean(center * center, axis=-1, keepdims=True) + epsilon)
    return center * inverse, inverse


def norm_back_rows(upstream, normal, inverse, gain):
    scaled = upstream * gain
    centred = scaled - jnp.mean(scaled, axis=-1, keepdims=True)
    return (centred - normal * jnp.mean(scaled * normal, axis=-1, keepdims=True)) * inverse


def column_sum(rows):
    return jnp.sum(rows, axis=0, keepdims=True)


def segment_bias(flags, bias):
    size = bias.shape[0]
    ends = [flags[2]]
    for i in range(3, 5):
        ends.append(ends[-1] + flags[i])
    row = lax.broadcasted_iota(jnp.int32, (1, size), 1)
    row_seg = sum((row >= e).astype(jnp.int32) for e in ends)

    def body(rows):
        col = lax.broadcasted_iota(jnp.int32, (RB, 1), 0) + rows.start
        col_seg = sum((col >= e).astype(jnp.int32) for e in ends)
        bias[rows, :] = jnp.where(col_seg == row_seg, 0.0, -1e30).astype(F32)

    row_blocks(size, body)


def attention_forward(flags, x, vec, weights, wait, outs, scratch):
    wq, wk, wv, wo = weights
    q_out, k_out, v_out, e_out, r_out, o_out, ot_out, *p_outs = outs
    qt_s, kh_s, vt_s, bias = scratch
    size = x.shape[0]
    width = wq.shape[1]
    heads = width // HD
    segment_bias(flags, bias)
    wait(0)
    wait(1)
    wait(2)

    def project(i):
        rows = part_of(i, 256)
        xb = x[rows, :]
        q = (dot(xb, wq[...]) + vec[V_BQV : V_BQV + 1, :width]).astype(BF).astype(F32) * (
            1.0 / math.sqrt(HD)
        )
        q_out[rows, :] = q.astype(BF)
        qt_s[:, rows] = q.T.astype(BF)
        k = dot(xb, wk[...]).astype(BF)
        k_out[rows, :] = k
        for h in range(heads):
            kh_s[h, rows, :] = k[:, h * HD : (h + 1) * HD]
        v = dot(xb, wv[...]) + vec[V_BQV : V_BQV + 1, width : 2 * width]
        v_out[rows, :] = v.astype(BF)
        vt_s[:, rows] = v.T.astype(BF)

    loop(size // 256, project)

    def attend(h):
        hs = part_of(h, HD)
        for j in range(size // 256):
            cols = pl.ds(j * 256, 256)
            scores = dot(kh_s[h], qt_s[hs, cols]) + bias[:, cols]
            highest = jnp.max(scores, axis=0, keepdims=True)
            raised = jnp.exp(scores - highest)
            inverse = 1.0 / jnp.sum(raised, axis=0, keepdims=True)
            raised = raised.astype(BF)
            e_out[h, :, cols] = raised
            r_out[h, :, cols] = inverse
            ot_out[hs, cols] = dot(vt_s[hs, :], raised) * inverse

    loop(heads, attend, 3)
    wait(3)

    for i, p_out in enumerate(p_outs):
        rows = part_of(i, size // 2)
        context = ot_out[:, rows].T.astype(BF)
        o_out[rows, :] = context
        p_out[...] = dot(context, wo[...]).astype(BF)


def attention_first_kernel(
    flags, own, far, peer_a, peer_b, vec,
    wq, wk, wv, wo, wq2, wk2, wv2, wo2,
    x_out, q_out, k_out, v_out, e_out, r_out, o_out, ot_out, p_out, p_out2,
    wq_s, wk_s, wv_s, wo_s, qt_s, kh_s, vt_s, bias, sems,
):
    first = flags[0] == 0
    held = (wq_s, wk_s, wv_s, wo_s)
    source = (wq, wk, wv, wo)
    start_fetch(first, source, (wq2, wk2, wv2, wo2), held, sems)
    half = own.shape[0]
    mine = pl.multiple_of(flags[1] * half, half)
    theirs = pl.multiple_of((1 - flags[1]) * half, half)
    x_out[pl.ds(mine, half), :] = jnp.where(first, own[...], far[...])
    x_out[pl.ds(theirs, half), :] = jnp.where(first, peer_a[...], peer_b[...])
    attention_forward(
        flags, x_out, vec, held, lambda i: wait_fetch(i, source, held, sems),
        (q_out, k_out, v_out, e_out, r_out, o_out, ot_out, p_out, p_out2), (qt_s, kh_s, vt_s, bias),
    )


def attention_next_kernel(
    flags, normal_one, part_a, part_a2, part_b, part_b2, vec_prev, vec,
    wq, wk, wv, wo, wq2, wk2, wv2, wo2,
    n2_out, i2_out, x_out, q_out, k_out, v_out, e_out, r_out, o_out, ot_out, p_out, p_out2,
    wq_s, wk_s, wv_s, wo_s, qt_s, kh_s, vt_s, bias, sems,
):
    held = (wq_s, wk_s, wv_s, wo_s)
    source = (wq, wk, wv, wo)
    start_fetch(flags[0] == 1, source, (wq2, wk2, wv2, wo2), held, sems)

    half = part_a.shape[0]
    for c, (one, two) in enumerate(((part_a, part_b), (part_a2, part_b2))):

        def body(rows, c=c, one=one, two=two):
            place = pl.ds(rows.start + c * half, RB)
            normal, inverse, output = second_norm(normal_one[place, :], one, two, vec_prev, rows)
            n2_out[place, :] = normal
            i2_out[place, :] = inverse
            x_out[place, :] = output.astype(BF)

        row_blocks(half, body)
    attention_forward(
        flags, x_out, vec, held, lambda i: wait_fetch(i, source, held, sems),
        (q_out, k_out, v_out, e_out, r_out, o_out, ot_out, p_out, p_out2), (qt_s, kh_s, vt_s, bias),
    )


def second_norm(normal_one, part_a, part_b, vec, rows):
    normed = normal_one * vec[V_G1 : V_G1 + 1, :] + vec[V_B1 : V_B1 + 1, :]
    total = part_a[rows, :].astype(F32) + part_b[rows, :].astype(F32)
    normal, inverse = norm_rows(total + vec[V_BU : V_BU + 1, :] + normed)
    return normal, inverse, normal * vec[V_G2 : V_G2 + 1, :] + vec[V_B2 : V_B2 + 1, :]


def ffn_forward_kernel(
    layer, flags, x, part_a, part_b, vec, wi, wu, wi2, wu2,
    n1_out, i1_out, n1b_out, a_out, d_out, p_out,
    wi_s, wu_s, sems,
):
    held = (wi_s, wu_s)
    source = (wi, wu)
    start_fetch(flags[0] == layer, source, (wi2, wu2), held, sems)
    size = x.shape[0]
    width = wi_s.shape[1]
    model = wi_s.shape[0]

    def first(rows):
        total = part_a[rows, :].astype(F32) + part_b[rows, :].astype(F32)
        normal, inverse = norm_rows(total + vec[V_BO : V_BO + 1, :] + x[rows, :].astype(F32))
        n1_out[rows, :] = normal
        i1_out[rows, :] = inverse
        n1b_out[rows, :] = (normal * vec[V_G1 : V_G1 + 1, :] + vec[V_B1 : V_B1 + 1, :]).astype(BF)

    row_blocks(size, first)
    wait_fetch(0, source, held, sems)
    block = 256

    def inner(rows):
        rows_in = n1b_out[rows, :]
        for j in range(width // block):
            cols = slice(j * block, (j + 1) * block)
            at = j * block
            bias = vec[V_BI + at // model : V_BI + at // model + 1, at % model : at % model + block]
            hidden = dot(rows_in, wi_s[:, cols]) + bias
            spread = 0.5 + 0.5 * lax.erf(hidden * root_half)
            a_out[rows, cols] = (hidden * spread).astype(BF)
            d_out[rows, cols] = (
                spread + hidden * jnp.exp(-0.5 * hidden * hidden) * inverse_root
            ).astype(BF)

    row_blocks(size, inner)
    wait_fetch(1, source, held, sems)

    def outer(i):
        rows = part_of(i, 256)
        p_out[rows, :] = dot(a_out[rows, :], wu_s[...]).astype(BF)

    loop(size // 256, outer)


def ffn_backward(g2, d, w, outs, wait, small):
    wi_s, wu_s = w
    gh_out, p_out = outs
    size = g2.shape[0]
    model, width = wi_s.shape
    wait(1)
    block = 384

    def hidden(i):
        rows = part_of(i, 256)
        gb = g2[rows, :]
        for j in range(width // block):
            cols = slice(j * block, (j + 1) * block)
            gh = (dot_nt(gb, wu_s[cols, :]) * d[rows, cols].astype(F32)).astype(BF)
            gh_out[rows, cols] = gh
            at = j * block
            small[3 + at // model : 4 + at // model, at % model : at % model + block] += column_sum(
                gh.astype(F32)
            )

    loop(size // 256, hidden)
    wait(0)

    def inner(i):
        rows = part_of(i, 256)
        p_out[rows, :] = dot_nt(gh_out[rows, :], wi_s[...]).astype(BF)

    loop(size // 256, inner)


def ffn_back_last_kernel(
    chunk, flags, normal_one, part_a, part_b, vec, own, far, peer_a, peer_b, d, small_in,
    wi, wu, wi2, wu2,
    y_out, g_out, gb_out, gh_out, p_out, small,
    gy_s, wi_s, wu_s, sems,
):
    held = (wi_s, wu_s)
    source = (wi, wu)
    second = flags[0] == 1
    start_fetch(second, source, (wi2, wu2), held, sems)
    here = flags[1] == chunk
    gy_s[...] = jnp.where(
        here,
        jnp.where(second, own[...], far[...]),
        jnp.where(second, peer_a[...], peer_b[...]),
    )
    small[...] = small_in[...]

    def body(rows):
        normal, inverse, output = second_norm(normal_one[rows, :], part_a, part_b, vec, rows)
        y_out[rows, :] = output.astype(BF)
        ffn_back_rows(gy_s[rows, :].astype(F32), normal, inverse, vec, rows, g_out, gb_out, small)

    row_blocks(y_out.shape[0], body)
    ffn_backward(gb_out, d, held, (gh_out, p_out), lambda i: wait_fetch(i, source, held, sems), small)


def ffn_back_rows(upstream, normal, inverse, vec, rows, g_out, gb_out, small):
    grad = norm_back_rows(upstream, normal, inverse, vec[V_G2 : V_G2 + 1, :])
    g_out[rows, :] = grad
    gb_out[rows, :] = grad.astype(BF)
    small[0:1, :] += column_sum(grad)
    small[1:2, :] += column_sum(upstream * normal)
    small[2:3, :] += column_sum(upstream)


def ffn_back_next_kernel(
    flags, g1, part_a, part_b, normal_two, inverse_two, vec, d, small_in, wi, wu, wi2, wu2,
    g_out, gb_out, gh_out, p_out, small,
    wi_s, wu_s, sems,
):
    held = (wi_s, wu_s)
    source = (wi, wu)
    start_fetch(flags[0] == 0, source, (wi2, wu2), held, sems)
    small[...] = small_in[...]

    def body(rows):
        total = part_a[rows, :].astype(F32) + part_b[rows, :].astype(F32)
        upstream = (g1[rows, :] + total).astype(BF).astype(F32)
        ffn_back_rows(
            upstream, normal_two[rows, :], inverse_two[rows, :], vec, rows, g_out, gb_out, small
        )

    row_blocks(g1.shape[0], body)
    ffn_backward(gb_out, d, held, (gh_out, p_out), lambda i: wait_fetch(i, source, held, sems), small)


def attention_back_kernel(
    layer, flags, g2, part_a, part_a2, part_b, part_b2, normal_one, inverse_one, vec,
    q, k, v, e, r, ot_f,
    wq, wk, wv, wo, wq2, wk2, wv2, wo2,
    g_out, gb_out, gqkv_out, p_out, p_out2, small,
    wq_s, wk_s, wv_s, wo_s, got_s, go_s, kt_s, vh_s, qh_s, gqt_s, sems,
):
    held = (wq_s, wk_s, wv_s, wo_s)
    source = (wq, wk, wv, wo)
    start_fetch(flags[0] == layer, source, (wq2, wk2, wv2, wo2), held, sems)
    size, model = g2.shape
    width = q.shape[1]
    heads = width // HD
    small[...] = jnp.zeros_like(small)

    half = size // 2
    for c, (one, two) in enumerate(((part_a, part_b), (part_a2, part_b2))):

        def body(rows, c=c, one=one, two=two):
            place = pl.ds(rows.start + c * half, RB)
            upstream = g2[place, :] + (one[rows, :].astype(F32) + two[rows, :].astype(F32))
            normal = normal_one[place, :]
            grad = norm_back_rows(upstream, normal, inverse_one[place, :], vec[V_G1 : V_G1 + 1, :])
            g_out[place, :] = grad
            gb_out[place, :] = grad.astype(BF)
            small[0:1, :] += column_sum(grad)
            small[1:2, :] += column_sum(upstream * normal)
            small[2:3, :] += column_sum(upstream)

        row_blocks(half, body)

    def split(i):
        rows = part_of(i, 256)
        kt_s[:, rows] = k[rows, :].astype(F32).T.astype(BF)
        for h in range(heads):
            hs = slice(h * HD, (h + 1) * HD)
            vh_s[h, rows, :] = v[rows, hs]
            qh_s[h, rows, :] = q[rows, hs]

    loop(size // 256, split)
    wait_fetch(3, source, held, sems)

    def context(i):
        rows = part_of(i, 256)
        gqt_s[:, rows] = dot_nt(gb_out[rows, :], wo_s[...]).T

    loop(size // 256, context)

    def attend(h):
        hs = part_of(h, HD)
        scaled = (gqt_s[hs, :] * r[h]).astype(BF)
        got_s[...] = scaled
        scaled = scaled.astype(F32)
        delta = column_sum(scaled * ot_f[hs, :])
        go_s[...] = scaled.T.astype(BF)
        grad_v = jnp.zeros((size, HD), F32)
        grad_k = jnp.zeros((size, HD), F32)
        for j in range(size // 256):
            cols = pl.ds(j * 256, 256)
            raised = e[h, :, cols]
            grad_p = dot(vh_s[h], got_s[:, cols]) - delta[:, j * 256 : (j + 1) * 256]
            grad_s = (raised.astype(F32) * grad_p).astype(BF)
            grad_v = grad_v + dot(raised, go_s[cols, :])
            grad_k = grad_k + dot(grad_s, qh_s[h, cols, :])
            gqt_s[hs, cols] = dot(kt_s[hs, :], grad_s) * (1.0 / math.sqrt(HD))
        vh_s[h] = grad_v.astype(BF)
        qh_s[h] = grad_k.astype(BF)

    loop(heads, attend, 3)
    for i in range(3):
        wait_fetch(i, source, held, sems)

    for i, p in enumerate((p_out, p_out2)):
        rows = pl.ds(i * half, half)
        gq = gqt_s[:, rows].T.astype(BF)
        gk = jnp.concatenate([qh_s[h, rows, :] for h in range(heads)], axis=1)
        gv = jnp.concatenate([vh_s[h, rows, :] for h in range(heads)], axis=1)
        gqkv_out[rows, :width] = gq
        gqkv_out[rows, width : 2 * width] = gk
        gqkv_out[rows, 2 * width :] = gv
        small[3:4, :width] += column_sum(gq.astype(F32))
        small[3:4, width:] += column_sum(gv.astype(F32))
        p[...] = (
            dot_nt(gq, wq_s[...]) + dot_nt(gk, wk_s[...]) + dot_nt(gv, wv_s[...])
        ).astype(BF)


HEAVY, LIGHT = 20, 0
PAD = 16
ORDER = (
    "KC2a", "KC2b", "KWF2", "KD2", "KWA2", "a2gn", "f2gn", "KC1a", "f2ba1", "KC1b", "KWF1",
    "f2aa1", "KD1", "KWA1", "f2aa2", "f1gn", "a2a1", "f2ba2", "a1gn", "a2a2", "f2aa3", "f1aa1",
    "f1ba1", "f2ba3", "f2aa4", "f1aa2", "a2a3", "a1a1", "f2ba4", "f1aa3", "f1ba2", "a2a4", "a1a2",
    "f2bg", "f1ba3", "f1aa4", "a1a3", "a2g", "f1ag", "f1ba4", "f2ag", "a1a4", "f1bg", "finF",
    "a1g", "finA",
)


def send_both(held, outs, sems):
    copies = [pltpu.make_async_copy(held.at[i], outs[i], sems.at[i]) for i in range(2)]
    for copy in copies:
        copy.start()
    for copy in copies:
        copy.wait()


def ffn_rows(block):
    return (block + PAD, block), lambda i, half: i * 2 * (block + PAD) + half * (block + PAD * (1 - i))


def ffn_product_kernel(flags, a, gb, gh, n1b, small, ours, theirs, held, sems):
    model = gb.shape[1]
    block = model // 2
    extra = jnp.concatenate([small[...], jnp.zeros((PAD - 8, model), F32)], axis=0).astype(BF)
    sizes, start = ffn_rows(block)
    for i in range(2):

        def products(j, i=i):
            here = pl.ds(pl.multiple_of(start(i, flags[6] ^ j), 16), block)
            held[flags[0], here, :] = dot_tn(a[:, part_of(2 * j + i, block)], gb[...]).astype(BF)
            held[1 - flags[0], here, :] = dot_tn(
                n1b[:, i * block : (i + 1) * block], gh[:, part_of(j, model)]
            ).astype(BF)

        loop(2, products)
    for i in range(2):
        for half in range(2):
            at = (half + 1) * sizes[0]
            held[i, at - PAD : at, :] = extra
    send_both(held, (ours, theirs), sems)


def attention_product_kernel(flags, x, gqkv, o, gb, small, ours, theirs, held, sems):
    model = gb.shape[1]
    width = o.shape[1]
    rows = model + PAD

    def products(i):
        here = pl.ds(pl.multiple_of((flags[6] ^ (i % 2)) * rows, 16), model)
        held[flags[0] ^ (i // 2), here, :] = dot_tn(x[...], gqkv[:, part_of(i, width)]).astype(BF)

    loop(3, products)
    base = pl.multiple_of((flags[6] ^ 1) * rows, 16)
    for i in range(2):
        held[1 - flags[0], pl.ds(base + i * width, width), :] = dot_tn(
            o[...], gb[:, i * width : (i + 1) * width]
        ).astype(BF)
    extra = jnp.concatenate([small[:, :width], small[:, width:]], axis=0).astype(BF)
    for i in range(2):
        for half in range(2):
            held[i, half * rows + model : (half + 1) * rows, :] = extra
    send_both(held, (ours, theirs), sems)


def fetch_sums(flags, layers, held, sems):
    for layer in range(2):

        @pl.when(flags[0] == layer)
        def _(layer=layer):
            for u, (sums, row, rows, at) in enumerate(layers[layer]):
                for far in range(2):
                    for beside in range(2):
                        slot = 2 * (flags[0] ^ far) + (flags[6] ^ beside)
                        pltpu.make_async_copy(
                            sums[2 * far + beside].at[pl.ds(row, rows), :],
                            held.at[slot, pl.ds(at, rows), :],
                            sems.at[4 * u + slot],
                        ).start()

    def wait(u, slot):
        sums, row, rows, at = layers[0][u]
        pltpu.make_async_copy(
            sums[0].at[pl.ds(row, rows), :], held.at[slot, pl.ds(at, rows), :],
            sems.at[4 * u + slot],
        ).wait()

    return wait


def ffn_finish_kernel(flags, *refs):
    sums = refs[:16]
    outer, inside, bias_outer, gain, bias, bias_inner = refs[16:22]
    held, outer_s, inside_s, sems, out_sems = refs[22:]
    model = outer.shape[1]
    block = model // 2
    layers = [
        [(mine[:4], 0, block, 0), (mine[4:], 0, block, block), (mine[:4], block, PAD, 2 * block)]
        for mine in (sums[:8], sums[8:])
    ]
    wait = fetch_sums(flags, layers, held, sems)
    copies = []
    for u in range(2):
        rows = slice(u * block, (u + 1) * block)
        for j in range(2):
            at = pl.ds(j * model + u * block, block)
            wait(u, j)
            outer_s[at, :] = held[j, rows, :].astype(F32)
            copies.append((outer_s.at[at, :], outer.at[at, :]))
            columns = pl.ds(j * model, model)
            wait(u, 2 + j)
            inside_s[rows, columns] = held[2 + j, rows, :].astype(F32)
            place = pl.ds(u * block, block)
            copies.append((inside_s.at[place, columns], inside.at[place, columns]))
            for i in (len(copies) - 2, len(copies) - 1):
                pltpu.make_async_copy(*copies[i], out_sems.at[i]).start()
    for slot in range(4):
        wait(2, slot)
    small = held[0, model : model + PAD, :].astype(F32)
    for i, out in enumerate((bias_outer, gain, bias)):
        out[...] = small[i : i + 1, :]
    for i in range(bias_inner.shape[1] // model):
        bias_inner[:, i * model : (i + 1) * model] = small[3 + i : 4 + i, :]
    for i, copy in enumerate(copies):
        pltpu.make_async_copy(*copy, out_sems.at[i]).wait()


def attention_finish_kernel(flags, *refs):
    sums, (q, k, v, out, bias_out, gain, bias, bias_q, bias_v) = refs[:8], refs[8:17]
    held, sums_s, out_s, sems, out_sems = refs[17:]
    model, width = q.shape
    rows = model + PAD
    wait = fetch_sums(flags, [[(sums[:4], 0, rows, 0)], [(sums[4:], 0, rows, 0)]], held, sems)
    copies = []
    for slot, target in enumerate((q, k, v, out)):
        wait(0, slot)
        if slot < 3:
            source = sums_s.at[slot]
            source[...] = held[slot, :model, :].astype(F32)
        else:
            source = out_s
            for i in range(2):
                source[:, i * width : (i + 1) * width] = held[
                    slot, i * width : (i + 1) * width, :
                ].astype(F32)
        copies.append(pltpu.make_async_copy(source, target, out_sems.at[slot]))
        copies[-1].start()
    left = held[0, model : model + PAD, :].astype(F32)
    for i, row in enumerate((bias_out, gain, bias)):
        row[:, :width] = left[i : i + 1, :]
        row[:, width:] = left[8 + i : 9 + i, :]
    bias_q[...] = left[3:4, :]
    bias_v[...] = left[11:12, :]
    for copy in copies:
        copy.wait()


def ordered(array, after):
    return lax.optimization_barrier((array,) + tuple(after))[0] if after else array


def call(
    kernel, operands, spaces, outs, scratch, flops, after=(), out_space="v", chunk=0, before=(),
    weight=LIGHT,
):
    count = len(operands)
    out_space = out_space * len(outs) if len(out_space) == 1 else out_space
    passed = [i for i, c in enumerate(out_space) if c == "c" and before]
    extra = [before[i] for i in passed]
    operands = (ordered(operands[0], after),) + tuple(operands[1:])

    def body(*refs):
        kernel(*refs[:count], *refs[count + len(extra) :])

    def spec(letter, shape):
        if letter == "c":
            return pl.BlockSpec((shape[0] // 2, shape[1]), lambda i: (chunk, 0))
        return pl.BlockSpec(memory_space={"s": pltpu.SMEM, "v": pltpu.VMEM, "a": pl.ANY}[letter])

    return pl.pallas_call(
        body,
        grid=(1,) if "c" in spaces else (),
        out_shape=[jax.ShapeDtypeStruct(s, t) for s, t in outs],
        in_specs=[spec(c, x.shape) for c, x in zip(spaces, operands)]
        + [pl.BlockSpec(memory_space=pl.ANY)] * len(extra),
        out_specs=[spec(c, s) for c, (s, _) in zip(out_space, outs)],
        scratch_shapes=scratch,
        input_output_aliases={count + i: o for i, o in enumerate(passed)},
        compiler_params=pltpu.CompilerParams(vmem_limit_bytes=VMEM_BYTES),
        cost_estimate=pl.CostEstimate(
            flops=flops * weight, bytes_accessed=(8 << 20) * weight, transcendentals=0
        ),
    )(*operands, *extra)


def attention_call(
    flags, lead, lead_spaces, weights, size, model, width, kernel, extra_outs, after=()
):
    heads = width // HD
    outs = extra_outs + [
        ((size, model), BF),
        ((size, width), BF),
        ((size, width), BF),
        ((size, width), BF),
        ((heads, size, size), BF),
        ((heads, 1, size), F32),
        ((size, width), BF),
        ((width, size), F32),
        ((size // 2, model), BF),
        ((size // 2, model), BF),
    ]
    scratch = [pltpu.VMEM((model, width), BF)] * 3 + [
        pltpu.VMEM((width, model), BF),
        pltpu.VMEM((width, size), BF),
        pltpu.VMEM((heads, size, HD), BF),
        pltpu.VMEM((width, size), BF),
        pltpu.VMEM((size, size), F32),
        pltpu.SemaphoreType.DMA((4,)),
    ]
    return call(
        kernel, (flags,) + lead + weights, "s" + lead_spaces + "a" * 8, outs, scratch,
        2 * size * width * model * 4 + 4 * heads * size * size * HD, after, weight=HEAVY,
    )


def swap(block, axis):
    return lax.ppermute(block, axis, [(0, 1), (1, 0)])


def across(block, routes):
    return lax.ppermute(
        block, ("section", "tensor"), [(a[0] * 2 + a[1], b[0] * 2 + b[1]) for a, b in routes]
    )


def batch_pairs():
    return [(i, i ^ 1) for i in range(lax.axis_size("batch"))]


def pair_swap(block):
    return lax.ppermute(block, "batch", batch_pairs())


def line_end():
    line = lax.axis_index("batch") // 2
    return (line == 0) | (line == 3)


STAGES = (
    ("in", ((0, 2), (1, 3), (6, 4), (7, 5))),
    ("middle", ((2, 4), (3, 5), (4, 2), (5, 3))),
    ("out", ((2, 0), (3, 1), (4, 6), (5, 7))),
)


def rest_of_line(mine):
    count = lax.axis_size("batch")
    if count & (count - 1):
        lines = [list(range(i, count, 2)) for i in range(2)]
        return lax.psum(mine, "batch", axis_index_groups=lines)
    step = 2
    while step < count:
        mine = mine + lax.ppermute(mine, "batch", [(i, i ^ step) for i in range(count)])
        step *= 2
    return mine


def pad_rows(rows, count):
    return jnp.concatenate([rows, jnp.zeros((count - rows.shape[0], rows.shape[1]), rows.dtype)], 0)


def shards(
    section_ends, lengths, w_query, b_query, w_key, w_value, b_value, w_out, b_out,
    norm1_gain, norm1_bias, w_inner, b_inner, w_outer, b_outer, norm2_gain, norm2_bias,
):
    section = lax.axis_index("section")
    tensor = lax.axis_index("tensor")
    first = section == 0
    held = section_ends[0]
    half, model = held.shape[1], held.shape[2]
    size = 2 * half
    width = w_query.shape[2]
    inner = w_inner.shape[2]
    heads = width // HD
    flags = jnp.concatenate(
        [
            jnp.stack([section, tensor]).astype(jnp.int32),
            lax.dynamic_slice_in_dim(lengths, section, 1, 0)[0],
            (lax.axis_index("batch") % 2).astype(jnp.int32)[None],
        ]
    )

    x_peer_a = across(held[0], [((0, 0), (0, 1)), ((0, 1), (0, 0))])
    x_peer_b = across(held[1], [((0, 0), (1, 1)), ((0, 1), (1, 0))])
    x_far = across(held[1], [((0, 0), (1, 0)), ((0, 1), (1, 1))])

    attention_own = (w_query[0], w_key[0], w_value[0], w_out[0])
    ffn_own = (w_inner[0], w_outer[0])
    vec_own = pad_rows(
        jnp.concatenate(
            [
                jnp.concatenate([b_query, b_value], axis=1),
                b_out, norm1_gain, norm1_bias, b_inner.reshape(-1, model), b_outer,
                norm2_gain, norm2_bias,
            ],
            axis=0,
        ),
        V_ROWS,
    )
    vec_far = swap(vec_own, "section")
    attention_far = tuple(swap(w, "section") for w in attention_own)
    ffn_far = tuple(swap(w, "section") for w in ffn_own)
    attention_w = attention_own + attention_far
    ffn_w = ffn_own + ffn_far
    vec_one = jnp.where(first, vec_own, vec_far)
    vec_two = jnp.where(first, vec_far, vec_own)

    def send(parts):
        return [swap(part, "tensor") for part in parts]

    def ffn_forward(layer, x, parts, vec, after=()):
        outs = ()
        sums = []
        for c, (part, got) in enumerate(zip(parts, send(parts))):
            outs = call(
                functools.partial(ffn_forward_kernel, layer),
                (flags, x, part, got, vec) + ffn_w,
                "scvvvaaaa",
                [
                    ((size, model), F32), ((size, 1), F32), ((size, model), BF),
                    ((size, inner), BF), ((size, inner), BF), ((half, model), BF),
                ],
                [
                    pltpu.VMEM((model, inner), BF), pltpu.VMEM((inner, model), BF),
                    pltpu.SemaphoreType.DMA((2,)),
                ],
                2 * size * model * inner, after, "cccccv", c, outs,
            )
            sums.append(outs[-1])
        return *outs[:-1], sums

    x_one, *heads_one, part, part2 = attention_call(
        flags, (held[0], x_far, x_peer_a, x_peer_b, vec_one), "vvvvv", attention_w,
        size, model, width, attention_first_kernel, [], ffn_far,
    )
    n1_one, i1_one, n1b_one, a_one, d_one, parts = ffn_forward(
        0, x_one, (part, part2), vec_one
    )
    later = [ordered(held[i], (n1b_one,)) for i in range(2)]
    gy_peer_a = across(later[1], [((1, 0), (1, 1)), ((1, 1), (1, 0))])
    gy_peer_b = across(later[0], [((1, 0), (0, 1)), ((1, 1), (0, 0))])
    gy_far = across(later[0], [((1, 0), (0, 0)), ((1, 1), (0, 1))])

    n2_one, i2_one, x_two, *heads_two, part, part2 = attention_call(
        flags, (n1_one, *parts, *send(parts), vec_one, vec_two), "vvvvvvv", attention_w,
        size, model, width, attention_next_kernel, [((size, model), F32), ((size, 1), F32)],
    )
    n1_two, i1_two, n1b_two, a_two, d_two, parts_two = ffn_forward(
        1, x_two, (part, part2), vec_two, (gy_peer_a, gy_peer_b, gy_far)
    )

    ffn_outs = [
        ((size, model), F32), ((size, model), BF), ((size, inner), BF), ((half, model), BF),
        ((8, model), F32),
    ]
    ffn_scratch = [
        pltpu.VMEM((model, inner), BF), pltpu.VMEM((inner, model), BF),
        pltpu.SemaphoreType.DMA((2,)),
    ]

    def attention_back(layer, g2, parts, got, n1, i1, vec, saved, after):
        q, k, v, e, r, o, ot_f = saved
        *outs, part, part2, small = call(
            functools.partial(attention_back_kernel, layer),
            (flags, g2, *parts, *got, n1, i1, vec, q, k, v, e, r, ot_f) + attention_w,
            "s" + "v" * 14 + "a" * 8,
            [
                ((size, model), F32), ((size, model), BF), ((size, 3 * width), BF),
                ((half, model), BF), ((half, model), BF), ((8, model), F32),
            ],
            [pltpu.VMEM((model, width), BF)] * 3
            + [
                pltpu.VMEM((width, model), BF),
                pltpu.VMEM((HD, size), BF),
                pltpu.VMEM((size, HD), BF),
                pltpu.VMEM((width, size), BF),
                pltpu.VMEM((heads, size, HD), BF),
                pltpu.VMEM((heads, size, HD), BF),
                pltpu.VMEM((width, size), F32),
                pltpu.SemaphoreType.DMA((4,)),
            ],
            2 * size * width * model * 4 + 8 * heads * size * size * HD,
            after, weight=HEAVY,
        )
        return *outs, [part, part2], small

    state = {}
    last = ()
    chunked = [()]

    def add(groups, arrays, shapes):
        sums = []
        for group, (rows, _) in zip(groups, shapes):
            terms = [arrays[i][row : row + rows] for i, row in group]
            sums.append(sum(terms[1:], ordered(terms[0], last)))
        return sums

    def back_last(c):
        part = parts_two[c]
        outs = call(
            functools.partial(ffn_back_last_kernel, c),
            (flags, n1_two, part, got_two[c], vec_two, held[1], gy_far, gy_peer_a, gy_peer_b,
             d_two, small_zero if c == 0 else state["small_f2"]) + ffn_w,
            "sc" + "v" * 7 + "cv" + "a" * 4,
            [((size, model), BF)] + ffn_outs,
            [pltpu.VMEM((half, model), BF)] + ffn_scratch,
            2 * size * model * inner, last, "ccccvv", c, chunked[0],
        )
        chunked[0] = outs if c == 0 else ()
        state["small_f2"] = outs[-1]
        state["y_two"], state["g2_two"], state["g2b_two"], state["gh_two"] = outs[:4]
        state.setdefault("sums_two", []).append(outs[-2])
        state.setdefault("sums_two_got", []).append(swap(outs[-2], "tensor"))
        return outs[-1]

    def back_next(c):
        outs = call(
            ffn_back_next_kernel,
            (flags, state["g1_two"], state["p4_two"][c], state["p4_two_got"][c], n2_one, i2_one,
             vec_one, d_one, small_zero if c == 0 else state["small_f1"]) + ffn_w,
            "scvvccvcv" + "a" * 4,
            ffn_outs,
            ffn_scratch,
            2 * size * model * inner, last, "cccvv", c, chunked[0],
        )
        chunked[0] = outs if c == 0 else ()
        state["small_f1"] = outs[-1]
        state["g2_one"], state["g2b_one"], state["gh_one"] = outs[:3]
        state.setdefault("sums_one", []).append(outs[-2])
        state.setdefault("sums_one_got", []).append(swap(outs[-2], "tensor"))
        return outs[-1]

    def back_attention(name, layer, *rest):
        grad, rows, gqkv, parts, small = attention_back(
            layer, state["g2_" + name], state["sums_" + name], state["sums_" + name + "_got"],
            *rest, last,
        )
        state["g1_" + name], state["g1b_" + name], state["gqkv_" + name] = grad, rows, gqkv
        state["p4_" + name], state["small_a_" + name] = parts, small
        if name == "two":
            state["p4_two_got"] = send(parts)
        return small

    def put(base, ours, theirs):
        state[base] = ours
        state[base + "_got"] = swap(theirs, "section")

    def ffn_products(base, a, gb, gh, n1b, small):
        rows = 2 * (model + PAD)
        ours, theirs = call(
            ffn_product_kernel, (flags, a, gb, gh, n1b, small), "svvvvv",
            [((rows, model), BF)] * 2,
            [pltpu.VMEM((2, rows, model), BF), pltpu.SemaphoreType.DMA((2,))],
            4 * size * model * inner, last, "a",
        )
        put(base, ours, theirs)
        return ours

    def attention_products(base, gqkv, x, o, gb, small):
        rows = 2 * (model + PAD)
        ours, theirs = call(
            attention_product_kernel, (flags, x, gqkv, o, gb, small), "svvvvv",
            [((rows, width), BF)] * 2,
            [pltpu.VMEM((2, rows, width), BF), pltpu.SemaphoreType.DMA((2,))],
            8 * size * model * width, last, "a",
        )
        put(base, ours, theirs)
        return ours

    units = {}
    for base in ("f1", "f2"):
        row = 0
        for name, rows in zip("ab", ffn_rows(model // 2)[0]):
            units[base + name] = (base, row, rows, model)
            row += 2 * rows
    for base in ("a1", "a2"):
        units[base] = (base, 0, model + PAD, width)

    def give(base):
        names = [n for n in units if units[n][0] == base]
        outs = add(
            [[(0, units[n][1] + units[n][2]), (1, units[n][1] + units[n][2])] for n in names],
            (state[base], state[base + "_got"]),
            [units[n][2:] for n in names],
        )
        for n, out in zip(names, outs):
            state[n + "x"] = pair_swap(out)
        return outs[0]

    def step(name, stage):
        base, row, rows, columns = units[name]
        shape = (rows, columns)
        if stage == 0:
            (mine,) = add(
                [[(0, row), (1, row), (2, 0)]],
                (state[base], state[base + "_got"], state[name + "x"]), [shape],
            )
        elif lax.axis_size("batch") != 8:
            mine = rest_of_line(state[name]) if stage == 1 else state[name]
        elif stage < 3:
            (mine,) = add([[(0, 0), (1, 0)]], (state[name], state[name + "s"]), [shape])
        else:
            mine = jnp.where(at_end, state[name + "s"], ordered(state[name], last))
        state[name] = mine
        if stage < 3:
            state[name + "s"] = lax.ppermute(mine, "batch", STAGES[stage][1]) if lax.axis_size("batch") == 8 else None
        else:
            state[name] = (mine, pair_swap(mine))
        return mine

    def share(name):
        both = state[name]
        route = (1, 0) if name[1] == "1" else (0, 1)
        first_half = ordered(both[0], last)
        state[name] = both + tuple(
            lax.ppermute(part, "section", [route]) for part in (first_half, ordered(both[1], last))
        )
        return first_half

    def finish_ffn():
        sums = sum((state[n] for n in sorted(units) if n[0] == "f"), ())
        outs = call(
            ffn_finish_kernel, (flags,) + sums, "s" + "a" * len(sums),
            [((inner, model), F32), ((model, inner), F32)] + [((1, model), F32)] * 3
            + [((1, inner), F32)],
            [
                pltpu.VMEM((4, model + PAD, model), BF), pltpu.VMEM((inner, model), F32),
                pltpu.VMEM((model, inner), F32), pltpu.SemaphoreType.DMA((12,)),
                pltpu.SemaphoreType.DMA((8,)),
            ],
            size * model, last, "aavvvv",
        )
        state["ffn"] = outs
        return outs[-1]

    def finish_attention():
        outs = call(
            attention_finish_kernel, (flags,) + state["a1"] + state["a2"], "s" + "a" * 8,
            [((model, width), F32)] * 3 + [((width, model), F32)] + [((1, model), F32)] * 3
            + [((1, width), F32)] * 2,
            [
                pltpu.VMEM((4, model + PAD, width), BF), pltpu.VMEM((3, model, width), F32),
                pltpu.VMEM((width, model), F32), pltpu.SemaphoreType.DMA((4,)),
                pltpu.SemaphoreType.DMA((4,)),
            ],
            size * model, last, "aaaavvvvv",
        )
        state["attention"] = outs
        return outs[-1]

    at_end = line_end()
    small_zero = jnp.zeros((8, model), F32)
    got_two = send(parts_two)
    tasks = {
        "KC2a": lambda: back_last(0),
        "KC2b": lambda: back_last(1),
        "KWF2": lambda: ffn_products(
            "f2", a_two, state["g2b_two"], state["gh_two"], n1b_two, state["small_f2"]
        ),
        "KD2": lambda: back_attention("two", 1, n1_two, i1_two, vec_two, heads_two),
        "KWA2": lambda: attention_products(
            "a2", state["gqkv_two"], x_two, heads_two[5], state["g1b_two"], state["small_a_two"]
        ),
        "KC1a": lambda: back_next(0),
        "KC1b": lambda: back_next(1),
        "KWF1": lambda: ffn_products(
            "f1", a_one, state["g2b_one"], state["gh_one"], n1b_one, state["small_f1"]
        ),
        "KD1": lambda: back_attention("one", 0, n1_one, i1_one, vec_one, heads_one),
        "KWA1": lambda: attention_products(
            "a1", state["gqkv_one"], x_one, heads_one[5], state["g1b_one"], state["small_a_one"]
        ),
        "finF": finish_ffn,
        "finA": finish_attention,
    }
    for base in ("f1", "f2", "a1", "a2"):
        tasks[base + "gn"] = functools.partial(give, base)
    for name in units:
        for stage in range(4):
            tasks[name + "a" + str(stage + 1)] = functools.partial(step, name, stage)
        tasks[name + "g"] = functools.partial(share, name)
    for name in ORDER:
        last = (tasks[name](),)

    part_one, part_one2 = state["p4_one"]
    part_mine = jnp.where(tensor == 0, part_one, part_one2)
    part_theirs = jnp.where(tensor == 0, part_one2, part_one)
    total = part_mine.astype(F32) + swap(part_theirs, "tensor").astype(F32)
    gx = (lax.dynamic_slice_in_dim(state["g1_one"], tensor * half, half, 0) + total).astype(BF)
    y_mine = lax.dynamic_slice_in_dim(state["y_two"], tensor * half, half, 0)
    y_far = lax.ppermute(y_mine, "section", [(0, 1)])
    gx_far = lax.ppermute(gx, "section", [(1, 0)])
    section_results = jnp.stack(
        [jnp.where(first, gx, y_far), jnp.where(first, gx_far, y_mine)], axis=0
    )[None]
    grad_outer, grad_inner, bias_outer, gain_two, bias_two, bias_inner = state["ffn"]
    grad_q, grad_k, grad_v, grad_out, bias_out, gain_one, bias_one, bias_q, bias_v = state["attention"]
    return (
        section_results,
        grad_q[None],
        bias_q,
        grad_k[None],
        grad_v[None],
        bias_v,
        grad_out[None],
        bias_out,
        gain_one,
        bias_one,
        grad_inner[None],
        bias_inner,
        grad_outer[None],
        bias_outer,
        gain_two,
        bias_two,
    )


def solution(mesh):
    in_specs = (
        P("section", "batch", "tensor", None),
        P("batch", None),
        P("section", None, "tensor"),
        P("section", "tensor"),
        P("section", None, "tensor"),
        P("section", None, "tensor"),
        P("section", "tensor"),
        P("section", "tensor", None),
        P("section", None),
        P("section", None),
        P("section", None),
        P("section", None, "tensor"),
        P("section", "tensor"),
        P("section", "tensor", None),
        P("section", None),
        P("section", None),
        P("section", None),
    )
    out_specs = (
        P("section", "batch", "tensor", None),
        P("section", None, "tensor"),
        P("section", "tensor"),
        P("section", None, "tensor"),
        P("section", None, "tensor"),
        P("section", "tensor"),
        P("section", "tensor", None),
        P("section", None),
        P("section", None),
        P("section", None),
        P("section", None, "tensor"),
        P("section", "tensor"),
        P("section", "tensor", None),
        P("section", None),
        P("section", None),
        P("section", None),
    )
    return jax.shard_map(shards, mesh=mesh, in_specs=in_specs, out_specs=out_specs, check_vma=False)
```
